256 devices in a mesh: context: 64 (over x, y, z_hi, core), tensor: 4 (over z_lo).
Axes of the slice: x: 4, y: 4, z: 8 (z_hi: 2, z_lo: 4; z = z_hi * 4 + z_lo), core: 2. Of those that a mesh axis runs over, the one named last changes fastest.
Arguments:
- tokens: bfloat16 [32768, 5120], P(('context', 'tensor')), may hold values from -6 to 6
- norm_gain: float32 [5120], replicated, may hold values from 0.1 to 1.9
- w_query: bfloat16 [5120, 4096], P('context', 'tensor'), may hold values from -0.078125 to 0.078125
- w_key: bfloat16 [5120, 512], P(None, 'tensor'), may hold values from -0.078125 to 0.078125
- w_value: bfloat16 [5120, 512], P(None, 'tensor'), may hold values from -0.078125 to 0.078125
- query_gain: float32 [128], replicated, may hold values from 1 to 8
- key_gain: float32 [128], replicated, may hold values from 1 to 8
- segments: int32 [32768], replicated, may hold values from 0 to 47, never falling along the last dimension, each value on 1 to 3072 neighbouring positions
- block_of: int32 [64], replicated, may hold values from 0 to 63, each once
Outputs:
- attended: bfloat16 [32768, 4096], P('context', 'tensor')
The draws below stay inside these ranges and needn't reach their ends.
Inputs may be any that keep to these rules, and one draw needn't show every extreme that they name: `segments`: ids never fall along the sequence; each document has at most 3072 tokens and one has exactly 3072. `block_of`: a permutation of the 64 blocks of the sequence.
All inputs are finite; a program needn't handle non-finite values.
Results may differ from the reference program's by a relative error of at most 0.0065.
The reference program's roundings to bfloat16 on the way count: a program that leaves them out, or rounds other values in their place, can miss the bound.
Values may be sent and summed in bfloat16 or wider, within the bound.
A program may use at most 128 MiB of HBM per device.

```python
import math
import jax
import jax.numpy as jnp
import numpy as np
from jax import lax

D = 5120
HEAD_DIM = 128
HEADS = 32
KV_HEADS = 4
SPAN = 6
BLOCK = 512
TOKENS = 32768
MAXDOC = 3072
DOCS = 48
N_CONTEXT = 64


def draw_query_gain(key, part):
    key = jax.random.fold_in(key, 1)
    return jax.random.uniform(key, (HEAD_DIM,), jnp.float32, 1.0, 2.0)


def draw_key_gain(key, part):
    key = jax.random.fold_in(key, 2)
    return jax.random.uniform(key, (HEAD_DIM,), jnp.float32, 1.0, 2.0)


def block_levels(stream_key, shape, shards, smallest, high):
    level, own = 1.0, jax.random.fold_in(stream_key, 6)
    for dim, parts in shards:
        heights = jnp.exp(jax.random.uniform(jax.random.fold_in(own, dim), (parts,), jnp.float32, smallest / len(shards), high / len(shards)))
        level = level * jnp.repeat(heights, shape[dim] // parts).reshape([-1 if axis == dim else 1 for axis in range(len(shape))])
    return level


def profile(number_of, total, reach, slope):
    portions = [(1 << 20) // math.isqrt(standing ** slope) + 1 for standing in range(2, number_of + 1)]
    spare, holding = total - reach - (number_of - 1), [1] * (number_of - 1)
    while spare > 0:
        movable = [i for i in range(number_of - 1) if holding[i] < reach]
        pool, left = sum([portions[i] for i in movable]), spare
        for i in movable:
            extra = min(reach - holding[i], max(1, left * portions[i] // pool), spare)
            holding[i] = holding[i] + extra
            spare = spare - extra
    return np.array([reach] + holding)


def uneven_parts(key, count, total, limit, lean):
    if count == 2:
        one = jax.random.randint(key, (), max(1, total - limit), min(limit, total - 1) + 1)
        return jnp.stack([one, total - one])
    sizes = jnp.asarray(profile(count, total, limit, lean), jnp.int32)
    twos = (count - 1) // 2
    donor, receiver = sizes[1:1 + 2 * twos:2], sizes[2:2 + 2 * twos:2]
    slack = jnp.minimum(donor - 1, limit - receiver)
    passed = jax.random.randint(jax.random.fold_in(key, 1), (twos,), 0, 1 << 20) % (slack + 1)
    sizes = sizes.at[1:1 + 2 * twos:2].set(donor - passed).at[2:2 + 2 * twos:2].set(receiver + passed)
    return sizes[jax.random.permutation(jax.random.fold_in(key, 2), count)]


def normal_values(stream_key, shape, deviation, most, pieces=(), kind=jnp.bfloat16):
    drawn = deviation * jax.random.normal(stream_key, shape, jnp.float32)
    if pieces:
        drawn = drawn * block_levels(stream_key, shape, pieces, -0.22, 0.18)
    return jnp.clip(drawn, -most, most).astype(kind)


def setup_inputs(seed: int = 0) -> dict:
    streams_of = jax.random.split(jax.random.key(seed), 10)
    return {
        "tokens": normal_values(streams_of[0], (TOKENS, D), 1.0, 6.0, ((0, 256),)),
        "norm_gain": jnp.clip(1.0 + 0.18 * jax.random.normal(streams_of[1], (D,), jnp.float32), 0.1, 1.9),
        "w_query": normal_values(streams_of[2], (D, HEADS * HEAD_DIM), D ** -0.5, 0.078125, ((0, 64), (1, 4))),
        "w_key": normal_values(streams_of[3], (D, KV_HEADS * HEAD_DIM), D ** -0.5, 0.078125, ((1, 4),)),
        "w_value": normal_values(streams_of[4], (D, KV_HEADS * HEAD_DIM), D ** -0.5, 0.078125, ((1, 4),)),
        "query_gain": draw_query_gain(jax.random.fold_in(streams_of[9], 71), 0),
        "key_gain": draw_key_gain(jax.random.fold_in(streams_of[9], 71), 0),
        "segments": jnp.searchsorted(jnp.cumsum(uneven_parts(streams_of[7], DOCS, TOKENS, MAXDOC, 2)), jnp.arange(TOKENS), side="right").astype(jnp.int32),
        "block_of": jax.random.permutation(streams_of[8], N_CONTEXT).astype(jnp.int32),
    }


def yarn_frequencies(dim):
    theta = 1000000.0
    factor = 4.0
    initial = 32768.0
    lowest = math.floor(dim * math.log(initial / (32.0 * 2 * math.pi)) / (2 * math.log(theta)))
    highest = math.ceil(dim * math.log(initial / (1.0 * 2 * math.pi)) / (2 * math.log(theta)))
    lowest = max(lowest, 0)
    highest = min(highest, dim - 1)
    spread = max(highest - lowest, 0.001)
    result = []
    for index in range(dim // 2):
        base_freq = theta ** (-2.0 * index / dim)
        ramp = min(max((index - lowest) / spread, 0.0), 1.0)
        result.append(base_freq / factor * ramp + base_freq * (1.0 - ramp))
    return result

def rotate(values, offsets):
    dim = values.shape[-1]
    scale = 0.1 * math.log(4.0) + 1.0
    freqs = jnp.asarray(yarn_frequencies(dim), jnp.float32)
    angles = offsets.astype(jnp.float32)[:, None] * freqs[None, :]
    cosine = jnp.concatenate([jnp.cos(angles), jnp.cos(angles)], -1) * scale
    sine = jnp.concatenate([jnp.sin(angles), jnp.sin(angles)], -1) * scale
    half = dim // 2
    turned = jnp.concatenate([-values[..., half:], values[..., :half]], -1)
    return values * cosine[:, None, :] + turned * sine[:, None, :]

def head_norm(values, gain):
    return values * lax.rsqrt(lax.optimization_barrier(jnp.mean(values * values, -1, keepdims=True)) + 1e-06) * gain

def reference(tokens, norm_gain, w_query, w_key, w_value, query_gain, key_gain, segments, block_of):
    group = HEADS // KV_HEADS
    widened = tokens.astype(jnp.float32)
    normed = (widened * lax.rsqrt(lax.optimization_barrier(jnp.mean(widened * widened, -1, keepdims=True)) + 1e-06) * norm_gain).astype(jnp.bfloat16)
    query = jnp.dot(normed, w_query, preferred_element_type=jnp.float32).reshape(TOKENS, HEADS, HEAD_DIM)
    key = jnp.dot(normed, w_key, preferred_element_type=jnp.float32).reshape(TOKENS, KV_HEADS, HEAD_DIM)
    value = jnp.dot(normed, w_value, preferred_element_type=jnp.float32).astype(jnp.bfloat16).reshape(TOKENS, KV_HEADS, HEAD_DIM)
    places = (block_of[:, None] * BLOCK + jnp.arange(BLOCK, dtype=jnp.int32)[None, :]).reshape(-1).astype(jnp.int32)
    doc_ids = segments[places]
    starts = jnp.searchsorted(segments, doc_ids, side='left').astype(jnp.int32)
    offsets = places - starts
    q_rot = rotate(head_norm(query, query_gain), offsets).astype(jnp.bfloat16)
    k_rot = rotate(head_norm(key, key_gain), offsets).astype(jnp.bfloat16)
    inverse = jnp.zeros((N_CONTEXT,), jnp.int32).at[block_of].set(jnp.arange(N_CONTEXT, dtype=jnp.int32))

    def to_sequence(array):
        return array.reshape((N_CONTEXT, BLOCK) + array.shape[1:])[inverse].reshape(array.shape)
    q_seq = to_sequence(q_rot)
    k_seq = to_sequence(k_rot)
    v_seq = to_sequence(value)
    margin = SPAN * BLOCK
    width = (SPAN + 1) * BLOCK
    k_pad = jnp.concatenate([jnp.zeros((margin, KV_HEADS, HEAD_DIM), jnp.bfloat16), k_seq], 0)
    v_pad = jnp.concatenate([jnp.zeros((margin, KV_HEADS, HEAD_DIM), jnp.bfloat16), v_seq], 0)
    seg_pad = jnp.concatenate([jnp.full((margin,), -1, jnp.int32), segments.astype(jnp.int32)], 0)

    def attend_block(index):
        first = (index * BLOCK).astype(jnp.int32)
        q_block = lax.dynamic_slice_in_dim(q_seq, first, BLOCK, 0)
        k_block = lax.dynamic_slice_in_dim(k_pad, first, width, 0)
        v_block = lax.dynamic_slice_in_dim(v_pad, first, width, 0)
        q_ids = lax.dynamic_slice_in_dim(segments.astype(jnp.int32), first, BLOCK, 0)
        k_ids = lax.dynamic_slice_in_dim(seg_pad, first, width, 0)
        q_places = first + jnp.arange(BLOCK, dtype=jnp.int32)
        k_places = first - margin + jnp.arange(width, dtype=jnp.int32)
        allowed = (q_ids[:, None] == k_ids[None, :]) & (k_places[None, :] <= q_places[:, None])
        grouped = q_block.astype(jnp.float32).reshape(BLOCK, KV_HEADS, group, HEAD_DIM)
        scores = jnp.einsum('qhgd,khd->hgqk', grouped, k_block.astype(jnp.float32)) * HEAD_DIM ** (-0.5)
        row_top = lax.optimization_barrier(jnp.max(jnp.where(allowed, scores, -1e+30), -1, keepdims=True))
        weights = jnp.where(allowed, jnp.exp(scores - row_top), 0.0)
        totals = lax.optimization_barrier(jnp.sum(weights, -1))
        rounded = lax.optimization_barrier(weights.astype(jnp.bfloat16)).astype(jnp.float32)
        summed = jnp.einsum('hgqk,khd->hgqd', rounded, v_block.astype(jnp.float32))
        result = summed / totals[..., None]
        return result.transpose(2, 0, 1, 3).reshape(BLOCK, HEADS * HEAD_DIM)
    blocks = lax.map(attend_block, jnp.arange(N_CONTEXT, dtype=jnp.int32))
    return blocks[block_of].reshape(TOKENS, HEADS * HEAD_DIM).astype(jnp.bfloat16)
```

```python
import functools
import math

import jax
import jax.numpy as jnp
from jax import lax
from jax.experimental import pallas as pl
from jax.experimental.pallas import tpu as pltpu
from jax.sharding import PartitionSpec as P

MESH = pl.DeviceIdType.MESH
BF16 = jnp.bfloat16
F32 = jnp.float32


def yarn_frequencies(dim):
    theta = 1000000.0
    factor = 4.0
    initial = 32768.0
    lowest = math.floor(dim * math.log(initial / (32.0 * 2 * math.pi)) / (2 * math.log(theta)))
    highest = math.ceil(dim * math.log(initial / (1.0 * 2 * math.pi)) / (2 * math.log(theta)))
    lowest = max(lowest, 0)
    highest = min(highest, dim - 1)
    spread = max(highest - lowest, 0.001)
    result = []
    for index in range(dim // 2):
        base_freq = theta ** (-2.0 * index / dim)
        ramp = min(max((index - lowest) / spread, 0.0), 1.0)
        result.append(base_freq / factor * ramp + base_freq * (1.0 - ramp))
    return result


def rotate(values, offsets):
    dim = values.shape[-1]
    scale = 0.1 * math.log(4.0) + 1.0
    freqs = jnp.asarray(yarn_frequencies(dim), jnp.float32)
    angles = offsets.astype(jnp.float32)[:, None] * freqs[None, :]
    cosine = jnp.concatenate([jnp.cos(angles), jnp.cos(angles)], -1) * scale
    sine = jnp.concatenate([jnp.sin(angles), jnp.sin(angles)], -1) * scale
    half = dim // 2
    turned = jnp.concatenate([-values[..., half:], values[..., :half]], -1)
    return values * cosine[:, None, :] + turned * sine[:, None, :]


def head_norm(values, gain):
    return values * lax.rsqrt(jnp.mean(values * values, -1, keepdims=True) + 1e-06) * gain


def root_norm(rows, gain):
    widened = rows.astype(jnp.float32)
    return (
        widened * lax.rsqrt(jnp.mean(widened * widened, -1, keepdims=True) + 1e-06) * gain
    ).astype(jnp.bfloat16)


def ctx_of(x, y, zh, k):
    return x * 16 + y * 4 + zh * 2 + k


def place():
    c = lax.axis_index("context")
    return c // 16, (c // 4) % 4, (c // 2) % 2, c % 2, lax.axis_index("tensor")


def gather_kernel(
    tok, wq, wk, wv,
    tok_all, wq_all, wk_all, wv_all,
    loc, tok_s, tok_r, w1_s, w1_r, zp_s, zp_r, zm_s, zm_r,
    yr_s, yr_r, yl_s, yl_r, fr_s, fr_r, fl_s, fl_r, co_s, co_r,
    kp_s, kp_r, km_s, km_r, kc_s, kc_r,
):
    x, y, zh, k, zl = place()
    me = ctx_of(x, y, zh, k)
    z = zh * 4 + zl
    d = (zl - x + 4) % 4
    zh_u = ((z - d + 8) % 8) // 4
    zh_d = 1 - zh_u

    def at_z(pos):
        pos = pos % 8
        return (ctx_of(x, y, pos // 4, k), pos % 4)

    up, down = at_z(z + 1), at_z(z + 7)
    x_dev = [(ctx_of((x + o) % 4, y, zh, k), zl) for o in range(4)]
    y_right, y_left = (ctx_of(x, (y + 1) % 4, zh, k), zl), (ctx_of(x, (y + 3) % 4, zh, k), zl)
    other = (ctx_of(x, y, zh, 1 - k), zl)

    barrier = pltpu.get_barrier_semaphore()
    for dev in (x_dev[1], x_dev[2], x_dev[3], up, down, y_right, y_left, other):
        pl.semaphore_signal(barrier, inc=1, device_id=dev, device_id_type=MESH)
    pl.semaphore_wait(barrier, 8)

    def remote(src, dst, ss, rs, dev):
        return pltpu.make_async_remote_copy(
            src_ref=src, dst_ref=dst, send_sem=ss, recv_sem=rs, device_id=dev, device_id_type=MESH
        )

    half = tok.shape[0] // 2
    halves = (pl.ds(0, half), pl.ds(half, half))

    def tok_copy(n, src, slot, part, dev):
        return remote(src, tok_all.at[slot, halves[part]], tok_s.at[n], tok_r.at[n], dev)

    sends = [
        tok_copy(0, tok.at[halves[0]], x, 0, x_dev[1]),
        tok_copy(3, tok.at[halves[1]], x, 1, x_dev[3]),
        tok_copy(1, tok.at[halves[1]], x, 1, x_dev[1]),
        tok_copy(2, tok.at[halves[0]], x, 0, x_dev[3]),
    ]
    w1_index = (x - zl + 4) % 4
    w1 = remote(wq, wq_all.at[me], w1_s.at[0], w1_r.at[w1_index], (ctx_of(zl, y, zh, k), zl))
    own_w = pltpu.make_async_copy(wq, wq_all.at[me], loc.at[1])

    @pl.when(d != 0)
    def _():
        w1.start()

    @pl.when(d == 0)
    def _():
        own_w.start()

    for copy in sends:
        copy.start()
    own_tok = pltpu.make_async_copy(tok, tok_all.at[x], loc.at[0])
    own_tok.start()
    own_k = pltpu.make_async_copy(wk, wk_all, loc.at[2])
    own_v = pltpu.make_async_copy(wv, wv_all, loc.at[3])

    @pl.when(d == 0)
    def _():
        own_k.start()
        own_v.start()

    def slot(i, zhalf, yy):
        return wq_all.at[ctx_of((x + i) % 4, yy, zhalf, k)]

    def zp(i):
        ref = slot(i, zh_u, y)
        return remote(ref, ref, zp_s.at[i], zp_r.at[i], up)

    def zm(i, zhalf):
        ref = slot(i, zhalf, y)
        return remote(ref, ref, zm_s.at[i], zm_r.at[i], down)

    def core(n, ref):
        return remote(ref, ref, co_s.at[n], co_r.at[n], other)

    def y_own(s, ref):
        return (
            remote(ref, ref, yr_s.at[s], yr_r.at[s], y_right),
            remote(ref, ref, yl_s.at[s], yl_r.at[s], y_left),
        )

    def fwd_right(i2, ref):
        return remote(ref, ref, fr_s.at[i2], fr_r.at[i2], y_right)

    def fwd_left(i2, ref):
        return remote(ref, ref, fl_s.at[i2], fl_r.at[i2], y_left)

    def spread(s, ref):
        right, left = y_own(s, ref)
        right.start()
        left.start()
        core(s, ref).start()

    def in_order(upper, lower):
        def step(t, carry):
            i = t - d

            @pl.when((i >= 0) & (i < 4))
            def _():
                upper(i)

            j = t - 4 + d

            @pl.when((j >= 0) & (j < 4))
            def _():
                lower(j)

            return carry

        lax.fori_loop(0, 8, step, 0)

    def z_upper(i):
        ref = slot(i, zh_u, y)

        @pl.when(d == 0)
        def _():
            @pl.when(i == 0)
            def _():
                own_w.wait()

            @pl.when(i != 0)
            def _():
                remote(ref, ref, w1_s.at[0], w1_r.at[i], other).wait_recv()

            zm(i, zh_u).start()

        @pl.when(d != 0)
        def _():
            zp(i).wait_recv()

        zp(i).start()
        spread(i, ref)

    def z_lower(i):
        ref = slot(i, zh_d, y)

        @pl.when(d == 0)
        def _():
            remote(ref, ref, zp_s.at[i], zp_r.at[i], up).wait_recv()

        @pl.when(d != 0)
        def _():
            zm(i, zh_d).wait_recv()

        @pl.when(d >= 2)
        def _():
            zm(i, zh_d).start()

        spread(4 + i, ref)

    in_order(z_upper, z_lower)

    left_x, right_x, far_x = (x + 3) % 4, (x + 1) % 4, (x + 2) % 4
    tok_copy(0, tok_all.at[left_x, halves[0]], left_x, 0, x_dev[1]).wait_recv()
    fwd_a = tok_copy(4, tok_all.at[left_x, halves[0]], left_x, 0, x_dev[1])
    fwd_a.start()
    tok_copy(3, tok_all.at[right_x, halves[1]], right_x, 1, x_dev[3]).wait_recv()
    fwd_b = tok_copy(5, tok_all.at[right_x, halves[1]], right_x, 1, x_dev[3])
    fwd_b.start()

    rows = wk.shape[0] // 8

    def part(i):
        return pl.ds((k * 4 + i) * rows, rows)

    def kv_core(n, ref):
        return remote(ref, ref, kc_s.at[n], kc_r.at[n], other)

    def kp(i, src):
        return remote(src.at[part(i)], wk_all.at[part(i)], kp_s.at[i], kp_r.at[i], up)

    def km(i, src):
        return remote(src.at[part(i)], wv_all.at[part(i)], km_s.at[i], km_r.at[i], down)

    y_l, y_r, y_far = (y + 3) % 4, (y + 1) % 4, (y + 2) % 4

    def ring(i, s, zhalf):
        ref = slot(i, zhalf, y_l)
        y_own(s, ref)[0].wait_recv()

        @pl.when(i % 2 == 0)
        def _():
            fwd_right(s // 2, ref).start()

        core(8 + s, ref).start()
        ref2 = slot(i, zhalf, y_r)
        y_own(s, ref2)[1].wait_recv()

        @pl.when(i % 2 == 1)
        def _():
            fwd_left(s // 2, ref2).start()

        core(16 + s, ref2).start()

    def kv_upper(i):
        @pl.when(d == 0)
        def _():
            kp(i, wk).start()
            km(i, wv).start()

        @pl.when(d != 0)
        def _():
            kp(i, wk_all).wait_recv()
            kv_core(i, wk_all.at[part(i)]).start()

        @pl.when((d == 1) | (d == 2))
        def _():
            kp(i, wk_all).start()

        ring(i, i, zh_u)

    def kv_lower(i):
        @pl.when(d != 0)
        def _():
            km(i, wv_all).wait_recv()
            kv_core(4 + i, wv_all.at[part(i)]).start()

        @pl.when(d >= 2)
        def _():
            km(i, wv_all).start()

        ring(i, 4 + i, zh_d)

    in_order(kv_upper, kv_lower)

    def far_upper(i):
        finish(i, i, zh_u)

    def far_lower(i):
        finish(i, 4 + i, zh_d)

    def finish(i, s, zhalf):
        ref = slot(i, zhalf, y_far)

        @pl.when(i % 2 == 0)
        def _():
            fwd_right(s // 2, ref).wait_recv()

        @pl.when(i % 2 == 1)
        def _():
            fwd_left(s // 2, ref).wait_recv()

        core(24 + s, ref).start()

    in_order(far_upper, far_lower)

    any_w = wq_all.at[me]

    def drain_core(n, carry):
        copy = core(n, any_w)
        copy.wait_send()
        copy.wait_recv()
        return carry

    lax.fori_loop(0, 32, drain_core, 0)

    def drain_y(s, carry):
        right, left = y_own(s, any_w)
        right.wait_send()
        left.wait_send()
        return carry

    lax.fori_loop(0, 8, drain_y, 0)

    def drain_four(i, carry):
        zp(i).wait_send()
        fwd_right(i, any_w).wait_send()
        fwd_left(i, any_w).wait_send()

        @pl.when((d == 0) | (d >= 2))
        def _():
            zm(i, zh_u).wait_send()
            km(i, wv_all).wait_send()

        @pl.when(d <= 2)
        def _():
            kp(i, wk_all).wait_send()

        @pl.when(d != 0)
        def _():
            for n, ref in ((i, wk_all), (4 + i, wv_all)):
                copy = kv_core(n, ref.at[part(i)])
                copy.wait_send()
                copy.wait_recv()

        return carry

    lax.fori_loop(0, 4, drain_four, 0)
    for copy in sends:
        copy.wait_send()
    fwd_a.wait_send()
    fwd_b.wait_send()
    tok_copy(1, tok_all.at[left_x, halves[1]], left_x, 1, x_dev[1]).wait_recv()
    tok_copy(2, tok_all.at[right_x, halves[0]], right_x, 0, x_dev[3]).wait_recv()
    tok_copy(4, tok_all.at[far_x, halves[0]], far_x, 0, x_dev[1]).wait_recv()
    tok_copy(5, tok_all.at[far_x, halves[1]], far_x, 1, x_dev[3]).wait_recv()
    own_tok.wait()

    @pl.when(d != 0)
    def _():
        w1.wait_send()

    @pl.when(d == 0)
    def _():
        own_k.wait()
        own_v.wait()


def gather(tokens, w_query, w_key, w_value):
    any_spec = pl.BlockSpec(memory_space=pl.ANY)
    dma = pltpu.SemaphoreType.DMA
    pair = lambda n: [dma((n,)), dma((n,))]
    return pl.pallas_call(
        gather_kernel,
        out_shape=(
            jax.ShapeDtypeStruct((4,) + tokens.shape, BF16),
            jax.ShapeDtypeStruct((64,) + w_query.shape, BF16),
            jax.ShapeDtypeStruct(w_key.shape, BF16),
            jax.ShapeDtypeStruct(w_value.shape, BF16),
        ),
        in_specs=[any_spec] * 4,
        out_specs=(any_spec,) * 4,
        scratch_shapes=[dma((4,))] + pair(6) + [dma((1,)), dma((4,))] + pair(4) + pair(4)
        + pair(8) + pair(8) + pair(4) + pair(4) + pair(32) + pair(4) + pair(4) + pair(8),
        compiler_params=pltpu.CompilerParams(collective_id=0, has_side_effects=True),
    )(tokens, w_query, w_key, w_value)


def exchange_kernel(
    table, q_in, kv_in,
    q_out, kv_all,
    qx, got, picked,
    loc, qx_s, qx_r, qz_s, qz_r, p1_s, p1_r, p2_s, p2_r,
):
    x, y, zh, k, zl = place()
    rest = y * 4 + zh * 2 + k
    mine = x * 8 + y * 2 + k
    barrier = pltpu.get_barrier_semaphore()

    def greet(dev):
        pl.semaphore_signal(barrier, inc=1, device_id=dev, device_id_type=MESH)

    for o in range(1, 4):
        greet((ctx_of((x + o) % 4, y, zh, k), zl))
        greet((ctx_of(x, y, zh, k), (zl + o) % 4))

    def greet_piece(r, carry):
        @pl.when((x != zl) | (r != rest))
        def _():
            greet((zl * 16 + r, x))

        return carry

    lax.fori_loop(0, 16, greet_piece, 0)

    def half_plane(d):
        return (ctx_of(d // 8, (d // 2) % 4, zh, d % 2), zl)

    def greet_plane(o, carry):
        greet(half_plane((mine + o) % 32))
        return carry

    lax.fori_loop(1, 32, greet_plane, 0)
    pl.semaphore_wait(barrier, 6 + 15 + 31 + ((x - zl + 4) % 4 + 3) // 4)

    def remote(src, dst, ss, rs, dev):
        return pltpu.make_async_remote_copy(
            src_ref=src, dst_ref=dst, send_sem=ss, recv_sem=rs, device_id=dev, device_id_type=MESH
        )

    def piece(r):
        p = (r // 4) * 2 + r % 2
        return remote(
            kv_in.at[p], got.at[pl.ds(rest * 4, 4)], p1_s.at[r], p1_r.at[rest], (zl * 16 + r, x)
        )

    own_piece = pltpu.make_async_copy(
        kv_in.at[(rest // 4) * 2 + rest % 2], got.at[pl.ds(rest * 4, 4)], loc.at[0]
    )

    def send_piece(o, carry):
        r = (rest + o) % 16

        @pl.when((x != zl) | (r != rest))
        def _():
            piece(r).start()

        return carry

    lax.fori_loop(0, 16, send_piece, 0)

    @pl.when(x == zl)
    def _():
        own_piece.start()

    def x_step(o):
        to = (x + o) % 4
        return remote(
            q_in.at[to], qx.at[x], qx_s.at[o], qx_r.at[o], (ctx_of(to, y, zh, k), zl)
        )

    for o in (1, 3, 2):
        x_step(o).start()

    def z_step(src, to):
        o = (to - zl + 4) % 4
        return remote(src, q_out.at[zl], qz_s.at[o], qz_r.at[o], (ctx_of(x, y, zh, k), to))

    def z_move(src, frm):
        @pl.when(frm != zl)
        def _():
            z_step(src, frm).start()

        @pl.when(frm == zl)
        def _():
            pltpu.make_async_copy(src, q_out.at[zl], loc.at[1]).start()

    z_move(q_in.at[x], x)

    def wait_piece(r, carry):
        @pl.when((x != zl) | (r != rest))
        def _():
            remote(
                kv_in.at[0], got.at[pl.ds(r * 4, 4)], p1_s.at[0], p1_r.at[r], (zl * 16 + r, x)
            ).wait_recv()

        return carry

    lax.fori_loop(0, 16, wait_piece, 0)

    @pl.when(x == zl)
    def _():
        own_piece.wait()

    def plane(d):
        return remote(
            picked.at[d], kv_all.at[:, :, mine], p2_s.at[d], p2_r.at[mine], half_plane(d)
        )

    def pick(d):
        for i in range(7):
            picked[d, :, i] = got[table[d, i]]

    def send_plane(o, carry):
        d = (mine + o) % 32
        pick(d)
        plane(d).start()
        return carry

    lax.fori_loop(1, 32, send_plane, 0)
    pick(mine)
    own_plane = pltpu.make_async_copy(picked.at[mine], kv_all.at[:, :, mine], loc.at[2])
    own_plane.start()

    for o in (1, 3, 2):
        frm = (x - o + 4) % 4
        remote(q_in.at[0], qx.at[frm], qx_s.at[o], qx_r.at[o], (ctx_of(frm, y, zh, k), zl)).wait_recv()
        z_move(qx.at[frm], frm)

    pltpu.make_async_copy(q_in.at[0], q_out.at[zl], loc.at[1]).wait()
    for o in (1, 2, 3):
        x_step(o).wait_send()
        z_step(q_in.at[0], (zl + o) % 4).wait_send()
        frm = (zl - o + 4) % 4
        remote(
            q_in.at[0], q_out.at[frm], qz_s.at[o], qz_r.at[o], (ctx_of(x, y, zh, k), frm)
        ).wait_recv()

    def drain_piece(r, carry):
        @pl.when((x != zl) | (r != rest))
        def _():
            piece(r).wait_send()

        return carry

    lax.fori_loop(0, 16, drain_piece, 0)
    own_plane.wait()

    def drain_plane(o, carry):
        d = (mine + o) % 32
        plane(d).wait_send()
        remote(
            picked.at[d], kv_all.at[:, :, d], p2_s.at[d], p2_r.at[d], half_plane(d)
        ).wait_recv()
        return carry

    lax.fori_loop(1, 32, drain_plane, 0)


def exchange(table, q_in, kv_in):
    any_spec = pl.BlockSpec(memory_space=pl.ANY)
    dma = pltpu.SemaphoreType.DMA
    pair = lambda n: [dma((n,)), dma((n,))]
    return pl.pallas_call(
        exchange_kernel,
        out_shape=(
            jax.ShapeDtypeStruct(q_in.shape, BF16),
            jax.ShapeDtypeStruct((2, 7, 32, 16, 128), BF16),
        ),
        in_specs=[pl.BlockSpec(memory_space=pltpu.SMEM), any_spec, any_spec],
        out_specs=(any_spec, any_spec),
        scratch_shapes=[
            pltpu.VMEM(q_in.shape, BF16),
            pltpu.VMEM((64, 2, 16, 128), BF16),
            pltpu.VMEM((32, 2, 7, 16, 128), BF16),
            dma((3,)),
        ] + pair(4) + pair(4) + pair(16) + pair(32),
        compiler_params=pltpu.CompilerParams(
            collective_id=1, has_side_effects=True, vmem_limit_bytes=16 << 20
        ),
    )(table, q_in, kv_in)


def attend_kernel(start_ref, q_ref, kv_ref, o_ref):
    length, head_size = q_ref.shape
    step = 256
    scale = head_size ** (-0.5) * math.log2(math.e)
    for r in range(length // step):
        rows = pl.ds(r * step, step)
        q = q_ref[rows, :]
        start = start_ref[rows, :]
        tiles = []
        top = None
        for i in range(7):
            scores = lax.dot_general(
                q, kv_ref[0, i], (((1,), (1,)), ((), ())), preferred_element_type=F32
            )
            at = lax.broadcasted_iota(jnp.int32, scores.shape, 1) + (i - 6) * length
            allowed = at >= start
            if i == 6:
                here = lax.broadcasted_iota(jnp.int32, scores.shape, 0) + r * step
                allowed = allowed & (at <= here)
            scores = jnp.where(allowed, scores, -1e30)
            tiles.append(scores)
            best = jnp.max(scores, -1, keepdims=True)
            top = best if top is None else jnp.maximum(top, best)
        total = None
        summed = None
        for i in range(7):
            weights = jnp.exp2((tiles[i] - top) * scale)
            added = jnp.sum(weights, -1, keepdims=True)
            part = jnp.dot(weights.astype(BF16), kv_ref[1, i], preferred_element_type=F32)
            total = added if total is None else total + added
            summed = part if summed is None else summed + part
        o_ref[rows, :] = (summed / total).astype(BF16)


def attend(start, q, kv):
    length, width = q.shape
    heads = width // 128
    return pl.pallas_call(
        attend_kernel,
        grid=(heads,),
        out_shape=jax.ShapeDtypeStruct(q.shape, BF16),
        in_specs=[
            pl.BlockSpec((length, 1), lambda h: (0, 0)),
            pl.BlockSpec((length, 128), lambda h: (0, h)),
            pl.BlockSpec(kv.shape, lambda h: (0, 0, 0, 0)),
        ],
        out_specs=pl.BlockSpec((length, 128), lambda h: (0, h)),
        compiler_params=pltpu.CompilerParams(vmem_limit_bytes=48 << 20),
    )(start, q, kv)


def shards(tokens, norm_gain, w_query, w_key, w_value, query_gain, key_gain, segments, block_of):
    x, y, zh, k, zl = place()
    rest = y * 4 + zh * 2 + k
    quarter = tokens.shape[0]
    length = quarter * 4
    tok_all, wq_all, wk_all, wv_all = gather(tokens, w_query, w_key, w_value)

    ids = jnp.arange(48, dtype=jnp.int32)
    starts = jnp.sum((segments[None, :] < ids[:, None]).astype(jnp.int32), 1)

    def start_of(at, size):
        doc = lax.dynamic_slice_in_dim(segments, at, size, 0)
        return jnp.sum(jnp.where(doc[:, None] == ids[None, :], starts[None, :], 0), 1)

    offsets = []
    for other in range(4):
        at = block_of[other * 16 + rest] * length + zl * quarter
        offsets.append(at + jnp.arange(quarter, dtype=jnp.int32) - start_of(at, quarter))
    offsets = jnp.concatenate(offsets)

    normed = root_norm(tok_all.reshape(length, -1), norm_gain)
    query = jnp.dot(normed, wq_all.reshape(normed.shape[1], -1), preferred_element_type=F32)
    key = jnp.dot(normed, wk_all, preferred_element_type=F32).reshape(length, 1, 128)
    value = jnp.dot(normed, wv_all, preferred_element_type=F32).astype(BF16)
    k_rot = rotate(head_norm(key, key_gain), offsets).astype(BF16)
    query = query.reshape(length, -1, 128)
    q_rot = rotate(head_norm(query, query_gain), offsets).astype(BF16)
    pieces = jnp.stack(
        [k_rot.reshape(4, 8, 16, 128), value.reshape(4, 8, 16, 128)], 2
    ).transpose(1, 0, 2, 3, 4)

    blocks = jnp.arange(64, dtype=jnp.int32)
    holder = jnp.sum(jnp.where(block_of[None, :] == blocks[:, None], blocks[None, :], 0), 1)
    d = jnp.arange(32, dtype=jnp.int32)
    wanted = block_of[ctx_of(d // 8, (d // 2) % 4, zh, d % 2)][:, None] - 6 + jnp.arange(7)[None, :]
    source = holder[jnp.maximum(wanted, 0)]
    table = (source % 16) * 4 + source // 16

    q_mine, kv = exchange(table, q_rot.reshape(4, quarter, -1), pieces)
    first = block_of[x * 16 + rest] * length
    start = (start_of(first, length) - first)[:, None]
    return attend(start, q_mine.reshape(length, -1), kv.reshape(2, 7, length, 128))


def solution(mesh):
    return jax.shard_map(
        shards,
        mesh=mesh,
        in_specs=(
            P(("context", "tensor"), None),
            P(),
            P("context", "tensor"),
            P(None, "tensor"),
            P(None, "tensor"),
            P(),
            P(),
            P(),
            P(),
        ),
        out_specs=P("context", "tensor"),
        check_vma=False,
    )
```

```python
import math

import jax
import jax.numpy as jnp
from jax import lax
from jax.experimental import pallas as pl
from jax.experimental.pallas import tpu as pltpu
from jax.sharding import PartitionSpec as P

MESH = pl.DeviceIdType.MESH
BF16 = jnp.bfloat16
F32 = jnp.float32


def yarn_frequencies(dim):
    theta = 1000000.0
    factor = 4.0
    initial = 32768.0
    lowest = math.floor(dim * math.log(initial / (32.0 * 2 * math.pi)) / (2 * math.log(theta)))
    highest = math.ceil(dim * math.log(initial / (1.0 * 2 * math.pi)) / (2 * math.log(theta)))
    lowest = max(lowest, 0)
    highest = min(highest, dim - 1)
    spread = max(highest - lowest, 0.001)
    result = []
    for index in range(dim // 2):
        base_freq = theta ** (-2.0 * index / dim)
        ramp = min(max((index - lowest) / spread, 0.0), 1.0)
        result.append(base_freq / factor * ramp + base_freq * (1.0 - ramp))
    return result


def ctx_of(x, y, zh, k):
    return x * 16 + y * 4 + zh * 2 + k


def place():
    c = lax.axis_index("context")
    return c // 16, (c // 4) % 4, (c // 2) % 2, c % 2, lax.axis_index("tensor")


def front_kernel(
    table, tok, norm_gain, wq, wk, wv, q_gain, k_gain, cosine, sine,
    q_out, kv_all,
    tok_all, wq_all, wkv_all, q_send, qx, kv_send, got, picked,
    loc, tok_s, tok_r, w1_s, w1_r, zp_s, zp_r, zm_s, zm_r,
    yr_s, yr_r, yl_s, yl_r, fr_s, fr_r, fl_s, fl_r, co_s, co_r,
    kp_s, kp_r, km_s, km_r, kc_s, kc_r,
    qx_s, qx_r, qz_s, qz_r, p1_s, p1_r, p2_s, p2_r,
):
    x, y, zh, k, zl = place()
    me = ctx_of(x, y, zh, k)
    z = zh * 4 + zl
    d = (zl - x + 4) % 4
    zh_u = ((z - d + 8) % 8) // 4
    zh_d = 1 - zh_u

    def at_z(pos):
        pos = pos % 8
        return (ctx_of(x, y, pos // 4, k), pos % 4)

    up, down = at_z(z + 1), at_z(z + 7)
    x_dev = [(ctx_of((x + o) % 4, y, zh, k), zl) for o in range(4)]
    y_right, y_left = (ctx_of(x, (y + 1) % 4, zh, k), zl), (ctx_of(x, (y + 3) % 4, zh, k), zl)
    other = (ctx_of(x, y, zh, 1 - k), zl)

    rest = y * 4 + zh * 2 + k
    mine = x * 8 + y * 2 + k

    def half_plane(n):
        return (ctx_of(n // 8, (n // 2) % 4, zh, n % 2), zl)

    barrier = pltpu.get_barrier_semaphore()

    def greet(dev):
        pl.semaphore_signal(barrier, inc=1, device_id=dev, device_id_type=MESH)

    for dev in (x_dev[1], x_dev[2], x_dev[3], up, down, y_right, y_left, other):
        greet(dev)
    for o in range(1, 4):
        greet((me, (zl + o) % 4))

    def greet_piece(r, carry):
        @pl.when((x != zl) | (r != rest))
        def _():
            greet((zl * 16 + r, x))

        return carry

    lax.fori_loop(0, 16, greet_piece, 0)

    def greet_plane(o, carry):
        greet(half_plane((mine + o) % 32))
        return carry

    lax.fori_loop(1, 32, greet_plane, 0)

    quarter = tok.shape[0]
    width = tok.shape[1]

    def norm_rows(n, carry):
        rows = pl.ds(pl.multiple_of(n * 16, 16), 16)
        wide = tok[rows, :].astype(F32)
        mean = jnp.mean(wide * wide, -1, keepdims=True)
        wide = wide * lax.rsqrt(mean + 1e-06) * norm_gain[...]
        tok_all[pl.ds(pl.multiple_of(x * quarter + n * 16, 16), 16), :] = wide.astype(BF16)
        return carry

    lax.fori_loop(0, quarter // 16, norm_rows, 0)
    pl.semaphore_wait(barrier, 8 + 3 + 15 + 31 + ((x - zl + 4) % 4 + 3) // 4)

    def remote(src, dst, ss, rs, dev):
        return pltpu.make_async_remote_copy(
            src_ref=src, dst_ref=dst, send_sem=ss, recv_sem=rs, device_id=dev, device_id_type=MESH
        )

    half = quarter // 2

    def tok_copy(n, slot, part, dev):
        ref = tok_all.at[pl.ds(pl.multiple_of(slot * quarter + part * half, 16), half)]
        return remote(ref, ref, tok_s.at[n], tok_r.at[n], dev)

    def w_slot(c):
        return wq_all.at[pl.ds(pl.multiple_of(c * w_rows, 16), w_rows)]

    w_rows = wq.shape[0]
    sends = [
        tok_copy(0, x, 0, x_dev[1]),
        tok_copy(3, x, 1, x_dev[3]),
        tok_copy(1, x, 1, x_dev[1]),
        tok_copy(2, x, 0, x_dev[3]),
    ]
    w1_index = (x - zl + 4) % 4
    w1 = remote(wq, w_slot(me), w1_s.at[0], w1_r.at[w1_index], (ctx_of(zl, y, zh, k), zl))
    own_w = pltpu.make_async_copy(wq, w_slot(me), loc.at[1])

    @pl.when(d != 0)
    def _():
        w1.start()

    @pl.when(d == 0)
    def _():
        own_w.start()

    for copy in sends:
        copy.start()

    @pl.when(d == 0)
    def _():
        wkv_all[:, :128] = wk[...]
        wkv_all[:, 128:] = wv[...]

    def slot(i, zhalf, yy):
        return w_slot(ctx_of((x + i) % 4, yy, zhalf, k))

    def zp(i):
        ref = slot(i, zh_u, y)
        return remote(ref, ref, zp_s.at[i], zp_r.at[i], up)

    def zm(i, zhalf):
        ref = slot(i, zhalf, y)
        return remote(ref, ref, zm_s.at[i], zm_r.at[i], down)

    def core(n, ref):
        return remote(ref, ref, co_s.at[n], co_r.at[n], other)

    def y_own(s, ref):
        return (
            remote(ref, ref, yr_s.at[s], yr_r.at[s], y_right),
            remote(ref, ref, yl_s.at[s], yl_r.at[s], y_left),
        )

    def fwd_right(i2, ref):
        return remote(ref, ref, fr_s.at[i2], fr_r.at[i2], y_right)

    def fwd_left(i2, ref):
        return remote(ref, ref, fl_s.at[i2], fl_r.at[i2], y_left)

    def spread(s, ref):
        right, left = y_own(s, ref)
        right.start()
        left.start()
        core(s, ref).start()

    def in_order(upper, lower):
        def step(t, carry):
            i = t - d

            @pl.when((i >= 0) & (i < 4))
            def _():
                upper(i)

            j = t - 4 + d

            @pl.when((j >= 0) & (j < 4))
            def _():
                lower(j)

            return carry

        lax.fori_loop(0, 8, step, 0)

    def z_upper(i):
        ref = slot(i, zh_u, y)

        @pl.when(d == 0)
        def _():
            @pl.when(i == 0)
            def _():
                own_w.wait()

            @pl.when(i != 0)
            def _():
                remote(ref, ref, w1_s.at[0], w1_r.at[i], other).wait_recv()

            zm(i, zh_u).start()

        @pl.when(d != 0)
        def _():
            zp(i).wait_recv()

        zp(i).start()
        spread(i, ref)

    def z_lower(i):
        ref = slot(i, zh_d, y)

        @pl.when(d == 0)
        def _():
            remote(ref, ref, zp_s.at[i], zp_r.at[i], up).wait_recv()

        @pl.when(d != 0)
        def _():
            zm(i, zh_d).wait_recv()

        @pl.when(d >= 2)
        def _():
            zm(i, zh_d).start()

        spread(4 + i, ref)

    in_order(z_upper, z_lower)

    left_x, right_x, far_x = (x + 3) % 4, (x + 1) % 4, (x + 2) % 4
    tok_copy(0, left_x, 0, x_dev[1]).wait_recv()
    fwd_a = tok_copy(4, left_x, 0, x_dev[1])
    fwd_a.start()
    tok_copy(3, right_x, 1, x_dev[3]).wait_recv()
    fwd_b = tok_copy(5, right_x, 1, x_dev[3])
    fwd_b.start()

    rows = wk.shape[0] // 8

    def part(i):
        return pl.ds(pl.multiple_of((k * 4 + i) * rows, 16), rows)

    def key_part(i):
        return wkv_all.at[part(i), pl.ds(0, 128)]

    def value_part(i):
        return wkv_all.at[part(i), pl.ds(128, 128)]

    def kv_core(n, ref):
        return remote(ref, ref, kc_s.at[n], kc_r.at[n], other)

    def kp(i):
        return remote(key_part(i), key_part(i), kp_s.at[i], kp_r.at[i], up)

    def km(i):
        return remote(value_part(i), value_part(i), km_s.at[i], km_r.at[i], down)

    y_l, y_r, y_far = (y + 3) % 4, (y + 1) % 4, (y + 2) % 4

    def ring(i, s, zhalf):
        ref = slot(i, zhalf, y_l)
        y_own(s, ref)[0].wait_recv()

        @pl.when(i % 2 == 0)
        def _():
            fwd_right(s // 2, ref).start()

        core(8 + s, ref).start()
        ref2 = slot(i, zhalf, y_r)
        y_own(s, ref2)[1].wait_recv()

        @pl.when(i % 2 == 1)
        def _():
            fwd_left(s // 2, ref2).start()

        core(16 + s, ref2).start()

    def kv_upper(i):
        @pl.when(d == 0)
        def _():
            kp(i).start()
            km(i).start()

        @pl.when(d != 0)
        def _():
            kp(i).wait_recv()
            kv_core(i, key_part(i)).start()

        @pl.when((d == 1) | (d == 2))
        def _():
            kp(i).start()

        ring(i, i, zh_u)

    def kv_lower(i):
        @pl.when(d != 0)
        def _():
            km(i).wait_recv()
            kv_core(4 + i, value_part(i)).start()

        @pl.when(d >= 2)
        def _():
            km(i).start()

        ring(i, 4 + i, zh_d)

    in_order(kv_upper, kv_lower)

    tok_copy(1, left_x, 1, x_dev[1]).wait_recv()
    tok_copy(2, right_x, 0, x_dev[3]).wait_recv()
    tok_copy(4, far_x, 0, x_dev[1]).wait_recv()
    tok_copy(5, far_x, 1, x_dev[3]).wait_recv()

    @pl.when(d != 0)
    def _():
        def core_part(i, carry):
            kv_core(i, key_part(i)).wait_recv()
            kv_core(4 + i, value_part(i)).wait_recv()
            return carry

        lax.fori_loop(0, 4, core_part, 0)

    def turn(t, gain):
        t = t * lax.rsqrt(jnp.mean(t * t, -1, keepdims=True) + 1e-06) * gain[...]
        return (t * cosine[...] + pltpu.roll(t, 64, 1) * sine[...]).astype(BF16)

    both = jnp.dot(tok_all[...], wkv_all[...], preferred_element_type=F32)
    key = turn(both[:, :128], k_gain)
    value = both[:, 128:].astype(BF16)
    for p in range(8):
        for n in range(4):
            at = n * 128 + p * 16
            kv_send[p, n, 0] = key[at : at + 16]
            kv_send[p, n, 1] = value[at : at + 16]

    def piece(r):
        p = (r // 4) * 2 + r % 2
        return remote(
            kv_send.at[p], got.at[pl.ds(rest * 4, 4)], p1_s.at[r], p1_r.at[rest], (zl * 16 + r, x)
        )

    own_piece = pltpu.make_async_copy(
        kv_send.at[(rest // 4) * 2 + rest % 2], got.at[pl.ds(rest * 4, 4)], loc.at[0]
    )

    def send_piece(o, carry):
        r = (rest + o) % 16

        @pl.when((x != zl) | (r != rest))
        def _():
            piece(r).start()

        return carry

    lax.fori_loop(0, 16, send_piece, 0)

    @pl.when(x == zl)
    def _():
        own_piece.start()

    def far_upper(i):
        finish(i, i, zh_u)

    def far_lower(i):
        finish(i, 4 + i, zh_d)

    def finish(i, s, zhalf):
        ref = slot(i, zhalf, y_far)

        @pl.when(i % 2 == 0)
        def _():
            fwd_right(s // 2, ref).wait_recv()

        @pl.when(i % 2 == 1)
        def _():
            fwd_left(s // 2, ref).wait_recv()

        core(24 + s, ref).start()

    in_order(far_upper, far_lower)

    any_w = w_slot(me)

    def wait_core(n, carry):
        core(n, any_w).wait_recv()
        return carry

    lax.fori_loop(0, 32, wait_core, 0)

    def wait_piece(r, carry):
        @pl.when((x != zl) | (r != rest))
        def _():
            remote(
                kv_send.at[0], got.at[pl.ds(r * 4, 4)], p1_s.at[0], p1_r.at[r], (zl * 16 + r, x)
            ).wait_recv()

        return carry

    lax.fori_loop(0, 16, wait_piece, 0)

    @pl.when(x == zl)
    def _():
        own_piece.wait()

    def plane(n):
        return remote(
            picked.at[n], kv_all.at[:, :, mine], p2_s.at[n], p2_r.at[mine], half_plane(n)
        )

    def pick(n):
        for i in range(7):
            picked[n, :, i] = got[table[n, i]]

    def send_plane(o, carry):
        n = (mine + o) % 32
        pick(n)
        plane(n).start()
        return carry

    lax.fori_loop(1, 32, send_plane, 0)
    pick(mine)
    own_plane = pltpu.make_async_copy(picked.at[mine], kv_all.at[:, :, mine], loc.at[2])
    own_plane.start()

    def heads(n):
        return pl.ds(n * 2, 2)

    def x_step(n, o):
        to = (x + o) % 4
        return remote(
            q_send.at[heads(n), to], qx.at[heads(n), x], qx_s.at[n, o], qx_r.at[n, o],
            (ctx_of(to, y, zh, k), zl),
        )

    def z_step(n, src, to):
        o = (to - zl + 4) % 4
        return remote(
            src.at[heads(n), to], q_out.at[heads(n), zl], qz_s.at[n, o], qz_r.at[n, o], (me, to)
        )

    def z_move(n, src, frm):
        @pl.when(frm != zl)
        def _():
            z_step(n, src, frm).start()

        @pl.when(frm == zl)
        def _():
            pltpu.make_async_copy(
                src.at[heads(n), frm], q_out.at[heads(n), zl], loc.at[3 + n]
            ).start()

    def project(n, carry):
        columns = pl.ds(pl.multiple_of(n * 256, 256), 256)
        both = jnp.dot(tok_all[...], wq_all[:, columns], preferred_element_type=F32)
        for h in range(2):
            head = turn(both[:, h * 128 : h * 128 + 128], q_gain)
            q_send[n * 2 + h] = head.reshape(4, quarter, 128)
        for o in (1, 3, 2):
            x_step(n, o).start()
        z_move(n, q_send, x)
        return carry

    lax.fori_loop(0, 4, project, 0)

    def pass_on(n, carry):
        for o in (1, 3, 2):
            frm = (x - o + 4) % 4
            remote(
                q_send.at[heads(n), 0], qx.at[heads(n), frm], qx_s.at[n, o], qx_r.at[n, o],
                (ctx_of(frm, y, zh, k), zl),
            ).wait_recv()
            z_move(n, qx, frm)
        return carry

    lax.fori_loop(0, 4, pass_on, 0)

    def drain_q(n, carry):
        pltpu.make_async_copy(
            q_send.at[heads(n), 0], q_out.at[heads(n), zl], loc.at[3 + n]
        ).wait()
        for o in (1, 2, 3):
            x_step(n, o).wait_send()
            z_step(n, q_send, (zl + o) % 4).wait_send()
            frm = (zl - o + 4) % 4
            remote(
                q_send.at[heads(n), 0], q_out.at[heads(n), frm], qz_s.at[n, o], qz_r.at[n, o],
                (me, frm),
            ).wait_recv()
        return carry

    lax.fori_loop(0, 4, drain_q, 0)

    def drain_piece(r, carry):
        @pl.when((x != zl) | (r != rest))
        def _():
            piece(r).wait_send()

        return carry

    lax.fori_loop(0, 16, drain_piece, 0)
    own_plane.wait()

    def drain_plane(o, carry):
        n = (mine + o) % 32
        plane(n).wait_send()
        remote(
            picked.at[n], kv_all.at[:, :, n], p2_s.at[n], p2_r.at[n], half_plane(n)
        ).wait_recv()
        return carry

    lax.fori_loop(1, 32, drain_plane, 0)

    def drain_core(n, carry):
        core(n, any_w).wait_send()
        return carry

    lax.fori_loop(0, 32, drain_core, 0)

    def drain_y(s, carry):
        right, left = y_own(s, any_w)
        right.wait_send()
        left.wait_send()
        return carry

    lax.fori_loop(0, 8, drain_y, 0)

    def drain_four(i, carry):
        zp(i).wait_send()
        fwd_right(i, any_w).wait_send()
        fwd_left(i, any_w).wait_send()

        @pl.when((d == 0) | (d >= 2))
        def _():
            zm(i, zh_u).wait_send()
            km(i).wait_send()

        @pl.when(d <= 2)
        def _():
            kp(i).wait_send()

        @pl.when(d != 0)
        def _():
            kv_core(i, key_part(i)).wait_send()
            kv_core(4 + i, value_part(i)).wait_send()

        return carry

    lax.fori_loop(0, 4, drain_four, 0)
    for copy in sends:
        copy.wait_send()
    fwd_a.wait_send()
    fwd_b.wait_send()

    @pl.when(d != 0)
    def _():
        w1.wait_send()


def front(table, tokens, norm_gain, w_query, w_key, w_value, q_gain, k_gain, cosine, sine):
    vmem = pl.BlockSpec(memory_space=pltpu.VMEM)
    hbm = pl.BlockSpec(memory_space=pl.ANY)
    dma = pltpu.SemaphoreType.DMA
    pair = lambda *n: [dma(n), dma(n)]
    rows, width = tokens.shape
    columns = w_query.shape[1]
    flops = 2 * 4 * rows * width * (columns + 256)
    return pl.pallas_call(
        front_kernel,
        out_shape=(
            jax.ShapeDtypeStruct((8, 4, rows, 128), BF16),
            jax.ShapeDtypeStruct((2, 7, 32, 16, 128), BF16),
        ),
        in_specs=[pl.BlockSpec(memory_space=pltpu.SMEM)] + [vmem] * 9,
        out_specs=(hbm, hbm),
        scratch_shapes=[
            pltpu.VMEM((4 * rows, width), BF16),
            pltpu.VMEM((width, columns), BF16),
            pltpu.VMEM((width, 256), BF16),
            pltpu.VMEM((8, 4, rows, 128), BF16),
            pltpu.VMEM((8, 4, rows, 128), BF16),
            pltpu.VMEM((8, 4, 2, 16, 128), BF16),
            pltpu.VMEM((64, 2, 16, 128), BF16),
            pltpu.VMEM((32, 2, 7, 16, 128), BF16),
            dma((7,)),
        ] + pair(6) + [dma((1,)), dma((4,))] + pair(4) + pair(4) + pair(8) + pair(8)
        + pair(4) + pair(4) + pair(32) + pair(4) + pair(4) + pair(8)
        + pair(4, 4) + pair(4, 4) + pair(16) + pair(32),
        cost_estimate=pl.CostEstimate(flops=flops, bytes_accessed=10 << 20, transcendentals=0),
        compiler_params=pltpu.CompilerParams(
            collective_id=0, has_side_effects=True, vmem_limit_bytes=50 << 20
        ),
    )(table, tokens, norm_gain, w_query, w_key, w_value, q_gain, k_gain, cosine, sine)


def attend_kernel(start_ref, q_ref, kv_ref, o_ref):
    _, length, head_size = q_ref.shape
    step = 256
    scale = head_size ** (-0.5) * math.log2(math.e)
    for r in range(length // step):
        rows = pl.ds(r * step, step)
        q = q_ref[0, rows, :]
        start = start_ref[rows, :]
        tiles = []
        top = None
        for i in range(7):
            scores = lax.dot_general(
                q, kv_ref[0, i], (((1,), (1,)), ((), ())), preferred_element_type=F32
            )
            at = lax.broadcasted_iota(jnp.int32, scores.shape, 1) + (i - 6) * length
            allowed = at >= start
            if i == 6:
                here = lax.broadcasted_iota(jnp.int32, scores.shape, 0) + r * step
                allowed = allowed & (at <= here)
            scores = jnp.where(allowed, scores, -1e30)
            tiles.append(scores)
            best = jnp.max(scores, -1, keepdims=True)
            top = best if top is None else jnp.maximum(top, best)
        total = None
        summed = None
        for i in range(7):
            weights = jnp.exp2((tiles[i] - top) * scale)
            added = jnp.sum(weights, -1, keepdims=True)
            part = jnp.dot(weights.astype(BF16), kv_ref[1, i], preferred_element_type=F32)
            total = added if total is None else total + added
            summed = part if summed is None else summed + part
        o_ref[rows, :] = (summed / total).astype(BF16)


def attend(start, q, kv):
    heads, length, size = q.shape
    return pl.pallas_call(
        attend_kernel,
        grid=(heads,),
        out_shape=jax.ShapeDtypeStruct((length, heads * size), BF16),
        in_specs=[
            pl.BlockSpec((length, 1), lambda h: (0, 0)),
            pl.BlockSpec((1, length, size), lambda h: (h, 0, 0)),
            pl.BlockSpec(kv.shape, lambda h: (0, 0, 0, 0)),
        ],
        out_specs=pl.BlockSpec((length, size), lambda h: (0, h)),
        compiler_params=pltpu.CompilerParams(vmem_limit_bytes=48 << 20),
    )(start, q, kv)


def shards(tokens, norm_gain, w_query, w_key, w_value, query_gain, key_gain, segments, block_of):
    x, y, zh, k, zl = place()
    rest = y * 4 + zh * 2 + k
    quarter = tokens.shape[0]
    length = quarter * 4

    ids = jnp.arange(48, dtype=jnp.int32)
    starts = jnp.sum((segments[None, :] < ids[:, None]).astype(jnp.int32), 1)

    def start_of(at, size):
        doc = lax.dynamic_slice_in_dim(segments, at, size, 0)
        return jnp.sum(jnp.where(doc[:, None] == ids[None, :], starts[None, :], 0), 1)

    offsets = []
    for other in range(4):
        at = block_of[other * 16 + rest] * length + zl * quarter
        offsets.append(at + jnp.arange(quarter, dtype=jnp.int32) - start_of(at, quarter))
    offsets = jnp.concatenate(offsets)

    angles = offsets.astype(F32)[:, None] * jnp.asarray(yarn_frequencies(128), F32)[None, :]
    scale = 0.1 * math.log(4.0) + 1.0
    cosine, sine = jnp.cos(angles) * scale, jnp.sin(angles) * scale
    cosine = jnp.concatenate([cosine, cosine], -1)
    sine = jnp.concatenate([-sine, sine], -1)

    blocks = jnp.arange(64, dtype=jnp.int32)
    holder = jnp.sum(jnp.where(block_of[None, :] == blocks[:, None], blocks[None, :], 0), 1)
    d = jnp.arange(32, dtype=jnp.int32)
    wanted = block_of[ctx_of(d // 8, (d // 2) % 4, zh, d % 2)][:, None] - 6 + jnp.arange(7)[None, :]
    source = holder[jnp.maximum(wanted, 0)]
    table = (source % 16) * 4 + source // 16

    q_mine, kv = front(
        table, tokens, norm_gain[None, :], w_query, w_key, w_value,
        query_gain[None, :], key_gain[None, :], cosine, sine,
    )
    first = block_of[x * 16 + rest] * length
    start = (start_of(first, length) - first)[:, None]
    return attend(start, q_mine.reshape(8, length, 128), kv.reshape(2, 7, length, 128))


def solution(mesh):
    return jax.shard_map(
        shards,
        mesh=mesh,
        in_specs=(
            P(("context", "tensor"), None),
            P(),
            P("context", "tensor"),
            P(None, "tensor"),
            P(None, "tensor"),
            P(),
            P(),
            P(),
            P(),
        ),
        out_specs=P("context", "tensor"),
        check_vma=False,
    )
```

```python
import math

import jax
import jax.numpy as jnp
from jax import lax
from jax.experimental import pallas as pl
from jax.experimental.pallas import tpu as pltpu
from jax.sharding import PartitionSpec as P

MESH = pl.DeviceIdType.MESH
BF16 = jnp.bfloat16
F32 = jnp.float32
STEPS = (
    (1, 0), (0, 1), (3, 0), (0, 3), (1, 1), (3, 3), (1, 3), (3, 1),
    (2, 0), (0, 2), (2, 1), (1, 2), (2, 3), (3, 2), (2, 2),
)
PLACES = ((0, 0, 1),) + tuple((dx, dy, dk) for dk in (0, 1) for dx, dy in STEPS)


def yarn_frequencies(dim):
    theta = 1000000.0
    factor = 4.0
    initial = 32768.0
    lowest = math.floor(dim * math.log(initial / (32.0 * 2 * math.pi)) / (2 * math.log(theta)))
    highest = math.ceil(dim * math.log(initial / (1.0 * 2 * math.pi)) / (2 * math.log(theta)))
    lowest = max(lowest, 0)
    highest = min(highest, dim - 1)
    spread = max(highest - lowest, 0.001)
    result = []
    for index in range(dim // 2):
        base_freq = theta ** (-2.0 * index / dim)
        ramp = min(max((index - lowest) / spread, 0.0), 1.0)
        result.append(base_freq / factor * ramp + base_freq * (1.0 - ramp))
    return result


def ctx_of(x, y, zh, k):
    return x * 16 + y * 4 + zh * 2 + k


def place():
    c = lax.axis_index("context")
    return c // 16, (c // 4) % 4, (c // 2) % 2, c % 2, lax.axis_index("tensor")


def front_kernel(
    table, tok, norm_gain, wq, wk, wv, q_gain, k_gain, cosine, sine,
    q_out, kv_all,
    tok_all, wq_all, wkv_all, q_send, qx, kv_send, got, picked,
    loc, tok_s, tok_r, w1_s, w1_r, zp_s, zp_r, zm_s, zm_r,
    yr_s, yr_r, yl_s, yl_r, fr_s, fr_r, fl_s, fl_r, co_s, co_r,
    kp_s, kp_r, km_s, km_r, kc_s, kc_r,
    qx_s, qx_r, qz_s, qz_r, p1_s, p1_r, p2_s, p2_r,
):
    x, y, zh, k, zl = place()
    me = ctx_of(x, y, zh, k)
    z = zh * 4 + zl
    d = (zl - x + 4) % 4
    zh_u = ((z - d + 8) % 8) // 4
    zh_d = 1 - zh_u

    def at_z(pos):
        pos = pos % 8
        return (ctx_of(x, y, pos // 4, k), pos % 4)

    up, down = at_z(z + 1), at_z(z + 7)
    x_dev = [(ctx_of((x + o) % 4, y, zh, k), zl) for o in range(4)]
    y_right, y_left = (ctx_of(x, (y + 1) % 4, zh, k), zl), (ctx_of(x, (y + 3) % 4, zh, k), zl)
    other = (ctx_of(x, y, zh, 1 - k), zl)

    rest = y * 4 + zh * 2 + k
    mine = x * 8 + y * 2 + k

    def half_plane(n):
        return (ctx_of(n // 8, (n // 2) % 4, zh, n % 2), zl)

    barrier = pltpu.get_barrier_semaphore()

    def greet(dev):
        pl.semaphore_signal(barrier, inc=1, device_id=dev, device_id_type=MESH)

    for dev in (x_dev[1], x_dev[2], x_dev[3], up, down, y_right, y_left, other):
        greet(dev)
    for o in range(1, 4):
        greet((me, (zl + o) % 4))

    def greet_piece(r, carry):
        @pl.when((x != zl) | (r != rest))
        def _():
            greet((zl * 16 + r, x))

        return carry

    lax.fori_loop(0, 16, greet_piece, 0)

    def greet_plane(o, carry):
        greet(half_plane((mine + o) % 32))
        return carry

    lax.fori_loop(1, 32, greet_plane, 0)

    quarter = tok.shape[0]
    width = tok.shape[1]

    def norm_rows(n, carry):
        rows = pl.ds(pl.multiple_of(n * 16, 16), 16)
        wide = tok[rows, :].astype(F32)
        mean = jnp.mean(wide * wide, -1, keepdims=True)
        wide = wide * lax.rsqrt(mean + 1e-06) * norm_gain[...]
        tok_all[pl.ds(pl.multiple_of(x * quarter + n * 16, 16), 16), :] = wide.astype(BF16)
        return carry

    lax.fori_loop(0, quarter // 16, norm_rows, 0)
    pl.semaphore_wait(barrier, 8 + 3 + 15 + 31 + ((x - zl + 4) % 4 + 3) // 4)

    def remote(src, dst, ss, rs, dev):
        return pltpu.make_async_remote_copy(
            src_ref=src, dst_ref=dst, send_sem=ss, recv_sem=rs, device_id=dev, device_id_type=MESH
        )

    half = quarter // 2

    def tok_copy(n, slot, part, dev):
        ref = tok_all.at[pl.ds(pl.multiple_of(slot * quarter + part * half, 16), half)]
        return remote(ref, ref, tok_s.at[n], tok_r.at[n], dev)

    def w_slot(c):
        return wq_all.at[pl.ds(pl.multiple_of(c * w_rows, 16), w_rows)]

    w_rows = wq.shape[0]
    sends = [
        tok_copy(0, x, 0, x_dev[1]),
        tok_copy(3, x, 1, x_dev[3]),
        tok_copy(1, x, 1, x_dev[1]),
        tok_copy(2, x, 0, x_dev[3]),
    ]
    w1_index = (x - zl + 4) % 4
    w1 = remote(wq, w_slot(me), w1_s.at[0], w1_r.at[w1_index], (ctx_of(zl, y, zh, k), zl))
    own_w = pltpu.make_async_copy(wq, w_slot(me), loc.at[1])

    @pl.when(d != 0)
    def _():
        w1.start()

    @pl.when(d == 0)
    def _():
        own_w.start()

    for copy in sends:
        copy.start()

    @pl.when(d == 0)
    def _():
        wkv_all[:, :128] = wk[...]
        wkv_all[:, 128:] = wv[...]

    def slot(i, zhalf, yy):
        return w_slot(ctx_of((x + i) % 4, yy, zhalf, k))

    def zp(i):
        ref = slot(i, zh_u, y)
        return remote(ref, ref, zp_s.at[i], zp_r.at[i], up)

    def zm(i, zhalf):
        ref = slot(i, zhalf, y)
        return remote(ref, ref, zm_s.at[i], zm_r.at[i], down)

    def core(n, ref):
        return remote(ref, ref, co_s.at[n], co_r.at[n], other)

    def y_own(s, ref):
        return (
            remote(ref, ref, yr_s.at[s], yr_r.at[s], y_right),
            remote(ref, ref, yl_s.at[s], yl_r.at[s], y_left),
        )

    def fwd_right(i2, ref):
        return remote(ref, ref, fr_s.at[i2], fr_r.at[i2], y_right)

    def fwd_left(i2, ref):
        return remote(ref, ref, fl_s.at[i2], fl_r.at[i2], y_left)

    def spread(s, ref):
        right, left = y_own(s, ref)
        right.start()
        left.start()
        core(s, ref).start()

    def in_order(upper, lower):
        def step(t, carry):
            i = t - d

            @pl.when((i >= 0) & (i < 4))
            def _():
                upper(i)

            j = t - 4 + d

            @pl.when((j >= 0) & (j < 4))
            def _():
                lower(j)

            return carry

        lax.fori_loop(0, 8, step, 0)

    def z_upper(i):
        ref = slot(i, zh_u, y)

        @pl.when(d == 0)
        def _():
            @pl.when(i == 0)
            def _():
                own_w.wait()

            @pl.when(i != 0)
            def _():
                remote(ref, ref, w1_s.at[0], w1_r.at[i], other).wait_recv()

            zm(i, zh_u).start()

        @pl.when(d != 0)
        def _():
            zp(i).wait_recv()

        zp(i).start()
        spread(i, ref)

    def z_lower(i):
        ref = slot(i, zh_d, y)

        @pl.when(d == 0)
        def _():
            remote(ref, ref, zp_s.at[i], zp_r.at[i], up).wait_recv()

        @pl.when(d != 0)
        def _():
            zm(i, zh_d).wait_recv()

        @pl.when(d >= 2)
        def _():
            zm(i, zh_d).start()

        spread(4 + i, ref)

    in_order(z_upper, z_lower)

    left_x, right_x, far_x = (x + 3) % 4, (x + 1) % 4, (x + 2) % 4
    tok_copy(0, left_x, 0, x_dev[1]).wait_recv()
    fwd_a = tok_copy(4, left_x, 0, x_dev[1])
    fwd_a.start()
    tok_copy(3, right_x, 1, x_dev[3]).wait_recv()
    fwd_b = tok_copy(5, right_x, 1, x_dev[3])
    fwd_b.start()

    rows = wk.shape[0] // 8

    def part(i):
        return pl.ds(pl.multiple_of((k * 4 + i) * rows, 16), rows)

    def key_part(i):
        return wkv_all.at[part(i), pl.ds(0, 128)]

    def value_part(i):
        return wkv_all.at[part(i), pl.ds(128, 128)]

    def kv_core(n, ref):
        return remote(ref, ref, kc_s.at[n], kc_r.at[n], other)

    def kp(i):
        return remote(key_part(i), key_part(i), kp_s.at[i], kp_r.at[i], up)

    def km(i):
        return remote(value_part(i), value_part(i), km_s.at[i], km_r.at[i], down)

    y_l, y_r, y_far = (y + 3) % 4, (y + 1) % 4, (y + 2) % 4

    def ring(i, s, zhalf):
        ref = slot(i, zhalf, y_l)
        y_own(s, ref)[0].wait_recv()

        @pl.when(i % 2 == 0)
        def _():
            fwd_right(s // 2, ref).start()

        core(8 + s, ref).start()
        ref2 = slot(i, zhalf, y_r)
        y_own(s, ref2)[1].wait_recv()

        @pl.when(i % 2 == 1)
        def _():
            fwd_left(s // 2, ref2).start()

        core(16 + s, ref2).start()

    def kv_upper(i):
        @pl.when(d == 0)
        def _():
            kp(i).start()
            km(i).start()

        @pl.when(d != 0)
        def _():
            kp(i).wait_recv()
            kv_core(i, key_part(i)).start()

        @pl.when((d == 1) | (d == 2))
        def _():
            kp(i).start()

        ring(i, i, zh_u)

    def kv_lower(i):
        @pl.when(d != 0)
        def _():
            km(i).wait_recv()
            kv_core(4 + i, value_part(i)).start()

        @pl.when(d >= 2)
        def _():
            km(i).start()

        ring(i, 4 + i, zh_d)

    in_order(kv_upper, kv_lower)

    tok_copy(1, left_x, 1, x_dev[1]).wait_recv()
    tok_copy(2, right_x, 0, x_dev[3]).wait_recv()
    tok_copy(4, far_x, 0, x_dev[1]).wait_recv()
    tok_copy(5, far_x, 1, x_dev[3]).wait_recv()

    @pl.when(d != 0)
    def _():
        def core_part(i, carry):
            kv_core(i, key_part(i)).wait_recv()
            kv_core(4 + i, value_part(i)).wait_recv()
            return carry

        lax.fori_loop(0, 4, core_part, 0)

    def turn(t, gain):
        t = t * lax.rsqrt(jnp.mean(t * t, -1, keepdims=True) + 1e-06) * gain[...]
        return (t * cosine[...] + pltpu.roll(t, 64, 1) * sine[...]).astype(BF16)

    both = jnp.dot(tok_all[...], wkv_all[...], preferred_element_type=F32)
    key = turn(both[:, :128], k_gain)
    value = both[:, 128:].astype(BF16)
    for p in range(8):
        for n in range(4):
            at = n * 128 + p * 16
            kv_send[p, n, 0] = key[at : at + 16]
            kv_send[p, n, 1] = value[at : at + 16]

    def piece(r):
        p = (r // 4) * 2 + r % 2
        return remote(
            kv_send.at[p], got.at[pl.ds(rest * 4, 4)], p1_s.at[r], p1_r.at[rest], (zl * 16 + r, x)
        )

    own_piece = pltpu.make_async_copy(
        kv_send.at[(rest // 4) * 2 + rest % 2], got.at[pl.ds(rest * 4, 4)], loc.at[0]
    )

    def send_piece(o, carry):
        r = (rest + o) % 16

        @pl.when((x != zl) | (r != rest))
        def _():
            piece(r).start()

        return carry

    lax.fori_loop(0, 16, send_piece, 0)

    @pl.when(x == zl)
    def _():
        own_piece.start()

    def far_upper(i):
        finish(i, i, zh_u)

    def far_lower(i):
        finish(i, 4 + i, zh_d)

    def finish(i, s, zhalf):
        ref = slot(i, zhalf, y_far)

        @pl.when(i % 2 == 0)
        def _():
            fwd_right(s // 2, ref).wait_recv()

        @pl.when(i % 2 == 1)
        def _():
            fwd_left(s // 2, ref).wait_recv()

        core(24 + s, ref).start()

    in_order(far_upper, far_lower)

    any_w = w_slot(me)

    def wait_core(n, carry):
        core(n, any_w).wait_recv()
        return carry

    lax.fori_loop(0, 32, wait_core, 0)

    def heads(n):
        return pl.ds(n * 2, 2)

    def x_step(n, o):
        to = (x + o) % 4
        return remote(
            q_send.at[heads(n), to], qx.at[heads(n), x], qx_s.at[n, o], qx_r.at[n, o],
            (ctx_of(to, y, zh, k), zl),
        )

    def z_step(n, src, to):
        o = (to - zl + 4) % 4
        return remote(
            src.at[heads(n), to], q_out.at[heads(n), zl], qz_s.at[n, o], qz_r.at[n, o], (me, to)
        )

    def z_move(n, src, frm):
        @pl.when(frm != zl)
        def _():
            z_step(n, src, frm).start()

        @pl.when(frm == zl)
        def _():
            pltpu.make_async_copy(
                src.at[heads(n), frm], q_out.at[heads(n), zl], loc.at[3 + n]
            ).start()

    def project(n, carry):
        columns = pl.ds(pl.multiple_of(n * 256, 256), 256)
        both = jnp.dot(tok_all[...], wq_all[:, columns], preferred_element_type=F32)
        for h in range(2):
            head = turn(both[:, h * 128 : h * 128 + 128], q_gain)
            q_send[n * 2 + h] = head.reshape(4, quarter, 128)
        for o in (1, 3, 2):
            x_step(n, o).start()
        z_move(n, q_send, x)
        return carry

    lax.fori_loop(0, 4, project, 0)

    def wait_piece(r, carry):
        @pl.when((x != zl) | (r != rest))
        def _():
            remote(
                kv_send.at[0], got.at[pl.ds(r * 4, 4)], p1_s.at[0], p1_r.at[r], (zl * 16 + r, x)
            ).wait_recv()

        return carry

    lax.fori_loop(0, 16, wait_piece, 0)

    @pl.when(x == zl)
    def _():
        own_piece.wait()

    def plane(n):
        return remote(
            picked.at[n], kv_all.at[:, :, mine], p2_s.at[n], p2_r.at[mine], half_plane(n)
        )

    def pick(n):
        for i in range(7):
            picked[n, :, i] = got[table[n, i]]

    for dx, dy, dk in PLACES:
        n = ((x + dx) % 4) * 8 + ((y + dy) % 4) * 2 + (k + dk) % 2
        pick(n)
        plane(n).start()
    pick(mine)
    own_plane = pltpu.make_async_copy(picked.at[mine], kv_all.at[:, :, mine], loc.at[2])
    own_plane.start()

    def pass_on(n, carry):
        for o in (1, 3, 2):
            frm = (x - o + 4) % 4
            remote(
                q_send.at[heads(n), 0], qx.at[heads(n), frm], qx_s.at[n, o], qx_r.at[n, o],
                (ctx_of(frm, y, zh, k), zl),
            ).wait_recv()
            z_move(n, qx, frm)
        return carry

    lax.fori_loop(0, 4, pass_on, 0)

    def drain_q(n, carry):
        pltpu.make_async_copy(
            q_send.at[heads(n), 0], q_out.at[heads(n), zl], loc.at[3 + n]
        ).wait()
        for o in (1, 2, 3):
            x_step(n, o).wait_send()
            z_step(n, q_send, (zl + o) % 4).wait_send()
            frm = (zl - o + 4) % 4
            remote(
                q_send.at[heads(n), 0], q_out.at[heads(n), frm], qz_s.at[n, o], qz_r.at[n, o],
                (me, frm),
            ).wait_recv()
        return carry

    lax.fori_loop(0, 4, drain_q, 0)

    def drain_piece(r, carry):
        @pl.when((x != zl) | (r != rest))
        def _():
            piece(r).wait_send()

        return carry

    lax.fori_loop(0, 16, drain_piece, 0)
    own_plane.wait()

    def drain_plane(o, carry):
        n = (mine + o) % 32
        plane(n).wait_send()
        remote(
            picked.at[n], kv_all.at[:, :, n], p2_s.at[n], p2_r.at[n], half_plane(n)
        ).wait_recv()
        return carry

    lax.fori_loop(1, 32, drain_plane, 0)

    def drain_core(n, carry):
        core(n, any_w).wait_send()
        return carry

    lax.fori_loop(0, 32, drain_core, 0)

    def drain_y(s, carry):
        right, left = y_own(s, any_w)
        right.wait_send()
        left.wait_send()
        return carry

    lax.fori_loop(0, 8, drain_y, 0)

    def drain_four(i, carry):
        zp(i).wait_send()
        fwd_right(i, any_w).wait_send()
        fwd_left(i, any_w).wait_send()

        @pl.when((d == 0) | (d >= 2))
        def _():
            zm(i, zh_u).wait_send()
            km(i).wait_send()

        @pl.when(d <= 2)
        def _():
            kp(i).wait_send()

        @pl.when(d != 0)
        def _():
            kv_core(i, key_part(i)).wait_send()
            kv_core(4 + i, value_part(i)).wait_send()

        return carry

    lax.fori_loop(0, 4, drain_four, 0)
    for copy in sends:
        copy.wait_send()
    fwd_a.wait_send()
    fwd_b.wait_send()

    @pl.when(d != 0)
    def _():
        w1.wait_send()


def front(table, tokens, norm_gain, w_query, w_key, w_value, q_gain, k_gain, cosine, sine):
    vmem = pl.BlockSpec(memory_space=pltpu.VMEM)
    hbm = pl.BlockSpec(memory_space=pl.ANY)
    dma = pltpu.SemaphoreType.DMA
    pair = lambda *n: [dma(n), dma(n)]
    rows, width = tokens.shape
    columns = w_query.shape[1]
    flops = 2 * 4 * rows * width * (columns + 256)
    return pl.pallas_call(
        front_kernel,
        out_shape=(
            jax.ShapeDtypeStruct((8, 4, rows, 128), BF16),
            jax.ShapeDtypeStruct((2, 7, 32, 16, 128), BF16),
        ),
        in_specs=[pl.BlockSpec(memory_space=pltpu.SMEM)] + [vmem] * 9,
        out_specs=(hbm, hbm),
        scratch_shapes=[
            pltpu.VMEM((4 * rows, width), BF16),
            pltpu.VMEM((width, columns), BF16),
            pltpu.VMEM((width, 256), BF16),
            pltpu.VMEM((8, 4, rows, 128), BF16),
            pltpu.VMEM((8, 4, rows, 128), BF16),
            pltpu.VMEM((8, 4, 2, 16, 128), BF16),
            pltpu.VMEM((64, 2, 16, 128), BF16),
            pltpu.VMEM((32, 2, 7, 16, 128), BF16),
            dma((7,)),
        ] + pair(6) + [dma((1,)), dma((4,))] + pair(4) + pair(4) + pair(8) + pair(8)
        + pair(4) + pair(4) + pair(32) + pair(4) + pair(4) + pair(8)
        + pair(4, 4) + pair(4, 4) + pair(16) + pair(32),
        cost_estimate=pl.CostEstimate(flops=flops, bytes_accessed=10 << 20, transcendentals=0),
        compiler_params=pltpu.CompilerParams(
            collective_id=0, has_side_effects=True, vmem_limit_bytes=50 << 20
        ),
    )(table, tokens, norm_gain, w_query, w_key, w_value, q_gain, k_gain, cosine, sine)


def attend_kernel(start_ref, q_ref, kv_ref, o_ref):
    _, length, head_size = q_ref.shape
    step = 256
    scale = head_size ** (-0.5) * math.log2(math.e)
    for r in range(length // step):
        rows = pl.ds(r * step, step)
        q = q_ref[0, rows, :]
        start = start_ref[rows, :]
        tiles = []
        top = None
        for i in range(7):
            scores = lax.dot_general(
                q, kv_ref[0, i], (((1,), (1,)), ((), ())), preferred_element_type=F32
            )
            at = lax.broadcasted_iota(jnp.int32, scores.shape, 1) + (i - 6) * length
            allowed = at >= start
            if i == 6:
                here = lax.broadcasted_iota(jnp.int32, scores.shape, 0) + r * step
                allowed = allowed & (at <= here)
            scores = jnp.where(allowed, scores, -1e30)
            tiles.append(scores)
            best = jnp.max(scores, -1, keepdims=True)
            top = best if top is None else jnp.maximum(top, best)
        total = None
        summed = None
        for i in range(7):
            weights = jnp.exp2((tiles[i] - top) * scale)
            added = jnp.sum(weights, -1, keepdims=True)
            part = jnp.dot(weights.astype(BF16), kv_ref[1, i], preferred_element_type=F32)
            total = added if total is None else total + added
            summed = part if summed is None else summed + part
        o_ref[rows, :] = (summed / total).astype(BF16)


def attend(start, q, kv):
    heads, length, size = q.shape
    return pl.pallas_call(
        attend_kernel,
        grid=(heads,),
        out_shape=jax.ShapeDtypeStruct((length, heads * size), BF16),
        in_specs=[
            pl.BlockSpec((length, 1), lambda h: (0, 0)),
            pl.BlockSpec((1, length, size), lambda h: (h, 0, 0)),
            pl.BlockSpec(kv.shape, lambda h: (0, 0, 0, 0)),
        ],
        out_specs=pl.BlockSpec((length, size), lambda h: (0, h)),
        compiler_params=pltpu.CompilerParams(vmem_limit_bytes=48 << 20),
    )(start, q, kv)


def shards(tokens, norm_gain, w_query, w_key, w_value, query_gain, key_gain, segments, block_of):
    x, y, zh, k, zl = place()
    rest = y * 4 + zh * 2 + k
    quarter = tokens.shape[0]
    length = quarter * 4

    ids = jnp.arange(48, dtype=jnp.int32)
    starts = jnp.sum((segments[None, :] < ids[:, None]).astype(jnp.int32), 1)

    def start_of(at, size):
        doc = lax.dynamic_slice_in_dim(segments, at, size, 0)
        return jnp.sum(jnp.where(doc[:, None] == ids[None, :], starts[None, :], 0), 1)

    offsets = []
    for other in range(4):
        at = block_of[other * 16 + rest] * length + zl * quarter
        offsets.append(at + jnp.arange(quarter, dtype=jnp.int32) - start_of(at, quarter))
    offsets = jnp.concatenate(offsets)

    angles = offsets.astype(F32)[:, None] * jnp.asarray(yarn_frequencies(128), F32)[None, :]
    scale = 0.1 * math.log(4.0) + 1.0
    cosine, sine = jnp.cos(angles) * scale, jnp.sin(angles) * scale
    cosine = jnp.concatenate([cosine, cosine], -1)
    sine = jnp.concatenate([-sine, sine], -1)

    blocks = jnp.arange(64, dtype=jnp.int32)
    holder = jnp.sum(jnp.where(block_of[None, :] == blocks[:, None], blocks[None, :], 0), 1)
    d = jnp.arange(32, dtype=jnp.int32)
    wanted = block_of[ctx_of(d // 8, (d // 2) % 4, zh, d % 2)][:, None] - 6 + jnp.arange(7)[None, :]
    source = holder[jnp.maximum(wanted, 0)]
    table = (source % 16) * 4 + source // 16

    q_mine, kv = front(
        table, tokens, norm_gain[None, :], w_query, w_key, w_value,
        query_gain[None, :], key_gain[None, :], cosine, sine,
    )
    first = block_of[x * 16 + rest] * length
    start = (start_of(first, length) - first)[:, None]
    return attend(start, q_mine.reshape(8, length, 128), kv.reshape(2, 7, length, 128))


def solution(mesh):
    return jax.shard_map(
        shards,
        mesh=mesh,
        in_specs=(
            P(("context", "tensor"), None),
            P(),
            P("context", "tensor"),
            P(None, "tensor"),
            P(None, "tensor"),
            P(),
            P(),
            P(),
            P(),
        ),
        out_specs=P("context", "tensor"),
        check_vma=False,
    )
```

```python
import math

import jax
import jax.numpy as jnp
from jax import lax
from jax.experimental import pallas as pl
from jax.experimental.pallas import tpu as pltpu
from jax.sharding import PartitionSpec as P

MESH = pl.DeviceIdType.MESH
BF16 = jnp.bfloat16
F32 = jnp.float32
STEPS = (
    (1, 0), (0, 1), (3, 0), (0, 3), (1, 1), (3, 3), (1, 3), (3, 1),
    (2, 0), (0, 2), (2, 1), (1, 2), (2, 3), (3, 2), (2, 2),
)
PLACES = ((0, 0, 1),) + tuple((dx, dy, dk) for dk in (0, 1) for dx, dy in STEPS)


def yarn_frequencies(dim):
    theta = 1000000.0
    factor = 4.0
    initial = 32768.0
    lowest = math.floor(dim * math.log(initial / (32.0 * 2 * math.pi)) / (2 * math.log(theta)))
    highest = math.ceil(dim * math.log(initial / (1.0 * 2 * math.pi)) / (2 * math.log(theta)))
    lowest = max(lowest, 0)
    highest = min(highest, dim - 1)
    spread = max(highest - lowest, 0.001)
    result = []
    for index in range(dim // 2):
        base_freq = theta ** (-2.0 * index / dim)
        ramp = min(max((index - lowest) / spread, 0.0), 1.0)
        result.append(base_freq / factor * ramp + base_freq * (1.0 - ramp))
    return result


def ctx_of(x, y, zh, k):
    return x * 16 + y * 4 + zh * 2 + k


def place():
    c = lax.axis_index("context")
    return c // 16, (c // 4) % 4, (c // 2) % 2, c % 2, lax.axis_index("tensor")


def front_kernel(
    table, tok, norm_gain, wq, wk, wv, q_gain, k_gain, cosine, sine,
    q_out, kv_all,
    tok_all, wq_all, wkv_all, q_send, qx, kv_send, got, picked,
    loc, tok_s, tok_r, w1_s, w1_r, zp_s, zp_r, zm_s, zm_r,
    yr_s, yr_r, yl_s, yl_r, fr_s, fr_r, fl_s, fl_r, co_s, co_r,
    kp_s, kp_r, km_s, km_r, kc_s, kc_r,
    qx_s, qx_r, qz_s, qz_r, p1_s, p1_r, p2_s, p2_r,
):
    x, y, zh, k, zl = place()
    me = ctx_of(x, y, zh, k)
    z = zh * 4 + zl
    d = (zl - x + 4) % 4
    zh_u = ((z - d + 8) % 8) // 4
    zh_d = 1 - zh_u

    def at_z(pos):
        pos = pos % 8
        return (ctx_of(x, y, pos // 4, k), pos % 4)

    up, down = at_z(z + 1), at_z(z + 7)
    x_dev = [(ctx_of((x + o) % 4, y, zh, k), zl) for o in range(4)]
    y_right, y_left = (ctx_of(x, (y + 1) % 4, zh, k), zl), (ctx_of(x, (y + 3) % 4, zh, k), zl)
    other = (ctx_of(x, y, zh, 1 - k), zl)

    rest = y * 4 + zh * 2 + k
    mine = x * 8 + y * 2 + k

    def half_plane(n):
        return (ctx_of(n // 8, (n // 2) % 4, zh, n % 2), zl)

    barrier = pltpu.get_barrier_semaphore()

    def greet(dev):
        pl.semaphore_signal(barrier, inc=1, device_id=dev, device_id_type=MESH)

    for dev in (x_dev[1], x_dev[2], x_dev[3], up, down, y_right, y_left, other):
        greet(dev)
    for o in range(1, 4):
        greet((me, (zl + o) % 4))

    def greet_piece(r, carry):
        @pl.when((x != zl) | (r != rest))
        def _():
            greet((zl * 16 + r, x))

        return carry

    lax.fori_loop(0, 16, greet_piece, 0)

    def greet_plane(o, carry):
        greet(half_plane((mine + o) % 32))
        return carry

    lax.fori_loop(1, 32, greet_plane, 0)

    quarter = tok.shape[0]
    width = tok.shape[1]

    def norm_rows(n, carry):
        rows = pl.ds(pl.multiple_of(n * 16, 16), 16)
        wide = tok[rows, :].astype(F32)
        mean = jnp.mean(wide * wide, -1, keepdims=True)
        wide = wide * lax.rsqrt(mean + 1e-06) * norm_gain[...]
        tok_all[pl.ds(pl.multiple_of(x * quarter + n * 16, 16), 16), :] = wide.astype(BF16)
        return carry

    lax.fori_loop(0, quarter // 16, norm_rows, 0)
    pl.semaphore_wait(barrier, 8 + 3 + 15 + 31 + ((x - zl + 4) % 4 + 3) // 4)

    def remote(src, dst, ss, rs, dev):
        return pltpu.make_async_remote_copy(
            src_ref=src, dst_ref=dst, send_sem=ss, recv_sem=rs, device_id=dev, device_id_type=MESH
        )

    half = quarter // 2

    def tok_copy(n, slot, part, dev):
        ref = tok_all.at[pl.ds(pl.multiple_of(slot * quarter + part * half, 16), half)]
        return remote(ref, ref, tok_s.at[n], tok_r.at[n], dev)

    def w_slot(c):
        return wq_all.at[pl.ds(pl.multiple_of(c * w_rows, 16), w_rows)]

    w_rows = wq.shape[0]
    sends = [
        tok_copy(0, x, 0, x_dev[1]),
        tok_copy(3, x, 1, x_dev[3]),
        tok_copy(1, x, 1, x_dev[1]),
        tok_copy(2, x, 0, x_dev[3]),
    ]
    w1_index = (x - zl + 4) % 4
    w1 = remote(wq, w_slot(me), w1_s.at[0], w1_r.at[w1_index], (ctx_of(zl, y, zh, k), zl))
    own_w = pltpu.make_async_copy(wq, w_slot(me), loc.at[1])

    @pl.when(d != 0)
    def _():
        w1.start()

    @pl.when(d == 0)
    def _():
        own_w.start()

    for copy in sends:
        copy.start()

    @pl.when(d == 0)
    def _():
        wkv_all[:, :128] = wk[...]
        wkv_all[:, 128:] = wv[...]

    def slot(i, zhalf, yy):
        return w_slot(ctx_of((x + i) % 4, yy, zhalf, k))

    def zp(i):
        ref = slot(i, zh_u, y)
        return remote(ref, ref, zp_s.at[i], zp_r.at[i], up)

    def zm(i, zhalf):
        ref = slot(i, zhalf, y)
        return remote(ref, ref, zm_s.at[i], zm_r.at[i], down)

    def core(n, ref):
        return remote(ref, ref, co_s.at[n], co_r.at[n], other)

    def y_own(s, ref):
        return (
            remote(ref, ref, yr_s.at[s], yr_r.at[s], y_right),
            remote(ref, ref, yl_s.at[s], yl_r.at[s], y_left),
        )

    def fwd_right(i2, ref):
        return remote(ref, ref, fr_s.at[i2], fr_r.at[i2], y_right)

    def fwd_left(i2, ref):
        return remote(ref, ref, fl_s.at[i2], fl_r.at[i2], y_left)

    def spread(s, ref):
        right, left = y_own(s, ref)
        right.start()
        left.start()
        core(s, ref).start()

    def when_four(i, act):
        @pl.when((i >= 0) & (i < 4))
        def _():
            act(i)

    def z_upper(i):
        ref = slot(i, zh_u, y)

        @pl.when(d == 0)
        def _():
            @pl.when(i == 0)
            def _():
                own_w.wait()

            @pl.when(i != 0)
            def _():
                remote(ref, ref, w1_s.at[0], w1_r.at[i], other).wait_recv()

            zm(i, zh_u).start()

        @pl.when(d != 0)
        def _():
            zp(i).wait_recv()

        zp(i).start()
        spread(i, ref)

    def z_lower(i):
        ref = slot(i, zh_d, y)

        @pl.when(d == 0)
        def _():
            remote(ref, ref, zp_s.at[i], zp_r.at[i], up).wait_recv()

        @pl.when(d != 0)
        def _():
            zm(i, zh_d).wait_recv()

        @pl.when(d >= 2)
        def _():
            zm(i, zh_d).start()

        spread(4 + i, ref)

    rows = wk.shape[0] // 8

    def part(i):
        return pl.ds(pl.multiple_of((k * 4 + i) * rows, 16), rows)

    def key_part(i):
        return wkv_all.at[part(i), pl.ds(0, 128)]

    def value_part(i):
        return wkv_all.at[part(i), pl.ds(128, 128)]

    def kv_core(n, ref):
        return remote(ref, ref, kc_s.at[n], kc_r.at[n], other)

    def kp(i):
        return remote(key_part(i), key_part(i), kp_s.at[i], kp_r.at[i], up)

    def km(i):
        return remote(value_part(i), value_part(i), km_s.at[i], km_r.at[i], down)

    y_l, y_r, y_far = (y + 3) % 4, (y + 1) % 4, (y + 2) % 4

    def ring(i, s, zhalf):
        ref = slot(i, zhalf, y_l)
        y_own(s, ref)[0].wait_recv()

        @pl.when(i % 2 == 0)
        def _():
            fwd_right(s // 2, ref).start()

        core(8 + s, ref).start()
        ref2 = slot(i, zhalf, y_r)
        y_own(s, ref2)[1].wait_recv()

        @pl.when(i % 2 == 1)
        def _():
            fwd_left(s // 2, ref2).start()

        core(16 + s, ref2).start()

    def kv_upper(i):
        @pl.when(d != 0)
        def _():
            kp(i).wait_recv()
            kv_core(i, key_part(i)).start()

            @pl.when(d != 3)
            def _():
                kp(i).start()

    def kv_lower(i):
        @pl.when(d != 0)
        def _():
            km(i).wait_recv()
            kv_core(4 + i, value_part(i)).start()

            @pl.when(d != 1)
            def _():
                km(i).start()

    def ring_upper(i):
        ring(i, i, zh_u)

    def ring_lower(i):
        ring(i, 4 + i, zh_d)

    def step(t, carry):
        when_four(t - d, z_upper)
        when_four(t - 4 + d, z_lower)

        @pl.when((d == 0) & (t == 3))
        def _():
            for i in range(4):
                kp(i).start()
                km(i).start()

        when_four(t - 4 - d, kv_upper)
        when_four(t - 8 + d, kv_lower)
        when_four(t - 4 - d, ring_upper)
        when_four(t - 8 + d, ring_lower)
        return carry

    lax.fori_loop(0, 7, step, 0)

    left_x, right_x, far_x = (x + 3) % 4, (x + 1) % 4, (x + 2) % 4
    tok_copy(0, left_x, 0, x_dev[1]).wait_recv()
    fwd_a = tok_copy(4, left_x, 0, x_dev[1])
    fwd_a.start()
    tok_copy(3, right_x, 1, x_dev[3]).wait_recv()
    fwd_b = tok_copy(5, right_x, 1, x_dev[3])
    fwd_b.start()

    lax.fori_loop(7, 12, step, 0)

    tok_copy(1, left_x, 1, x_dev[1]).wait_recv()
    tok_copy(2, right_x, 0, x_dev[3]).wait_recv()
    tok_copy(4, far_x, 0, x_dev[1]).wait_recv()
    tok_copy(5, far_x, 1, x_dev[3]).wait_recv()

    @pl.when(d != 0)
    def _():
        def core_part(i, carry):
            kv_core(i, key_part(i)).wait_recv()
            kv_core(4 + i, value_part(i)).wait_recv()
            return carry

        lax.fori_loop(0, 4, core_part, 0)

    def turn(t, gain):
        t = t * lax.rsqrt(jnp.mean(t * t, -1, keepdims=True) + 1e-06) * gain[...]
        return (t * cosine[...] + pltpu.roll(t, 64, 1) * sine[...]).astype(BF16)

    both = jnp.dot(tok_all[...], wkv_all[...], preferred_element_type=F32)
    key = turn(both[:, :128], k_gain)
    value = both[:, 128:].astype(BF16)
    for p in range(8):
        for n in range(4):
            at = n * 128 + p * 16
            kv_send[p, n, 0] = key[at : at + 16]
            kv_send[p, n, 1] = value[at : at + 16]

    def piece(r):
        p = (r // 4) * 2 + r % 2
        return remote(
            kv_send.at[p], got.at[pl.ds(rest * 4, 4)], p1_s.at[r], p1_r.at[rest], (zl * 16 + r, x)
        )

    own_piece = pltpu.make_async_copy(
        kv_send.at[(rest // 4) * 2 + rest % 2], got.at[pl.ds(rest * 4, 4)], loc.at[0]
    )

    def send_piece(o, carry):
        r = (rest + o) % 16

        @pl.when((x != zl) | (r != rest))
        def _():
            piece(r).start()

        return carry

    lax.fori_loop(0, 16, send_piece, 0)

    @pl.when(x == zl)
    def _():
        own_piece.start()

    def far_upper(i):
        finish(i, i, zh_u)

    def far_lower(i):
        finish(i, 4 + i, zh_d)

    def finish(i, s, zhalf):
        ref = slot(i, zhalf, y_far)

        @pl.when(i % 2 == 0)
        def _():
            fwd_right(s // 2, ref).wait_recv()

        @pl.when(i % 2 == 1)
        def _():
            fwd_left(s // 2, ref).wait_recv()

        core(24 + s, ref).start()

    def far_step(t, carry):
        when_four(t - d, far_upper)
        when_four(t - 4 + d, far_lower)
        return carry

    lax.fori_loop(0, 8, far_step, 0)

    any_w = w_slot(me)

    def wait_core(n, carry):
        core(n, any_w).wait_recv()
        return carry

    lax.fori_loop(0, 32, wait_core, 0)

    def heads(n):
        return pl.ds(n * 2, 2)

    def x_step(n, o):
        to = (x + o) % 4
        return remote(
            q_send.at[heads(n), to], qx.at[heads(n), x], qx_s.at[n, o], qx_r.at[n, o],
            (ctx_of(to, y, zh, k), zl),
        )

    def z_step(n, src, to):
        o = (to - zl + 4) % 4
        return remote(
            src.at[heads(n), to], q_out.at[heads(n), zl], qz_s.at[n, o], qz_r.at[n, o], (me, to)
        )

    def z_move(n, src, frm):
        @pl.when(frm != zl)
        def _():
            z_step(n, src, frm).start()

        @pl.when(frm == zl)
        def _():
            pltpu.make_async_copy(
                src.at[heads(n), frm], q_out.at[heads(n), zl], loc.at[3 + n]
            ).start()

    def project(n, carry):
        columns = pl.ds(pl.multiple_of(n * 256, 256), 256)
        both = jnp.dot(tok_all[...], wq_all[:, columns], preferred_element_type=F32)
        for h in range(2):
            head = turn(both[:, h * 128 : h * 128 + 128], q_gain)
            q_send[n * 2 + h] = head.reshape(4, quarter, 128)
        for o in (1, 3, 2):
            x_step(n, o).start()
        z_move(n, q_send, x)
        return carry

    lax.fori_loop(0, 4, project, 0)

    def wait_piece(r, carry):
        @pl.when((x != zl) | (r != rest))
        def _():
            remote(
                kv_send.at[0], got.at[pl.ds(r * 4, 4)], p1_s.at[0], p1_r.at[r], (zl * 16 + r, x)
            ).wait_recv()

        return carry

    lax.fori_loop(0, 16, wait_piece, 0)

    @pl.when(x == zl)
    def _():
        own_piece.wait()

    def plane(n):
        return remote(
            picked.at[n], kv_all.at[:, :, mine], p2_s.at[n], p2_r.at[mine], half_plane(n)
        )

    def pick(n):
        for i in range(7):
            picked[n, :, i] = got[table[n, i]]

    for dx, dy, dk in PLACES:
        n = ((x + dx) % 4) * 8 + ((y + dy) % 4) * 2 + (k + dk) % 2
        pick(n)
        plane(n).start()
    pick(mine)
    own_plane = pltpu.make_async_copy(picked.at[mine], kv_all.at[:, :, mine], loc.at[2])
    own_plane.start()

    def pass_on(n, carry):
        for o in (1, 3, 2):
            frm = (x - o + 4) % 4
            remote(
                q_send.at[heads(n), 0], qx.at[heads(n), frm], qx_s.at[n, o], qx_r.at[n, o],
                (ctx_of(frm, y, zh, k), zl),
            ).wait_recv()
            z_move(n, qx, frm)
        return carry

    lax.fori_loop(0, 4, pass_on, 0)

    def drain_q(n, carry):
        pltpu.make_async_copy(
            q_send.at[heads(n), 0], q_out.at[heads(n), zl], loc.at[3 + n]
        ).wait()
        for o in (1, 2, 3):
            x_step(n, o).wait_send()
            z_step(n, q_send, (zl + o) % 4).wait_send()
            frm = (zl - o + 4) % 4
            remote(
                q_send.at[heads(n), 0], q_out.at[heads(n), frm], qz_s.at[n, o], qz_r.at[n, o],
                (me, frm),
            ).wait_recv()
        return carry

    lax.fori_loop(0, 4, drain_q, 0)

    def drain_piece(r, carry):
        @pl.when((x != zl) | (r != rest))
        def _():
            piece(r).wait_send()

        return carry

    lax.fori_loop(0, 16, drain_piece, 0)
    own_plane.wait()

    def drain_plane(o, carry):
        n = (mine + o) % 32
        plane(n).wait_send()
        remote(
            picked.at[n], kv_all.at[:, :, n], p2_s.at[n], p2_r.at[n], half_plane(n)
        ).wait_recv()
        return carry

    lax.fori_loop(1, 32, drain_plane, 0)

    def drain_core(n, carry):
        core(n, any_w).wait_send()
        return carry

    lax.fori_loop(0, 32, drain_core, 0)

    def drain_y(s, carry):
        right, left = y_own(s, any_w)
        right.wait_send()
        left.wait_send()
        return carry

    lax.fori_loop(0, 8, drain_y, 0)

    def drain_four(i, carry):
        zp(i).wait_send()
        fwd_right(i, any_w).wait_send()
        fwd_left(i, any_w).wait_send()

        @pl.when((d == 0) | (d >= 2))
        def _():
            zm(i, zh_u).wait_send()
            km(i).wait_send()

        @pl.when(d <= 2)
        def _():
            kp(i).wait_send()

        @pl.when(d != 0)
        def _():
            kv_core(i, key_part(i)).wait_send()
            kv_core(4 + i, value_part(i)).wait_send()

        return carry

    lax.fori_loop(0, 4, drain_four, 0)
    for copy in sends:
        copy.wait_send()
    fwd_a.wait_send()
    fwd_b.wait_send()

    @pl.when(d != 0)
    def _():
        w1.wait_send()


def front(table, tokens, norm_gain, w_query, w_key, w_value, q_gain, k_gain, cosine, sine):
    vmem = pl.BlockSpec(memory_space=pltpu.VMEM)
    hbm = pl.BlockSpec(memory_space=pl.ANY)
    dma = pltpu.SemaphoreType.DMA
    pair = lambda *n: [dma(n), dma(n)]
    rows, width = tokens.shape
    columns = w_query.shape[1]
    flops = 2 * 4 * rows * width * (columns + 256)
    return pl.pallas_call(
        front_kernel,
        out_shape=(
            jax.ShapeDtypeStruct((8, 4, rows, 128), BF16),
            jax.ShapeDtypeStruct((2, 7, 32, 16, 128), BF16),
        ),
        in_specs=[pl.BlockSpec(memory_space=pltpu.SMEM)] + [vmem] * 9,
        out_specs=(hbm, hbm),
        scratch_shapes=[
            pltpu.VMEM((4 * rows, width), BF16),
            pltpu.VMEM((width, columns), BF16),
            pltpu.VMEM((width, 256), BF16),
            pltpu.VMEM((8, 4, rows, 128), BF16),
            pltpu.VMEM((8, 4, rows, 128), BF16),
            pltpu.VMEM((8, 4, 2, 16, 128), BF16),
            pltpu.VMEM((64, 2, 16, 128), BF16),
            pltpu.VMEM((32, 2, 7, 16, 128), BF16),
            dma((7,)),
        ] + pair(6) + [dma((1,)), dma((4,))] + pair(4) + pair(4) + pair(8) + pair(8)
        + pair(4) + pair(4) + pair(32) + pair(4) + pair(4) + pair(8)
        + pair(4, 4) + pair(4, 4) + pair(16) + pair(32),
        cost_estimate=pl.CostEstimate(flops=flops, bytes_accessed=10 << 20, transcendentals=0),
        compiler_params=pltpu.CompilerParams(
            collective_id=0, has_side_effects=True, vmem_limit_bytes=50 << 20
        ),
    )(table, tokens, norm_gain, w_query, w_key, w_value, q_gain, k_gain, cosine, sine)


def attend_kernel(q_doc, k_doc, q_ref, kv_ref, o_ref, keys, values, q_mask):
    heads, length, size = q_ref.shape
    span = 6 * length
    step = 256
    scale = size ** (-0.5) * math.log2(math.e)
    lane = lax.broadcasted_iota(jnp.int32, (length, 128), 1)
    q_mask[...] = jnp.where(q_doc[...] == lane, 0.0, -1e30).astype(BF16)
    for i in range(7):
        rows = pl.ds(i * length, length)
        keys[rows, :128] = kv_ref[0, i]
        keys[rows, 128:] = jnp.where(k_doc[rows, :] == lane, 1.0, 0.0).astype(BF16)
        values[rows, :128] = kv_ref[1, i]
        values[rows, 128:] = jnp.ones((length, 128), BF16)

    def score(h, r):
        rows = pl.ds(r * step, step)
        q = jnp.concatenate([q_ref[h, rows, :], q_mask[rows, :]], -1)
        parts = [(r * step + at, length) for at in range(0, span, length)]
        parts.append((r * step + span, step))
        tiles = []
        top = None
        for at, width in parts:
            s = lax.dot_general(
                q, keys[pl.ds(at, width), :], (((1,), (1,)), ((), ())), preferred_element_type=F32
            )
            if width == step:
                here = lax.broadcasted_iota(jnp.int32, s.shape, 0)
                s = jnp.where(lax.broadcasted_iota(jnp.int32, s.shape, 1) <= here, s, -1e30)
            tiles.append(s)
            for c in range(0, width, 128):
                best = s[:, c : c + 128]
                top = best if top is None else jnp.maximum(top, best)
        return parts, tiles, jnp.max(top, -1, keepdims=True)

    def finish(h, r, parts, tiles, top):
        summed = None
        for (at, width), s in zip(parts, tiles):
            e = jnp.exp2((s - top) * scale).astype(BF16)
            part = jnp.dot(e, values[pl.ds(at, width), :], preferred_element_type=F32)
            summed = part if summed is None else summed + part
        out = summed[:, :128] / summed[:, 128:]
        o_ref[pl.ds(r * step, step), h * 128 : h * 128 + 128] = out.astype(BF16)

    ahead = None
    for h in range(heads):
        for r in range(length // step):
            now = (h, r) + score(h, r)
            if ahead is not None:
                finish(*ahead)
            ahead = now
    finish(*ahead)


def attend(q_doc, k_doc, q, kv):
    heads, length, size = q.shape
    return pl.pallas_call(
        attend_kernel,
        out_shape=jax.ShapeDtypeStruct((length, heads * size), BF16),
        in_specs=[pl.BlockSpec(memory_space=pltpu.VMEM)] * 4,
        out_specs=pl.BlockSpec(memory_space=pltpu.VMEM),
        scratch_shapes=[
            pltpu.VMEM((7 * length, 256), BF16),
            pltpu.VMEM((7 * length, 256), BF16),
            pltpu.VMEM((length, 128), BF16),
        ],
        compiler_params=pltpu.CompilerParams(vmem_limit_bytes=50 << 20),
    )(q_doc, k_doc, q, kv)


def shards(tokens, norm_gain, w_query, w_key, w_value, query_gain, key_gain, segments, block_of):
    x, y, zh, k, zl = place()
    rest = y * 4 + zh * 2 + k
    quarter = tokens.shape[0]
    length = quarter * 4

    ids = jnp.arange(48, dtype=jnp.int32)
    starts = jnp.sum((segments[None, :] < ids[:, None]).astype(jnp.int32), 1)

    def start_of(at, size):
        doc = lax.dynamic_slice_in_dim(segments, at, size, 0)
        return jnp.sum(jnp.where(doc[:, None] == ids[None, :], starts[None, :], 0), 1)

    offsets = []
    for other in range(4):
        at = block_of[other * 16 + rest] * length + zl * quarter
        offsets.append(at + jnp.arange(quarter, dtype=jnp.int32) - start_of(at, quarter))
    offsets = jnp.concatenate(offsets)

    angles = offsets.astype(F32)[:, None] * jnp.asarray(yarn_frequencies(128), F32)[None, :]
    scale = 0.1 * math.log(4.0) + 1.0
    cosine, sine = jnp.cos(angles) * scale, jnp.sin(angles) * scale
    cosine = jnp.concatenate([cosine, cosine], -1)
    sine = jnp.concatenate([-sine, sine], -1)

    blocks = jnp.arange(64, dtype=jnp.int32)
    holder = jnp.sum(jnp.where(block_of[None, :] == blocks[:, None], blocks[None, :], 0), 1)
    d = jnp.arange(32, dtype=jnp.int32)
    wanted = block_of[ctx_of(d // 8, (d // 2) % 4, zh, d % 2)][:, None] - 6 + jnp.arange(7)[None, :]
    source = holder[jnp.maximum(wanted, 0)]
    table = (source % 16) * 4 + source // 16

    q_mine, kv = front(
        table, tokens, norm_gain[None, :], w_query, w_key, w_value,
        query_gain[None, :], key_gain[None, :], cosine, sine,
    )
    first = block_of[x * 16 + rest] * length
    padded = jnp.concatenate([jnp.full((6 * length,), 63, jnp.int32), segments])
    k_doc = lax.dynamic_slice_in_dim(padded, first, 7 * length, 0)[:, None]
    return attend(k_doc[6 * length :], k_doc, q_mine.reshape(8, length, 128), kv.reshape(2, 7, length, 128))


def solution(mesh):
    return jax.shard_map(
        shards,
        mesh=mesh,
        in_specs=(
            P(("context", "tensor"), None),
            P(),
            P("context", "tensor"),
            P(None, "tensor"),
            P(None, "tensor"),
            P(),
            P(),
            P(),
            P(),
        ),
        out_specs=P("context", "tensor"),
        check_vma=False,
    )
```

```python
import math

import jax
import jax.numpy as jnp
from jax import lax
from jax.experimental import pallas as pl
from jax.experimental.pallas import tpu as pltpu
from jax.sharding import PartitionSpec as P

MESH = pl.DeviceIdType.MESH
BF16 = jnp.bfloat16
F32 = jnp.float32
ROPE_SCALE = 0.1 * math.log(4.0) + 1.0
STEPS = (
    (1, 0), (0, 1), (3, 0), (0, 3), (1, 1), (3, 3), (1, 3), (3, 1),
    (2, 0), (0, 2), (2, 1), (1, 2), (2, 3), (3, 2), (2, 2),
)
PLACES = ((0, 0, 1),) + tuple((dx, dy, dk) for dk in (0, 1) for dx, dy in STEPS)


def yarn_frequencies(dim):
    theta = 1000000.0
    factor = 4.0
    initial = 32768.0
    lowest = math.floor(dim * math.log(initial / (32.0 * 2 * math.pi)) / (2 * math.log(theta)))
    highest = math.ceil(dim * math.log(initial / (1.0 * 2 * math.pi)) / (2 * math.log(theta)))
    lowest = max(lowest, 0)
    highest = min(highest, dim - 1)
    spread = max(highest - lowest, 0.001)
    result = []
    for index in range(dim // 2):
        base_freq = theta ** (-2.0 * index / dim)
        ramp = min(max((index - lowest) / spread, 0.0), 1.0)
        result.append(base_freq / factor * ramp + base_freq * (1.0 - ramp))
    return result


def ctx_of(x, y, zh, k):
    return x * 16 + y * 4 + zh * 2 + k


def place():
    c = lax.axis_index("context")
    return c // 16, (c // 4) % 4, (c // 2) % 2, c % 2, lax.axis_index("tensor")


def attend(q_ref, kv_ref, k_mask, q_mask, o_ref):
    heads = q_ref.shape[0]
    length = q_mask.shape[0]
    span = 6 * length
    step = 256
    scale = 128 ** (-0.5) * math.log2(math.e)
    ones = jnp.ones((step, 128), BF16)

    def score(h, r):
        quarters = step // 128
        q = q_ref[h, pl.ds(r * quarters, quarters)].reshape(step, 128)
        q = jnp.concatenate([q, q_mask[pl.ds(r * step, step), :]], -1)
        tiles = []
        top = None
        for at in range(r * step, span + r * step + step, step):
            rows = (at // length, pl.ds(at % length, step))
            keys = jnp.concatenate([kv_ref[(0,) + rows], k_mask[rows]], -1)
            s = lax.dot_general(q, keys, (((1,), (1,)), ((), ())), preferred_element_type=F32)
            if at == span + r * step:
                here = lax.broadcasted_iota(jnp.int32, s.shape, 0)
                s = jnp.where(lax.broadcasted_iota(jnp.int32, s.shape, 1) <= here, s, -1e30)
            tiles.append((rows, s))
            for c in range(0, step, 128):
                best = s[:, c : c + 128]
                top = best if top is None else jnp.maximum(top, best)
        return tiles, jnp.max(top, -1, keepdims=True)

    def finish(h, r, tiles, top):
        summed = None
        for rows, s in tiles:
            e = jnp.exp2((s - top) * scale).astype(BF16)
            values = jnp.concatenate([kv_ref[(1,) + rows], ones], -1)
            part = jnp.dot(e, values, preferred_element_type=F32)
            summed = part if summed is None else summed + part
        out = summed[:, :128] / summed[:, 128:]
        columns = pl.ds(pl.multiple_of(h * 128, 128), 128)
        o_ref[pl.ds(r * step, step), columns] = out.astype(BF16)

    def some(g, carry):
        ahead = None
        for n in range(4):
            for r in range(length // step):
                h = g * 4 + n
                now = (h, r) + score(h, r)
                if ahead is not None:
                    finish(*ahead)
                ahead = now
        finish(*ahead)
        return carry

    lax.fori_loop(0, heads // 4, some, 0)


def front_kernel(
    block_of, slot_of, segs, freqs, tok, norm_gain, wq, wk, wv, q_gain, k_gain,
    o_ref,
    tok_all, wq_all, wkv_all, q_send, qx, kv_send, got, picked,
    q_out, kv_all, cosine, sine, k_mask, q_mask,
    loc, tok_s, tok_r, w1_s, w1_r, zp_s, zp_r, zm_s, zm_r,
    yr_s, yr_r, yl_s, yl_r, fr_s, fr_r, fl_s, fl_r, co_s, co_r,
    kp_s, kp_r, km_s, km_r, kc_s, kc_r,
    qx_s, qx_r, qz_s, qz_r, p1_s, p1_r, p2_s, p2_r,
):
    x, y, zh, k, zl = place()
    me = ctx_of(x, y, zh, k)
    z = zh * 4 + zl
    d = (zl - x + 4) % 4
    zh_u = ((z - d + 8) % 8) // 4
    zh_d = 1 - zh_u

    def at_z(pos):
        pos = pos % 8
        return (ctx_of(x, y, pos // 4, k), pos % 4)

    up, down = at_z(z + 1), at_z(z + 7)
    x_dev = [(ctx_of((x + o) % 4, y, zh, k), zl) for o in range(4)]
    y_right, y_left = (ctx_of(x, (y + 1) % 4, zh, k), zl), (ctx_of(x, (y + 3) % 4, zh, k), zl)
    other = (ctx_of(x, y, zh, 1 - k), zl)

    rest = y * 4 + zh * 2 + k
    mine = x * 8 + y * 2 + k

    def half_plane(n):
        return (ctx_of(n // 8, (n // 2) % 4, zh, n % 2), zl)

    barrier = pltpu.get_barrier_semaphore()

    def greet(dev):
        pl.semaphore_signal(barrier, inc=1, device_id=dev, device_id_type=MESH)

    for dev in (x_dev[1], x_dev[2], x_dev[3], up, down, y_right, y_left, other):
        greet(dev)
    for o in range(1, 4):
        greet((me, (zl + o) % 4))

    def greet_piece(r, carry):
        @pl.when((x != zl) | (r != rest))
        def _():
            greet((zl * 16 + r, x))

        return carry

    lax.fori_loop(0, 16, greet_piece, 0)

    def greet_plane(o, carry):
        greet(half_plane((mine + o) % 32))
        return carry

    lax.fori_loop(1, 32, greet_plane, 0)

    quarter = tok.shape[0]
    width = tok.shape[1]

    def norm_rows(n, carry):
        rows = pl.ds(pl.multiple_of(n * 16, 16), 16)
        wide = tok[rows, :].astype(F32)
        mean = jnp.mean(wide * wide, -1, keepdims=True)
        wide = wide * lax.rsqrt(mean + 1e-06) * norm_gain[...]
        tok_all[pl.ds(pl.multiple_of(x * quarter + n * 16, 16), 16), :] = wide.astype(BF16)
        return carry

    lax.fori_loop(0, quarter // 16, norm_rows, 0)
    pl.semaphore_wait(barrier, 8 + 3 + 15 + 31 + ((x - zl + 4) % 4 + 3) // 4)

    def remote(src, dst, ss, rs, dev):
        return pltpu.make_async_remote_copy(
            src_ref=src, dst_ref=dst, send_sem=ss, recv_sem=rs, device_id=dev, device_id_type=MESH
        )

    half = quarter // 2

    def tok_copy(n, slot, part, dev):
        ref = tok_all.at[pl.ds(pl.multiple_of(slot * quarter + part * half, 16), half)]
        return remote(ref, ref, tok_s.at[n], tok_r.at[n], dev)

    def w_slot(c):
        return wq_all.at[pl.ds(pl.multiple_of(c * w_rows, 16), w_rows)]

    w_rows = wq.shape[0]
    sends = [
        tok_copy(0, x, 0, x_dev[1]),
        tok_copy(3, x, 1, x_dev[3]),
        tok_copy(1, x, 1, x_dev[1]),
        tok_copy(2, x, 0, x_dev[3]),
    ]
    w1_index = (x - zl + 4) % 4
    w1 = remote(wq, w_slot(me), w1_s.at[0], w1_r.at[w1_index], (ctx_of(zl, y, zh, k), zl))
    own_w = pltpu.make_async_copy(wq, w_slot(me), loc.at[1])

    @pl.when(d != 0)
    def _():
        w1.start()

    @pl.when(d == 0)
    def _():
        own_w.start()

    for copy in sends:
        copy.start()

    @pl.when(d == 0)
    def _():
        wkv_all[:, :128] = wk[...]
        wkv_all[:, 128:] = wv[...]

    def slot(i, zhalf, yy):
        return w_slot(ctx_of((x + i) % 4, yy, zhalf, k))

    def zp(i):
        ref = slot(i, zh_u, y)
        return remote(ref, ref, zp_s.at[i], zp_r.at[i], up)

    def zm(i, zhalf):
        ref = slot(i, zhalf, y)
        return remote(ref, ref, zm_s.at[i], zm_r.at[i], down)

    def core(n, ref):
        return remote(ref, ref, co_s.at[n], co_r.at[n], other)

    def y_own(s, ref):
        return (
            remote(ref, ref, yr_s.at[s], yr_r.at[s], y_right),
            remote(ref, ref, yl_s.at[s], yl_r.at[s], y_left),
        )

    def fwd_right(i2, ref):
        return remote(ref, ref, fr_s.at[i2], fr_r.at[i2], y_right)

    def fwd_left(i2, ref):
        return remote(ref, ref, fl_s.at[i2], fl_r.at[i2], y_left)

    def spread(s, ref):
        right, left = y_own(s, ref)
        right.start()
        left.start()
        core(s, ref).start()

    def when_four(i, act):
        @pl.when((i >= 0) & (i < 4))
        def _():
            act(i)

    def z_upper(i):
        ref = slot(i, zh_u, y)

        @pl.when(d == 0)
        def _():
            @pl.when(i == 0)
            def _():
                own_w.wait()

            @pl.when(i != 0)
            def _():
                remote(ref, ref, w1_s.at[0], w1_r.at[i], other).wait_recv()

            zm(i, zh_u).start()

        @pl.when(d != 0)
        def _():
            zp(i).wait_recv()

        zp(i).start()
        spread(i, ref)

    def z_lower(i):
        ref = slot(i, zh_d, y)

        @pl.when(d == 0)
        def _():
            remote(ref, ref, zp_s.at[i], zp_r.at[i], up).wait_recv()

        @pl.when(d != 0)
        def _():
            zm(i, zh_d).wait_recv()

        @pl.when(d >= 2)
        def _():
            zm(i, zh_d).start()

        spread(4 + i, ref)

    rows = wk.shape[0] // 8

    def part(i):
        return pl.ds(pl.multiple_of((k * 4 + i) * rows, 16), rows)

    def key_part(i):
        return wkv_all.at[part(i), pl.ds(0, 128)]

    def value_part(i):
        return wkv_all.at[part(i), pl.ds(128, 128)]

    def kv_core(n, ref):
        return remote(ref, ref, kc_s.at[n], kc_r.at[n], other)

    def kp(i):
        return remote(key_part(i), key_part(i), kp_s.at[i], kp_r.at[i], up)

    def km(i):
        return remote(value_part(i), value_part(i), km_s.at[i], km_r.at[i], down)

    y_l, y_r, y_far = (y + 3) % 4, (y + 1) % 4, (y + 2) % 4

    def ring(i, s, zhalf):
        ref = slot(i, zhalf, y_l)
        y_own(s, ref)[0].wait_recv()

        @pl.when(i % 2 == 0)
        def _():
            fwd_right(s // 2, ref).start()

        core(8 + s, ref).start()
        ref2 = slot(i, zhalf, y_r)
        y_own(s, ref2)[1].wait_recv()

        @pl.when(i % 2 == 1)
        def _():
            fwd_left(s // 2, ref2).start()

        core(16 + s, ref2).start()

    def kv_upper(i):
        @pl.when(d != 0)
        def _():
            kp(i).wait_recv()
            kv_core(i, key_part(i)).start()

            @pl.when(d != 3)
            def _():
                kp(i).start()

    def kv_lower(i):
        @pl.when(d != 0)
        def _():
            km(i).wait_recv()
            kv_core(4 + i, value_part(i)).start()

            @pl.when(d != 1)
            def _():
                km(i).start()

    def ring_upper(i):
        ring(i, i, zh_u)

    def ring_lower(i):
        ring(i, 4 + i, zh_d)

    lane = lax.broadcasted_iota(jnp.int32, (128, 128), 1)

    def doc_row(at, absent):
        return jnp.where(at >= 0, segs[jnp.maximum(at, 0)], absent).astype(F32)

    def down_rows(row):
        return jnp.broadcast_to(row, (128, 128)).T

    def rope_table(n):
        row = block_of[n * 16 + rest] * 4 + zl
        docs = down_rows(segs[row].astype(F32))

        def count(j, total):
            return total + jnp.where(doc_row(row - 24 + j, -1) < docs, 1.0, 0.0)

        before = lax.fori_loop(0, 25, count, jnp.zeros((128, 128), F32))
        here = lax.broadcasted_iota(jnp.int32, (128, 1), 0).astype(F32)
        offset = 3072.0 + here - jnp.sum(before, -1, keepdims=True)
        angle = offset * freqs[...]
        rows = pl.ds(pl.multiple_of(n * 128, 128), 128)
        cosine[rows, :] = jnp.cos(angle) * ROPE_SCALE
        turned = jnp.sin(angle) * ROPE_SCALE
        sine[rows, :] = jnp.where(lane < 64, -turned, turned)

    def mask_rows(n):
        for j in range(4):
            docs = down_rows(doc_row(block_of[me] * 4 - 24 + n * 4 + j, 63))
            same = docs == lane.astype(F32)
            k_mask[n, pl.ds(j * 128, 128), :] = jnp.where(same, 1.0, 0.0).astype(BF16)

            @pl.when(n == 6)
            def _():
                q_mask[pl.ds(j * 128, 128), :] = jnp.where(same, 0.0, -1e30).astype(BF16)

    def step(t, carry):
        when_four(t - d, z_upper)
        when_four(t - 4 + d, z_lower)

        @pl.when((d == 0) & (t == 3))
        def _():
            for i in range(4):
                kp(i).start()
                km(i).start()

        when_four(t - 4 - d, kv_upper)
        when_four(t - 8 + d, kv_lower)
        when_four(t - 4 - d, ring_upper)
        when_four(t - 8 + d, ring_lower)
        when_four(t, rope_table)

        @pl.when((t >= 4) & (t < 11))
        def _():
            mask_rows(t - 4)

        return carry

    lax.fori_loop(0, 7, step, 0)

    left_x, right_x, far_x = (x + 3) % 4, (x + 1) % 4, (x + 2) % 4
    tok_copy(0, left_x, 0, x_dev[1]).wait_recv()
    fwd_a = tok_copy(4, left_x, 0, x_dev[1])
    fwd_a.start()
    tok_copy(3, right_x, 1, x_dev[3]).wait_recv()
    fwd_b = tok_copy(5, right_x, 1, x_dev[3])
    fwd_b.start()

    lax.fori_loop(7, 12, step, 0)

    tok_copy(1, left_x, 1, x_dev[1]).wait_recv()
    tok_copy(2, right_x, 0, x_dev[3]).wait_recv()
    tok_copy(4, far_x, 0, x_dev[1]).wait_recv()
    tok_copy(5, far_x, 1, x_dev[3]).wait_recv()

    @pl.when(d != 0)
    def _():
        def core_part(i, carry):
            kv_core(i, key_part(i)).wait_recv()
            kv_core(4 + i, value_part(i)).wait_recv()
            return carry

        lax.fori_loop(0, 4, core_part, 0)

    def turn(t, gain):
        t = t * lax.rsqrt(jnp.mean(t * t, -1, keepdims=True) + 1e-06) * gain[...]
        return (t * cosine[...] + pltpu.roll(t, 64, 1) * sine[...]).astype(BF16)

    both = jnp.dot(tok_all[...], wkv_all[...], preferred_element_type=F32)
    key = turn(both[:, :128], k_gain)
    value = both[:, 128:].astype(BF16)
    for p in range(8):
        for n in range(4):
            at = n * 128 + p * 16
            kv_send[p, n, 0] = key[at : at + 16]
            kv_send[p, n, 1] = value[at : at + 16]

    def piece(r):
        p = (r // 4) * 2 + r % 2
        return remote(
            kv_send.at[p], got.at[pl.ds(rest * 4, 4)], p1_s.at[r], p1_r.at[rest], (zl * 16 + r, x)
        )

    own_piece = pltpu.make_async_copy(
        kv_send.at[(rest // 4) * 2 + rest % 2], got.at[pl.ds(rest * 4, 4)], loc.at[0]
    )

    def send_piece(o, carry):
        r = (rest + o) % 16

        @pl.when((x != zl) | (r != rest))
        def _():
            piece(r).start()

        return carry

    lax.fori_loop(0, 16, send_piece, 0)

    @pl.when(x == zl)
    def _():
        own_piece.start()

    def far_upper(i):
        finish(i, i, zh_u)

    def far_lower(i):
        finish(i, 4 + i, zh_d)

    def finish(i, s, zhalf):
        ref = slot(i, zhalf, y_far)

        @pl.when(i % 2 == 0)
        def _():
            fwd_right(s // 2, ref).wait_recv()

        @pl.when(i % 2 == 1)
        def _():
            fwd_left(s // 2, ref).wait_recv()

        core(24 + s, ref).start()

    def far_step(t, carry):
        when_four(t - d, far_upper)
        when_four(t - 4 + d, far_lower)
        return carry

    lax.fori_loop(0, 8, far_step, 0)

    any_w = w_slot(me)

    def wait_core(n, carry):
        core(n, any_w).wait_recv()
        return carry

    lax.fori_loop(0, 32, wait_core, 0)

    def heads(n):
        return pl.ds(n * 2, 2)

    def x_step(n, o):
        to = (x + o) % 4
        return remote(
            q_send.at[heads(n), to], qx.at[heads(n), x], qx_s.at[n, o], qx_r.at[n, o],
            (ctx_of(to, y, zh, k), zl),
        )

    def z_step(n, src, to):
        o = (to - zl + 4) % 4
        return remote(
            src.at[heads(n), to], q_out.at[heads(n), zl], qz_s.at[n, o], qz_r.at[n, o], (me, to)
        )

    def z_move(n, src, frm):
        @pl.when(frm != zl)
        def _():
            z_step(n, src, frm).start()

        @pl.when(frm == zl)
        def _():
            pltpu.make_async_copy(
                src.at[heads(n), frm], q_out.at[heads(n), zl], loc.at[3 + n]
            ).start()

    def project(n, carry):
        columns = pl.ds(pl.multiple_of(n * 256, 256), 256)
        both = jnp.dot(tok_all[...], wq_all[:, columns], preferred_element_type=F32)
        for h in range(2):
            head = turn(both[:, h * 128 : h * 128 + 128], q_gain)
            q_send[n * 2 + h] = head.reshape(4, quarter, 128)
        for o in (1, 3, 2):
            x_step(n, o).start()
        z_move(n, q_send, x)
        return carry

    lax.fori_loop(0, 4, project, 0)

    def wait_piece(r, carry):
        @pl.when((x != zl) | (r != rest))
        def _():
            remote(
                kv_send.at[0], got.at[pl.ds(r * 4, 4)], p1_s.at[0], p1_r.at[r], (zl * 16 + r, x)
            ).wait_recv()

        return carry

    lax.fori_loop(0, 16, wait_piece, 0)

    @pl.when(x == zl)
    def _():
        own_piece.wait()

    own_keys = pl.ds(pl.multiple_of(mine * 16, 16), 16)

    def plane(n):
        return remote(
            picked.at[n], kv_all.at[:, :, own_keys], p2_s.at[n], p2_r.at[mine], half_plane(n)
        )

    def pick(n):
        block = block_of[half_plane(n)[0]]
        for i in range(7):
            picked[n, :, i] = got[slot_of[jnp.maximum(block - 6 + i, 0)]]

    for dx, dy, dk in PLACES:
        n = ((x + dx) % 4) * 8 + ((y + dy) % 4) * 2 + (k + dk) % 2
        pick(n)
        plane(n).start()
    pick(mine)
    own_plane = pltpu.make_async_copy(picked.at[mine], kv_all.at[:, :, own_keys], loc.at[2])
    own_plane.start()

    def pass_on(n, carry):
        for o in (1, 3, 2):
            frm = (x - o + 4) % 4
            remote(
                q_send.at[heads(n), 0], qx.at[heads(n), frm], qx_s.at[n, o], qx_r.at[n, o],
                (ctx_of(frm, y, zh, k), zl),
            ).wait_recv()
            z_move(n, qx, frm)
        return carry

    lax.fori_loop(0, 4, pass_on, 0)

    def q_here(n, carry):
        pltpu.make_async_copy(
            q_send.at[heads(n), 0], q_out.at[heads(n), zl], loc.at[3 + n]
        ).wait()
        for o in (1, 2, 3):
            frm = (zl - o + 4) % 4
            remote(
                q_send.at[heads(n), 0], q_out.at[heads(n), frm], qz_s.at[n, o], qz_r.at[n, o],
                (me, frm),
            ).wait_recv()
        return carry

    lax.fori_loop(0, 4, q_here, 0)
    own_plane.wait()

    def plane_here(o, carry):
        n = (mine + o) % 32
        theirs = pl.ds(pl.multiple_of(n * 16, 16), 16)
        remote(
            picked.at[n], kv_all.at[:, :, theirs], p2_s.at[n], p2_r.at[n], half_plane(n)
        ).wait_recv()
        return carry

    lax.fori_loop(1, 32, plane_here, 0)
    attend(q_out, kv_all, k_mask, q_mask, o_ref)

    def drain_q(n, carry):
        for o in (1, 2, 3):
            x_step(n, o).wait_send()
            z_step(n, q_send, (zl + o) % 4).wait_send()
        return carry

    lax.fori_loop(0, 4, drain_q, 0)

    def drain_piece(r, carry):
        @pl.when((x != zl) | (r != rest))
        def _():
            piece(r).wait_send()

        return carry

    lax.fori_loop(0, 16, drain_piece, 0)

    def drain_plane(o, carry):
        plane((mine + o) % 32).wait_send()
        return carry

    lax.fori_loop(1, 32, drain_plane, 0)

    def drain_core(n, carry):
        core(n, any_w).wait_send()
        return carry

    lax.fori_loop(0, 32, drain_core, 0)

    def drain_y(s, carry):
        right, left = y_own(s, any_w)
        right.wait_send()
        left.wait_send()
        return carry

    lax.fori_loop(0, 8, drain_y, 0)

    def drain_four(i, carry):
        zp(i).wait_send()
        fwd_right(i, any_w).wait_send()
        fwd_left(i, any_w).wait_send()

        @pl.when((d == 0) | (d >= 2))
        def _():
            zm(i, zh_u).wait_send()
            km(i).wait_send()

        @pl.when(d <= 2)
        def _():
            kp(i).wait_send()

        @pl.when(d != 0)
        def _():
            kv_core(i, key_part(i)).wait_send()
            kv_core(4 + i, value_part(i)).wait_send()

        return carry

    lax.fori_loop(0, 4, drain_four, 0)
    for copy in sends:
        copy.wait_send()
    fwd_a.wait_send()
    fwd_b.wait_send()

    @pl.when(d != 0)
    def _():
        w1.wait_send()


def front(block_of, slot_of, segs, freqs, tokens, norm_gain, w_query, w_key, w_value, q_gain, k_gain):
    vmem = pl.BlockSpec(memory_space=pltpu.VMEM)
    dma = pltpu.SemaphoreType.DMA
    pair = lambda *n: [dma(n), dma(n)]
    rows, width = tokens.shape
    columns = w_query.shape[1]
    flops = 2 * 4 * rows * width * (columns + 256)
    return pl.pallas_call(
        front_kernel,
        out_shape=jax.ShapeDtypeStruct((4 * rows, columns), BF16),
        in_specs=[pl.BlockSpec(memory_space=pltpu.SMEM)] * 2 + [vmem] * 9,
        out_specs=vmem,
        scratch_shapes=[
            pltpu.VMEM((4 * rows, width), BF16),
            pltpu.VMEM((width, columns), BF16),
            pltpu.VMEM((width, 256), BF16),
            pltpu.VMEM((8, 4, rows, 128), BF16),
            pltpu.VMEM((8, 4, rows, 128), BF16),
            pltpu.VMEM((8, 4, 2, 16, 128), BF16),
            pltpu.VMEM((64, 2, 16, 128), BF16),
            pltpu.VMEM((32, 2, 7, 16, 128), BF16),
            pltpu.VMEM((8, 4, rows, 128), BF16),
            pltpu.VMEM((2, 7, 4 * rows, 128), BF16),
            pltpu.VMEM((4 * rows, 128), F32),
            pltpu.VMEM((4 * rows, 128), F32),
            pltpu.VMEM((7, 4 * rows, 128), BF16),
            pltpu.VMEM((4 * rows, 128), BF16),
            dma((7,)),
        ] + pair(6) + [dma((1,)), dma((4,))] + pair(4) + pair(4) + pair(8) + pair(8)
        + pair(4) + pair(4) + pair(32) + pair(4) + pair(4) + pair(8)
        + pair(4, 4) + pair(4, 4) + pair(16) + pair(32),
        cost_estimate=pl.CostEstimate(flops=flops, bytes_accessed=10 << 20, transcendentals=0),
        compiler_params=pltpu.CompilerParams(
            collective_id=0, has_side_effects=True, vmem_limit_bytes=56 << 20
        ),
    )(block_of, slot_of, segs, freqs, tokens, norm_gain, w_query, w_key, w_value, q_gain, k_gain)


def shards(tokens, norm_gain, w_query, w_key, w_value, query_gain, key_gain, segments, block_of):
    blocks = jnp.arange(64, dtype=jnp.int32)
    slot = (blocks % 16) * 4 + blocks // 16
    slot_of = jnp.sum(jnp.where(block_of[None, :] == blocks[:, None], slot[None, :], 0), 1)
    freqs = jnp.asarray(yarn_frequencies(128) * 2, F32)
    return front(
        block_of, slot_of, segments.reshape(-1, 1, 128), freqs[None, :], tokens,
        norm_gain[None, :], w_query, w_key, w_value, query_gain[None, :], key_gain[None, :],
    )


def solution(mesh):
    return jax.shard_map(
        shards,
        mesh=mesh,
        in_specs=(
            P(("context", "tensor"), None),
            P(),
            P("context", "tensor"),
            P(None, "tensor"),
            P(None, "tensor"),
            P(),
            P(),
            P(),
            P(),
        ),
        out_specs=P("context", "tensor"),
        check_vma=False,
    )
```

```python
import math

import jax
import jax.numpy as jnp
from jax import lax
from jax.experimental import pallas as pl
from jax.experimental.pallas import tpu as pltpu
from jax.sharding import PartitionSpec as P

MESH = pl.DeviceIdType.MESH
BF16 = jnp.bfloat16
F32 = jnp.float32
ROPE_SCALE = 0.1 * math.log(4.0) + 1.0
STEPS = (
    (1, 0), (0, 1), (3, 0), (0, 3), (1, 1), (3, 3), (1, 3), (3, 1),
    (2, 0), (0, 2), (2, 1), (1, 2), (2, 3), (3, 2), (2, 2),
)
PLACES = ((0, 0, 1),) + tuple((dx, dy, dk) for dk in (0, 1) for dx, dy in STEPS)


def yarn_frequencies(dim):
    theta = 1000000.0
    factor = 4.0
    initial = 32768.0
    lowest = math.floor(dim * math.log(initial / (32.0 * 2 * math.pi)) / (2 * math.log(theta)))
    highest = math.ceil(dim * math.log(initial / (1.0 * 2 * math.pi)) / (2 * math.log(theta)))
    lowest = max(lowest, 0)
    highest = min(highest, dim - 1)
    spread = max(highest - lowest, 0.001)
    result = []
    for index in range(dim // 2):
        base_freq = theta ** (-2.0 * index / dim)
        ramp = min(max((index - lowest) / spread, 0.0), 1.0)
        result.append(base_freq / factor * ramp + base_freq * (1.0 - ramp))
    return result


def ctx_of(x, y, zh, k):
    return x * 16 + y * 4 + zh * 2 + k


def place():
    c = lax.axis_index("context")
    return c // 16, (c // 4) % 4, (c // 2) % 2, c % 2, lax.axis_index("tensor")


def attend(q_ref, kv_ref, k_mask, q_mask, o_ref):
    heads = q_ref.shape[0]
    length = q_mask.shape[0]
    span = 6 * length
    step = 256
    scale = 128 ** (-0.5) * math.log2(math.e)
    ones = jnp.ones((step, 128), BF16)

    def score(h, r):
        quarters = step // 128
        q = q_ref[h, pl.ds(r * quarters, quarters)].reshape(step, 128)
        q = jnp.concatenate([q, q_mask[pl.ds(r * step, step), :]], -1)
        tiles = []
        top = None
        for at in range(r * step, span + r * step + step, step):
            rows = (at // length, pl.ds(at % length, step))
            keys = jnp.concatenate([kv_ref[(0,) + rows], k_mask[rows]], -1)
            s = lax.dot_general(q, keys, (((1,), (1,)), ((), ())), preferred_element_type=F32)
            if at == span + r * step:
                here = lax.broadcasted_iota(jnp.int32, s.shape, 0)
                s = jnp.where(lax.broadcasted_iota(jnp.int32, s.shape, 1) <= here, s, -1e30)
            tiles.append((rows, s))
            for c in range(0, step, 128):
                best = s[:, c : c + 128]
                top = best if top is None else jnp.maximum(top, best)
        return tiles, jnp.max(top, -1, keepdims=True)

    def finish(h, r, tiles, top):
        summed = None
        for rows, s in tiles:
            e = jnp.exp2((s - top) * scale).astype(BF16)
            values = jnp.concatenate([kv_ref[(1,) + rows], ones], -1)
            part = jnp.dot(e, values, preferred_element_type=F32)
            summed = part if summed is None else summed + part
        out = summed[:, :128] / summed[:, 128:]
        columns = pl.ds(pl.multiple_of(h * 128, 128), 128)
        o_ref[pl.ds(r * step, step), columns] = out.astype(BF16)

    def some(g, carry):
        ahead = None
        for n in range(4):
            for r in range(length // step):
                h = g * 4 + n
                now = (h, r) + score(h, r)
                if ahead is not None:
                    finish(*ahead)
                ahead = now
        finish(*ahead)
        return carry

    lax.fori_loop(0, heads // 4, some, 0)


def front_kernel(
    block_of, slot_of, segs, freqs, tok, norm_gain, wq, wk, wv, q_gain, k_gain,
    o_ref,
    tok_all, wq_all, wkv_all, q_send, qx, kv_send, got_k, got_v, picked,
    q_out, kv_all, cosine, sine, k_mask, q_mask,
    loc, tok_s, tok_r, w1_s, w1_r, zp_s, zp_r, zm_s, zm_r,
    yr_s, yr_r, yl_s, yl_r, fr_s, fr_r, fl_s, fl_r, co_s, co_r,
    kp_s, kp_r, km_s, km_r, kc_s, kc_r,
    qx_s, qx_r, qz_s, qz_r, p1_s, p1_r, p2_s, p2_r, own_s,
):
    x, y, zh, k, zl = place()
    me = ctx_of(x, y, zh, k)
    z = zh * 4 + zl
    d = (zl - x + 4) % 4
    zh_u = ((z - d + 8) % 8) // 4
    zh_d = 1 - zh_u

    def at_z(pos):
        pos = pos % 8
        return (ctx_of(x, y, pos // 4, k), pos % 4)

    up, down = at_z(z + 1), at_z(z + 7)
    x_dev = [(ctx_of((x + o) % 4, y, zh, k), zl) for o in range(4)]
    y_right, y_left = (ctx_of(x, (y + 1) % 4, zh, k), zl), (ctx_of(x, (y + 3) % 4, zh, k), zl)
    other = (ctx_of(x, y, zh, 1 - k), zl)

    rest = y * 4 + zh * 2 + k
    mine = x * 8 + y * 2 + k

    def half_plane(n):
        return (ctx_of(n // 8, (n // 2) % 4, zh, n % 2), zl)

    barrier = pltpu.get_barrier_semaphore()

    def greet(dev):
        pl.semaphore_signal(barrier, inc=1, device_id=dev, device_id_type=MESH)

    for dev in (x_dev[1], x_dev[2], x_dev[3], up, down, y_right, y_left, other):
        greet(dev)
    for o in range(1, 4):
        greet((me, (zl + o) % 4))

    def greet_piece(r, carry):
        @pl.when((x != zl) | (r != rest))
        def _():
            greet((zl * 16 + r, x))

        return carry

    lax.fori_loop(0, 16, greet_piece, 0)

    def greet_plane(o, carry):
        greet(half_plane((mine + o) % 32))
        return carry

    lax.fori_loop(1, 32, greet_plane, 0)

    quarter = tok.shape[0]
    width = tok.shape[1]

    def norm_rows(n, carry):
        rows = pl.ds(pl.multiple_of(n * 16, 16), 16)
        wide = tok[rows, :].astype(F32)
        mean = jnp.mean(wide * wide, -1, keepdims=True)
        wide = wide * lax.rsqrt(mean + 1e-06) * norm_gain[...]
        tok_all[rows, :] = wide.astype(BF16)
        return carry

    lax.fori_loop(0, quarter // 16, norm_rows, 0)
    pl.semaphore_wait(barrier, 8 + 3 + 15 + 31 + ((x - zl + 4) % 4 + 3) // 4)

    def remote(src, dst, ss, rs, dev):
        return pltpu.make_async_remote_copy(
            src_ref=src, dst_ref=dst, send_sem=ss, recv_sem=rs, device_id=dev, device_id_type=MESH
        )

    half = quarter // 2

    def tok_copy(n, src, dst, part, dev):
        ref = lambda slot: tok_all.at[pl.ds(slot * quarter + part * half, half)]
        return remote(ref(src), ref(dst), tok_s.at[n], tok_r.at[n], dev)

    def w_slot(c):
        return wq_all.at[pl.ds(pl.multiple_of(c * w_rows, 16), w_rows)]

    w_rows = wq.shape[0]
    sends = [
        tok_copy(0, 0, 2, 0, x_dev[1]),
        tok_copy(3, 0, 1, 1, x_dev[3]),
        tok_copy(1, 0, 2, 1, x_dev[1]),
        tok_copy(2, 0, 1, 0, x_dev[3]),
    ]
    w1_index = (x - zl + 4) % 4
    w1 = remote(wq, w_slot(me), w1_s.at[0], w1_r.at[w1_index], (ctx_of(zl, y, zh, k), zl))
    own_w = pltpu.make_async_copy(wq, w_slot(me), loc.at[2])

    @pl.when(d != 0)
    def _():
        w1.start()

    @pl.when(d == 0)
    def _():
        own_w.start()

    for copy in sends:
        copy.start()

    @pl.when(d == 0)
    def _():
        wkv_all[:, :128] = wk[...]
        wkv_all[:, 128:] = wv[...]

    def slot(i, zhalf, yy):
        return w_slot(ctx_of((x + i) % 4, yy, zhalf, k))

    def zp(i):
        ref = slot(i, zh_u, y)
        return remote(ref, ref, zp_s.at[i], zp_r.at[i], up)

    def zm(i, zhalf):
        ref = slot(i, zhalf, y)
        return remote(ref, ref, zm_s.at[i], zm_r.at[i], down)

    def core(n, ref):
        return remote(ref, ref, co_s.at[n], co_r.at[n], other)

    def y_own(s, ref):
        return (
            remote(ref, ref, yr_s.at[s], yr_r.at[s], y_right),
            remote(ref, ref, yl_s.at[s], yl_r.at[s], y_left),
        )

    def fwd_right(i2, ref):
        return remote(ref, ref, fr_s.at[i2], fr_r.at[i2], y_right)

    def fwd_left(i2, ref):
        return remote(ref, ref, fl_s.at[i2], fl_r.at[i2], y_left)

    def spread(s, ref):
        right, left = y_own(s, ref)
        right.start()
        left.start()
        core(s, ref).start()

    def when_four(i, act):
        @pl.when((i >= 0) & (i < 4))
        def _():
            act(i)

    def z_upper(i):
        ref = slot(i, zh_u, y)

        @pl.when(d == 0)
        def _():
            @pl.when(i == 0)
            def _():
                own_w.wait()

            @pl.when(i != 0)
            def _():
                remote(ref, ref, w1_s.at[0], w1_r.at[i], other).wait_recv()

            zm(i, zh_u).start()

        @pl.when(d != 0)
        def _():
            zp(i).wait_recv()

        zp(i).start()
        spread(i, ref)

    def z_lower(i):
        ref = slot(i, zh_d, y)

        @pl.when(d == 0)
        def _():
            remote(ref, ref, zp_s.at[i], zp_r.at[i], up).wait_recv()

        @pl.when(d != 0)
        def _():
            zm(i, zh_d).wait_recv()

        @pl.when(d >= 2)
        def _():
            zm(i, zh_d).start()

        spread(4 + i, ref)

    rows = wk.shape[0] // 8

    def part(i):
        return pl.ds(pl.multiple_of((k * 4 + i) * rows, 16), rows)

    def key_part(i):
        return wkv_all.at[part(i), pl.ds(0, 128)]

    def value_part(i):
        return wkv_all.at[part(i), pl.ds(128, 128)]

    def kv_core(n, ref):
        return remote(ref, ref, kc_s.at[n], kc_r.at[n], other)

    def kp(i):
        return remote(key_part(i), key_part(i), kp_s.at[i], kp_r.at[i], up)

    def km(i):
        return remote(value_part(i), value_part(i), km_s.at[i], km_r.at[i], down)

    y_l, y_r, y_far = (y + 3) % 4, (y + 1) % 4, (y + 2) % 4

    def ring(i, s, zhalf):
        ref = slot(i, zhalf, y_l)
        y_own(s, ref)[0].wait_recv()

        @pl.when(i % 2 == 0)
        def _():
            fwd_right(s // 2, ref).start()

        core(8 + s, ref).start()
        ref2 = slot(i, zhalf, y_r)
        y_own(s, ref2)[1].wait_recv()

        @pl.when(i % 2 == 1)
        def _():
            fwd_left(s // 2, ref2).start()

        core(16 + s, ref2).start()

    def kv_upper(i):
        @pl.when(d != 0)
        def _():
            kp(i).wait_recv()
            kv_core(i, key_part(i)).start()

            @pl.when(d != 3)
            def _():
                kp(i).start()

    def kv_lower(i):
        @pl.when(d != 0)
        def _():
            km(i).wait_recv()
            kv_core(4 + i, value_part(i)).start()

            @pl.when(d != 1)
            def _():
                km(i).start()

    def ring_upper(i):
        ring(i, i, zh_u)

    def ring_lower(i):
        ring(i, 4 + i, zh_d)

    lane = lax.broadcasted_iota(jnp.int32, (128, 128), 1)

    def doc_row(at, absent):
        return jnp.where(at >= 0, segs[jnp.maximum(at, 0)], absent).astype(F32)

    def down_rows(row):
        return jnp.broadcast_to(row, (128, 128)).T

    def rope_table(n):
        row = block_of[((x + n + n // 2 - n // 3 * 2) % 4) * 16 + rest] * 4 + zl
        docs = down_rows(segs[row].astype(F32))

        def count(j, total):
            return total + jnp.where(doc_row(row - 24 + j, -1) < docs, 1.0, 0.0)

        before = lax.fori_loop(0, 25, count, jnp.zeros((128, 128), F32))
        here = lax.broadcasted_iota(jnp.int32, (128, 1), 0).astype(F32)
        offset = 3072.0 + here - jnp.sum(before, -1, keepdims=True)
        angle = offset * freqs[...]
        rows = pl.ds(pl.multiple_of(n * 128, 128), 128)
        cosine[rows, :] = jnp.cos(angle) * ROPE_SCALE
        turned = jnp.sin(angle) * ROPE_SCALE
        sine[rows, :] = jnp.where(lane < 64, -turned, turned)

    def mask_rows(n):
        for j in range(4):
            docs = down_rows(doc_row(block_of[me] * 4 - 24 + n * 4 + j, 63))
            same = docs == lane.astype(F32)
            k_mask[n, pl.ds(j * 128, 128), :] = jnp.where(same, 1.0, 0.0).astype(BF16)

            @pl.when(n == 6)
            def _():
                q_mask[pl.ds(j * 128, 128), :] = jnp.where(same, 0.0, -1e30).astype(BF16)

    def step(t, carry):
        when_four(t - d, z_upper)
        when_four(t - 4 + d, z_lower)

        @pl.when((d == 0) & (t == 3))
        def _():
            for i in range(4):
                kp(i).start()
                km(i).start()

        when_four(t - 4 - d, kv_upper)
        when_four(t - 8 + d, kv_lower)
        when_four(t - 4 - d, ring_upper)
        when_four(t - 8 + d, ring_lower)
        when_four(t, rope_table)

        @pl.when((t >= 4) & (t < 11))
        def _():
            mask_rows(t - 4)

        return carry

    lax.fori_loop(0, 7, step, 0)

    tok_copy(0, 0, 2, 0, x_dev[1]).wait_recv()
    fwd_a = tok_copy(4, 2, 3, 0, x_dev[1])
    fwd_a.start()
    tok_copy(3, 0, 1, 1, x_dev[3]).wait_recv()
    fwd_b = tok_copy(5, 1, 3, 1, x_dev[3])
    fwd_b.start()

    lax.fori_loop(7, 12, step, 0)

    tok_copy(1, 0, 2, 1, x_dev[1]).wait_recv()
    tok_copy(2, 0, 1, 0, x_dev[3]).wait_recv()

    @pl.when(d != 0)
    def _():
        def core_part(i, carry):
            kv_core(i, key_part(i)).wait_recv()
            kv_core(4 + i, value_part(i)).wait_recv()
            return carry

        lax.fori_loop(0, 4, core_part, 0)

    def turn(t, gain, rows):
        t = t * lax.rsqrt(jnp.mean(t * t, -1, keepdims=True) + 1e-06) * gain[...]
        return (t * cosine[rows, :] + pltpu.roll(t, 64, 1) * sine[rows, :]).astype(BF16)

    def keys_values(first, count):
        rows = pl.ds(first * quarter, count * quarter)
        both = jnp.dot(tok_all[rows, :], wkv_all[...], preferred_element_type=F32)
        key = turn(both[:, :128], k_gain, rows)
        value = both[:, 128:].astype(BF16)
        for p in range(8):
            for n in range(count):
                at = n * quarter + p * 16
                kv_send[0, p, first + n] = key[at : at + 16]
                kv_send[1, p, first + n] = value[at : at + 16]

    early = pl.ds(0, 3)

    def piece(m, r, src_rest, dst_p):
        if m == 0:
            src, dst = kv_send.at[0, dst_p, early], got_k.at[pl.ds(src_rest * 4, 3)]
        elif m == 1:
            src, dst = kv_send.at[0, dst_p, 3], got_k.at[src_rest * 4 + 3]
        else:
            src, dst = kv_send.at[1, dst_p], got_v.at[pl.ds(src_rest * 4, 4)]
        return src, dst, p1_s.at[m, r], p1_r.at[m, src_rest]

    def to_piece(r):
        return (r // 4) * 2 + r % 2

    def send_pieces(m):
        def send_piece(o, carry):
            r = (rest + o) % 16

            @pl.when((x != zl) | (r != rest))
            def _():
                remote(*piece(m, r, rest, to_piece(r)), (zl * 16 + r, x)).start()

            return carry

        lax.fori_loop(0, 16, send_piece, 0)

        @pl.when(x == zl)
        def _():
            src, dst, _, _ = piece(m, rest, rest, to_piece(rest))
            pltpu.make_async_copy(src, dst, own_s.at[m]).start()

    def wait_pieces(m):
        def wait_piece(r, carry):
            @pl.when((x != zl) | (r != rest))
            def _():
                remote(*piece(m, r, r, 0), (zl * 16 + r, x)).wait_recv()

            return carry

        lax.fori_loop(0, 16, wait_piece, 0)

        @pl.when(x == zl)
        def _():
            src, dst, _, _ = piece(m, rest, rest, to_piece(rest))
            pltpu.make_async_copy(src, dst, own_s.at[m]).wait()

    keys_values(0, 3)
    send_pieces(0)
    tok_copy(4, 2, 3, 0, x_dev[1]).wait_recv()
    tok_copy(5, 1, 3, 1, x_dev[3]).wait_recv()
    keys_values(3, 1)
    send_pieces(1)
    send_pieces(2)

    def far_upper(i):
        finish(i, i, zh_u)

    def far_lower(i):
        finish(i, 4 + i, zh_d)

    def finish(i, s, zhalf):
        ref = slot(i, zhalf, y_far)

        @pl.when(i % 2 == 0)
        def _():
            fwd_right(s // 2, ref).wait_recv()

        @pl.when(i % 2 == 1)
        def _():
            fwd_left(s // 2, ref).wait_recv()

        core(24 + s, ref).start()

    def far_step(t, carry):
        when_four(t - d, far_upper)
        when_four(t - 4 + d, far_lower)
        return carry

    lax.fori_loop(0, 8, far_step, 0)

    any_w = w_slot(me)

    def wait_core(n, carry):
        core(n, any_w).wait_recv()
        return carry

    lax.fori_loop(0, 32, wait_core, 0)

    def heads(n):
        return pl.ds(n * 2, 2)

    def x_step(n, o):
        return remote(
            q_send.at[heads(n), (0, 1, 3, 2)[o]], qx.at[heads(n), x], qx_s.at[n, o],
            qx_r.at[n, o], x_dev[o],
        )

    def z_step(n, src, to):
        o = (to - zl + 4) % 4
        return remote(
            src, q_out.at[heads(n), zl], qz_s.at[n, o], qz_r.at[n, o], (me, to)
        )

    def z_move(n, src, frm):
        @pl.when(frm != zl)
        def _():
            z_step(n, src, frm).start()

        @pl.when(frm == zl)
        def _():
            pltpu.make_async_copy(
                src, q_out.at[heads(n), zl], loc.at[3 + n]
            ).start()

    def project(n, carry):
        columns = pl.ds(pl.multiple_of(n * 256, 256), 256)
        both = jnp.dot(tok_all[...], wq_all[:, columns], preferred_element_type=F32)
        for h in range(2):
            head = turn(both[:, h * 128 : h * 128 + 128], q_gain, pl.ds(0, 4 * quarter))
            q_send[n * 2 + h] = head.reshape(4, quarter, 128)
        for o in (1, 3, 2):
            x_step(n, o).start()
        z_move(n, q_send.at[heads(n), 0], x)
        return carry

    lax.fori_loop(0, 4, project, 0)

    own_keys = pl.ds(pl.multiple_of(mine * 16, 16), 16)

    def plane(m, n):
        return remote(
            picked.at[m, n], kv_all.at[m, :, own_keys], p2_s.at[m, n], p2_r.at[m, mine],
            half_plane(n),
        )

    def pick(m, n):
        block = block_of[half_plane(n)[0]]
        for i in range(7):
            slot = slot_of[jnp.maximum(block - 6 + i, 0)]
            picked[m, n, i] = (got_k, got_v)[m][slot]

    def send_plane(m):
        for dx, dy, dk in PLACES:
            n = ((x + dx) % 4) * 8 + ((y + dy) % 4) * 2 + (k + dk) % 2
            pick(m, n)
            plane(m, n).start()
        pick(m, mine)
        pltpu.make_async_copy(picked.at[m, mine], kv_all.at[m, :, own_keys], loc.at[m]).start()

    wait_pieces(0)
    wait_pieces(1)
    send_plane(0)
    wait_pieces(2)
    send_plane(1)

    def pass_on(n, carry):
        for o in (1, 3, 2):
            frm = (x - o + 4) % 4
            remote(
                q_send.at[heads(n), 0], qx.at[heads(n), frm], qx_s.at[n, o], qx_r.at[n, o],
                (ctx_of(frm, y, zh, k), zl),
            ).wait_recv()
            z_move(n, qx.at[heads(n), frm], frm)
        return carry

    lax.fori_loop(0, 4, pass_on, 0)

    def q_here(n, carry):
        pltpu.make_async_copy(
            q_send.at[heads(n), 0], q_out.at[heads(n), zl], loc.at[3 + n]
        ).wait()
        for o in (1, 2, 3):
            frm = (zl - o + 4) % 4
            remote(
                q_send.at[heads(n), 0], q_out.at[heads(n), frm], qz_s.at[n, o], qz_r.at[n, o],
                (me, frm),
            ).wait_recv()
        return carry

    lax.fori_loop(0, 4, q_here, 0)
    for m in range(2):
        pltpu.make_async_copy(picked.at[m, mine], kv_all.at[m, :, own_keys], loc.at[m]).wait()

    def plane_here(o, carry):
        n = (mine + o) % 32
        theirs = pl.ds(pl.multiple_of(n * 16, 16), 16)
        for m in range(2):
            remote(
                picked.at[m, n], kv_all.at[m, :, theirs], p2_s.at[m, n], p2_r.at[m, n],
                half_plane(n),
            ).wait_recv()
        return carry

    lax.fori_loop(1, 32, plane_here, 0)
    attend(q_out, kv_all, k_mask, q_mask, o_ref)

    def drain_q(n, carry):
        for o in (1, 2, 3):
            x_step(n, o).wait_send()
            z_step(n, q_send.at[heads(n), 0], (zl + o) % 4).wait_send()
        return carry

    lax.fori_loop(0, 4, drain_q, 0)

    def drain_piece(r, carry):
        @pl.when((x != zl) | (r != rest))
        def _():
            for m in range(3):
                remote(*piece(m, r, rest, to_piece(r)), (zl * 16 + r, x)).wait_send()

        return carry

    lax.fori_loop(0, 16, drain_piece, 0)

    def drain_plane(o, carry):
        for m in range(2):
            plane(m, (mine + o) % 32).wait_send()
        return carry

    lax.fori_loop(1, 32, drain_plane, 0)

    def drain_core(n, carry):
        core(n, any_w).wait_send()
        return carry

    lax.fori_loop(0, 32, drain_core, 0)

    def drain_y(s, carry):
        right, left = y_own(s, any_w)
        right.wait_send()
        left.wait_send()
        return carry

    lax.fori_loop(0, 8, drain_y, 0)

    def drain_four(i, carry):
        zp(i).wait_send()
        fwd_right(i, any_w).wait_send()
        fwd_left(i, any_w).wait_send()

        @pl.when((d == 0) | (d >= 2))
        def _():
            zm(i, zh_u).wait_send()
            km(i).wait_send()

        @pl.when(d <= 2)
        def _():
            kp(i).wait_send()

        @pl.when(d != 0)
        def _():
            kv_core(i, key_part(i)).wait_send()
            kv_core(4 + i, value_part(i)).wait_send()

        return carry

    lax.fori_loop(0, 4, drain_four, 0)
    for copy in sends:
        copy.wait_send()
    fwd_a.wait_send()
    fwd_b.wait_send()

    @pl.when(d != 0)
    def _():
        w1.wait_send()


def front(block_of, slot_of, segs, freqs, tokens, norm_gain, w_query, w_key, w_value, q_gain, k_gain):
    vmem = pl.BlockSpec(memory_space=pltpu.VMEM)
    dma = pltpu.SemaphoreType.DMA
    pair = lambda *n: [dma(n), dma(n)]
    rows, width = tokens.shape
    columns = w_query.shape[1]
    flops = 2 * 4 * rows * width * (columns + 256)
    return pl.pallas_call(
        front_kernel,
        out_shape=jax.ShapeDtypeStruct((4 * rows, columns), BF16),
        in_specs=[pl.BlockSpec(memory_space=pltpu.SMEM)] * 2 + [vmem] * 9,
        out_specs=vmem,
        scratch_shapes=[
            pltpu.VMEM((4 * rows, width), BF16),
            pltpu.VMEM((width, columns), BF16),
            pltpu.VMEM((width, 256), BF16),
            pltpu.VMEM((8, 4, rows, 128), BF16),
            pltpu.VMEM((8, 4, rows, 128), BF16),
            pltpu.VMEM((2, 8, 4, 16, 128), BF16),
            pltpu.VMEM((64, 16, 128), BF16),
            pltpu.VMEM((64, 16, 128), BF16),
            pltpu.VMEM((2, 32, 7, 16, 128), BF16),
            pltpu.VMEM((8, 4, rows, 128), BF16),
            pltpu.VMEM((2, 7, 4 * rows, 128), BF16),
            pltpu.VMEM((4 * rows, 128), F32),
            pltpu.VMEM((4 * rows, 128), F32),
            pltpu.VMEM((7, 4 * rows, 128), BF16),
            pltpu.VMEM((4 * rows, 128), BF16),
            dma((7,)),
        ] + pair(6) + [dma((1,)), dma((4,))] + pair(4) + pair(4) + pair(8) + pair(8)
        + pair(4) + pair(4) + pair(32) + pair(4) + pair(4) + pair(8)
        + pair(4, 4) + pair(4, 4) + pair(3, 16) + pair(2, 32) + [dma((3,))],
        cost_estimate=pl.CostEstimate(flops=flops, bytes_accessed=10 << 20, transcendentals=0),
        compiler_params=pltpu.CompilerParams(
            collective_id=0, has_side_effects=True, vmem_limit_bytes=56 << 20
        ),
    )(block_of, slot_of, segs, freqs, tokens, norm_gain, w_query, w_key, w_value, q_gain, k_gain)


def shards(tokens, norm_gain, w_query, w_key, w_value, query_gain, key_gain, segments, block_of):
    blocks = jnp.arange(64, dtype=jnp.int32)
    ahead = (blocks // 16 - lax.axis_index("tensor") + 4) % 4
    slot = (blocks % 16) * 4 + ahead + ahead // 2 - ahead // 3 * 2
    slot_of = jnp.sum(jnp.where(block_of[None, :] == blocks[:, None], slot[None, :], 0), 1)
    freqs = jnp.asarray(yarn_frequencies(128) * 2, F32)
    return front(
        block_of, slot_of, segments.reshape(-1, 1, 128), freqs[None, :], tokens,
        norm_gain[None, :], w_query, w_key, w_value, query_gain[None, :], key_gain[None, :],
    )


def solution(mesh):
    return jax.shard_map(
        shards,
        mesh=mesh,
        in_specs=(
            P(("context", "tensor"), None),
            P(),
            P("context", "tensor"),
            P(None, "tensor"),
            P(None, "tensor"),
            P(),
            P(),
            P(),
            P(),
        ),
        out_specs=P("context", "tensor"),
        check_vma=False,
    )
```

```python
import math

import jax
import jax.numpy as jnp
from jax import lax
from jax.experimental import pallas as pl
from jax.experimental.pallas import tpu as pltpu
from jax.sharding import PartitionSpec as P

MESH = pl.DeviceIdType.MESH
BF16 = jnp.bfloat16
F32 = jnp.float32
ROPE_SCALE = 0.1 * math.log(4.0) + 1.0
STEPS = (
    (1, 0), (0, 1), (3, 0), (0, 3), (1, 1), (3, 3), (1, 3), (3, 1),
    (2, 0), (0, 2), (2, 1), (1, 2), (2, 3), (3, 2), (2, 2),
)
PLACES = ((0, 0, 1),) + tuple((dx, dy, dk) for dk in (0, 1) for dx, dy in STEPS)


def yarn_frequencies(dim):
    theta = 1000000.0
    factor = 4.0
    initial = 32768.0
    lowest = math.floor(dim * math.log(initial / (32.0 * 2 * math.pi)) / (2 * math.log(theta)))
    highest = math.ceil(dim * math.log(initial / (1.0 * 2 * math.pi)) / (2 * math.log(theta)))
    lowest = max(lowest, 0)
    highest = min(highest, dim - 1)
    spread = max(highest - lowest, 0.001)
    result = []
    for index in range(dim // 2):
        base_freq = theta ** (-2.0 * index / dim)
        ramp = min(max((index - lowest) / spread, 0.0), 1.0)
        result.append(base_freq / factor * ramp + base_freq * (1.0 - ramp))
    return result


def ctx_of(x, y, zh, k):
    return x * 16 + y * 4 + zh * 2 + k


def place():
    c = lax.axis_index("context")
    return c // 16, (c // 4) % 4, (c // 2) % 2, c % 2, lax.axis_index("tensor")


def attend(q_ref, kv_ref, k_mask, q_mask, o_ref):
    heads = q_ref.shape[0]
    length = q_mask.shape[0]
    span = 6 * length
    step = 256
    scale = 128 ** (-0.5) * math.log2(math.e)
    ones = jnp.ones((step, 128), BF16)

    def score(h, r):
        quarters = step // 128
        q = q_ref[h, pl.ds(r * quarters, quarters)].reshape(step, 128)
        q = jnp.concatenate([q, q_mask[pl.ds(r * step, step), :]], -1)
        tiles = []
        top = None
        for at in range(r * step, span + r * step + step, step):
            rows = (at // length, pl.ds(at % length, step))
            keys = jnp.concatenate([kv_ref[(0,) + rows], k_mask[rows]], -1)
            s = lax.dot_general(q, keys, (((1,), (1,)), ((), ())), preferred_element_type=F32)
            if at == span + r * step:
                here = lax.broadcasted_iota(jnp.int32, s.shape, 0)
                s = jnp.where(lax.broadcasted_iota(jnp.int32, s.shape, 1) <= here, s, -1e30)
            tiles.append((rows, s))
            for c in range(0, step, 128):
                best = s[:, c : c + 128]
                top = best if top is None else jnp.maximum(top, best)
        return tiles, jnp.max(top, -1, keepdims=True)

    def finish(h, r, tiles, top):
        summed = None
        for rows, s in tiles:
            e = jnp.exp2((s - top) * scale).astype(BF16)
            values = jnp.concatenate([kv_ref[(1,) + rows], ones], -1)
            part = jnp.dot(e, values, preferred_element_type=F32)
            summed = part if summed is None else summed + part
        out = summed[:, :128] / summed[:, 128:]
        columns = pl.ds(pl.multiple_of(h * 128, 128), 128)
        o_ref[pl.ds(r * step, step), columns] = out.astype(BF16)

    def some(g, carry):
        ahead = None
        for n in range(4):
            for r in range(length // step):
                h = g * 4 + n
                now = (h, r) + score(h, r)
                if ahead is not None:
                    finish(*ahead)
                ahead = now
        finish(*ahead)
        return carry

    lax.fori_loop(0, heads // 4, some, 0)


def front_kernel(
    block_of, slot_of, segs, freqs, tok, norm_gain, wq, wk, wv, q_gain, k_gain,
    o_ref,
    tok_all, wq_all, wkv_all, q_send, qx, kv_send, got_k, got_v, picked,
    q_out, kv_all, cosine, sine, k_mask, q_mask,
    loc, tok_s, tok_r, w1_s, w1_r, zp_s, zp_r, zm_s, zm_r,
    yr_s, yr_r, yl_s, yl_r, fr_s, fr_r, fl_s, fl_r, co_s, co_r,
    kp_s, kp_r, km_s, km_r, kc_s, kc_r,
    qx_s, qx_r, qz_s, qz_r, p1_s, p1_r, p2_s, p2_r, own_s,
):
    x, y, zh, k, zl = place()
    me = ctx_of(x, y, zh, k)
    z = zh * 4 + zl
    d = (zl - x + 4) % 4
    zh_u = ((z - d + 8) % 8) // 4
    zh_d = 1 - zh_u

    def at_z(pos):
        pos = pos % 8
        return (ctx_of(x, y, pos // 4, k), pos % 4)

    up, down = at_z(z + 1), at_z(z + 7)
    x_dev = [(ctx_of((x + o) % 4, y, zh, k), zl) for o in range(4)]
    y_right, y_left = (ctx_of(x, (y + 1) % 4, zh, k), zl), (ctx_of(x, (y + 3) % 4, zh, k), zl)
    other = (ctx_of(x, y, zh, 1 - k), zl)

    rest = y * 4 + zh * 2 + k
    mine = x * 8 + y * 2 + k

    def half_plane(n):
        return (ctx_of(n // 8, (n // 2) % 4, zh, n % 2), zl)

    barrier = pltpu.get_barrier_semaphore()

    def greet(dev):
        pl.semaphore_signal(barrier, inc=1, device_id=dev, device_id_type=MESH)

    for dev in (x_dev[1], x_dev[2], x_dev[3], up, down, y_right, y_left, other):
        greet(dev)
    for o in range(1, 4):
        greet((me, (zl + o) % 4))

    def greet_piece(r, carry):
        @pl.when((x != zl) | (r != rest))
        def _():
            greet((zl * 16 + r, x))

        return carry

    lax.fori_loop(0, 16, greet_piece, 0)

    def greet_plane(o, carry):
        greet(half_plane((mine + o) % 32))
        return carry

    lax.fori_loop(1, 32, greet_plane, 0)

    quarter = tok.shape[0]
    width = tok.shape[1]

    def norm_rows(n, carry):
        rows = pl.ds(pl.multiple_of(n * 16, 16), 16)
        wide = tok[rows, :].astype(F32)
        mean = jnp.mean(wide * wide, -1, keepdims=True)
        wide = wide * lax.rsqrt(mean + 1e-06) * norm_gain[...]
        tok_all[rows, :] = wide.astype(BF16)
        return carry

    pl.semaphore_wait(barrier, 8 + 3 + 15 + 31 + ((x - zl + 4) % 4 + 3) // 4)

    def remote(src, dst, ss, rs, dev):
        return pltpu.make_async_remote_copy(
            src_ref=src, dst_ref=dst, send_sem=ss, recv_sem=rs, device_id=dev, device_id_type=MESH
        )

    half = quarter // 2

    def tok_copy(n, src, dst, part, dev):
        ref = lambda slot: tok_all.at[pl.ds(slot * quarter + part * half, half)]
        return remote(ref(src), ref(dst), tok_s.at[n], tok_r.at[n], dev)

    def w_slot(c):
        return wq_all.at[pl.ds(pl.multiple_of(c * w_rows, 16), w_rows)]

    w_rows = wq.shape[0]
    sends = [
        tok_copy(0, 0, 2, 0, x_dev[1]),
        tok_copy(3, 0, 1, 1, x_dev[3]),
        tok_copy(1, 0, 2, 1, x_dev[1]),
        tok_copy(2, 0, 1, 0, x_dev[3]),
    ]
    w1_index = (x - zl + 4) % 4
    w1 = remote(wq, w_slot(me), w1_s.at[0], w1_r.at[w1_index], (ctx_of(zl, y, zh, k), zl))
    own_w = pltpu.make_async_copy(wq, w_slot(me), loc.at[2])

    @pl.when(d != 0)
    def _():
        w1.start()

    @pl.when(d == 0)
    def _():
        own_w.start()

    own_k = pltpu.make_async_copy(wk, wkv_all.at[:, pl.ds(0, 128)], loc.at[0])
    own_v = pltpu.make_async_copy(wv, wkv_all.at[:, pl.ds(128, 128)], loc.at[1])

    @pl.when(d == 0)
    def _():
        own_k.start()
        own_v.start()

    def slot(i, zhalf, yy):
        return w_slot(ctx_of((x + i) % 4, yy, zhalf, k))

    def zp(i):
        ref = slot(i, zh_u, y)
        return remote(ref, ref, zp_s.at[i], zp_r.at[i], up)

    def zm(i, zhalf):
        ref = slot(i, zhalf, y)
        return remote(ref, ref, zm_s.at[i], zm_r.at[i], down)

    def core(n, ref):
        return remote(ref, ref, co_s.at[n], co_r.at[n], other)

    def y_own(s, ref):
        return (
            remote(ref, ref, yr_s.at[s], yr_r.at[s], y_right),
            remote(ref, ref, yl_s.at[s], yl_r.at[s], y_left),
        )

    def fwd_right(i2, ref):
        return remote(ref, ref, fr_s.at[i2], fr_r.at[i2], y_right)

    def fwd_left(i2, ref):
        return remote(ref, ref, fl_s.at[i2], fl_r.at[i2], y_left)

    def spread(s, ref):
        right, left = y_own(s, ref)
        right.start()
        left.start()
        core(s, ref).start()

    def when_four(i, act):
        @pl.when((i >= 0) & (i < 4))
        def _():
            act(i)

    def z_upper(i):
        ref = slot(i, zh_u, y)

        @pl.when(d == 0)
        def _():
            @pl.when(i == 0)
            def _():
                own_w.wait()

            @pl.when(i != 0)
            def _():
                remote(ref, ref, w1_s.at[0], w1_r.at[i], other).wait_recv()

            zm(i, zh_u).start()

        @pl.when(d != 0)
        def _():
            zp(i).wait_recv()

        zp(i).start()
        spread(i, ref)

    def z_lower(i):
        ref = slot(i, zh_d, y)

        @pl.when(d == 0)
        def _():
            remote(ref, ref, zp_s.at[i], zp_r.at[i], up).wait_recv()

        @pl.when(d != 0)
        def _():
            zm(i, zh_d).wait_recv()

        @pl.when(d >= 2)
        def _():
            zm(i, zh_d).start()

        spread(4 + i, ref)

    rows = wk.shape[0] // 8

    def part(i):
        return pl.ds(pl.multiple_of((k * 4 + i) * rows, 16), rows)

    def key_part(i):
        return wkv_all.at[part(i), pl.ds(0, 128)]

    def value_part(i):
        return wkv_all.at[part(i), pl.ds(128, 128)]

    def kv_core(n, ref):
        return remote(ref, ref, kc_s.at[n], kc_r.at[n], other)

    def kp(i):
        return remote(key_part(i), key_part(i), kp_s.at[i], kp_r.at[i], up)

    def km(i):
        return remote(value_part(i), value_part(i), km_s.at[i], km_r.at[i], down)

    y_l, y_r, y_far = (y + 3) % 4, (y + 1) % 4, (y + 2) % 4

    def ring(i, s, zhalf):
        ref = slot(i, zhalf, y_l)
        y_own(s, ref)[0].wait_recv()

        @pl.when(i % 2 == 0)
        def _():
            fwd_right(s // 2, ref).start()

        core(8 + s, ref).start()
        ref2 = slot(i, zhalf, y_r)
        y_own(s, ref2)[1].wait_recv()

        @pl.when(i % 2 == 1)
        def _():
            fwd_left(s // 2, ref2).start()

        core(16 + s, ref2).start()

    def kv_upper(i):
        @pl.when(d != 0)
        def _():
            kp(i).wait_recv()
            kv_core(i, key_part(i)).start()

            @pl.when(d != 3)
            def _():
                kp(i).start()

    def kv_lower(i):
        @pl.when(d != 0)
        def _():
            km(i).wait_recv()
            kv_core(4 + i, value_part(i)).start()

            @pl.when(d != 1)
            def _():
                km(i).start()

    def ring_upper(i):
        ring(i, i, zh_u)

    def ring_lower(i):
        ring(i, 4 + i, zh_d)

    lane = lax.broadcasted_iota(jnp.int32, (128, 128), 1)

    def doc_row(at, absent):
        return jnp.where(at >= 0, segs[jnp.maximum(at, 0)], absent).astype(F32)

    def down_rows(row):
        return jnp.broadcast_to(row, (128, 128)).T

    def rope_table(n):
        row = block_of[((x + n + n // 2 - n // 3 * 2) % 4) * 16 + rest] * 4 + zl
        docs = down_rows(segs[row].astype(F32))

        def count(j, total):
            return total + jnp.where(doc_row(row - 24 + j, -1) < docs, 1.0, 0.0)

        before = lax.fori_loop(0, 25, count, jnp.zeros((128, 128), F32))
        here = lax.broadcasted_iota(jnp.int32, (128, 1), 0).astype(F32)
        offset = 3072.0 + here - jnp.sum(before, -1, keepdims=True)
        angle = offset * freqs[...]
        rows = pl.ds(pl.multiple_of(n * 128, 128), 128)
        cosine[rows, :] = jnp.cos(angle) * ROPE_SCALE
        turned = jnp.sin(angle) * ROPE_SCALE
        sine[rows, :] = jnp.where(lane < 64, -turned, turned)

    def mask_rows(n):
        for j in range(4):
            docs = down_rows(doc_row(block_of[me] * 4 - 24 + n * 4 + j, 63))
            same = docs == lane.astype(F32)
            k_mask[n, pl.ds(j * 128, 128), :] = jnp.where(same, 1.0, 0.0).astype(BF16)

            @pl.when(n == 6)
            def _():
                q_mask[pl.ds(j * 128, 128), :] = jnp.where(same, 0.0, -1e30).astype(BF16)

    def step(t, carry):
        when_four(t - d, z_upper)
        when_four(t - 4 + d, z_lower)

        @pl.when((d == 0) & (t == 3))
        def _():
            own_k.wait()
            own_v.wait()
            for i in range(4):
                kp(i).start()
                km(i).start()

        when_four(t - 4 - d, kv_upper)
        when_four(t - 8 + d, kv_lower)
        when_four(t - 4 - d, ring_upper)
        when_four(t - 8 + d, ring_lower)
        when_four(t - 1, rope_table)

        @pl.when((t >= 4) & (t < 11))
        def _():
            mask_rows(t - 4)

        return carry

    lax.fori_loop(0, 1, step, 0)
    lax.fori_loop(0, quarter // 16, norm_rows, 0)
    for copy in sends:
        copy.start()
    lax.fori_loop(1, 7, step, 0)

    tok_copy(0, 0, 2, 0, x_dev[1]).wait_recv()
    fwd_a = tok_copy(4, 2, 3, 0, x_dev[1])
    fwd_a.start()
    tok_copy(3, 0, 1, 1, x_dev[3]).wait_recv()
    fwd_b = tok_copy(5, 1, 3, 1, x_dev[3])
    fwd_b.start()

    lax.fori_loop(7, 12, step, 0)

    tok_copy(1, 0, 2, 1, x_dev[1]).wait_recv()
    tok_copy(2, 0, 1, 0, x_dev[3]).wait_recv()

    @pl.when(d != 0)
    def _():
        def core_part(i, carry):
            kv_core(i, key_part(i)).wait_recv()
            kv_core(4 + i, value_part(i)).wait_recv()
            return carry

        lax.fori_loop(0, 4, core_part, 0)

    def turn(t, gain, rows):
        t = t * lax.rsqrt(jnp.mean(t * t, -1, keepdims=True) + 1e-06) * gain[...]
        return (t * cosine[rows, :] + pltpu.roll(t, 64, 1) * sine[rows, :]).astype(BF16)

    def keys_values(first, count):
        rows = pl.ds(first * quarter, count * quarter)
        both = jnp.dot(tok_all[rows, :], wkv_all[...], preferred_element_type=F32)
        key = turn(both[:, :128], k_gain, rows)
        value = both[:, 128:].astype(BF16)
        for p in range(8):
            for n in range(count):
                at = n * quarter + p * 16
                kv_send[0, p, first + n] = key[at : at + 16]
                kv_send[1, p, first + n] = value[at : at + 16]

    early = pl.ds(0, 3)

    def piece(m, r, src_rest, dst_p):
        if m == 0:
            src, dst = kv_send.at[0, dst_p, early], got_k.at[pl.ds(src_rest * 4, 3)]
        elif m == 1:
            src, dst = kv_send.at[0, dst_p, 3], got_k.at[src_rest * 4 + 3]
        else:
            src, dst = kv_send.at[1, dst_p], got_v.at[pl.ds(src_rest * 4, 4)]
        return src, dst, p1_s.at[m, r], p1_r.at[m, src_rest]

    def to_piece(r):
        return (r // 4) * 2 + r % 2

    def send_pieces(m):
        def send_piece(o, carry):
            r = (rest + o) % 16

            @pl.when((x != zl) | (r != rest))
            def _():
                remote(*piece(m, r, rest, to_piece(r)), (zl * 16 + r, x)).start()

            return carry

        lax.fori_loop(0, 16, send_piece, 0)

        @pl.when(x == zl)
        def _():
            src, dst, _, _ = piece(m, rest, rest, to_piece(rest))
            pltpu.make_async_copy(src, dst, own_s.at[m]).start()

    def wait_pieces(m):
        def wait_piece(r, carry):
            @pl.when((x != zl) | (r != rest))
            def _():
                remote(*piece(m, r, r, 0), (zl * 16 + r, x)).wait_recv()

            return carry

        lax.fori_loop(0, 16, wait_piece, 0)

        @pl.when(x == zl)
        def _():
            src, dst, _, _ = piece(m, rest, rest, to_piece(rest))
            pltpu.make_async_copy(src, dst, own_s.at[m]).wait()

    keys_values(0, 3)
    send_pieces(0)
    tok_copy(4, 2, 3, 0, x_dev[1]).wait_recv()
    tok_copy(5, 1, 3, 1, x_dev[3]).wait_recv()
    keys_values(3, 1)
    send_pieces(1)
    send_pieces(2)

    def far_upper(i):
        finish(i, i, zh_u)

    def far_lower(i):
        finish(i, 4 + i, zh_d)

    def finish(i, s, zhalf):
        ref = slot(i, zhalf, y_far)

        @pl.when(i % 2 == 0)
        def _():
            fwd_right(s // 2, ref).wait_recv()

        @pl.when(i % 2 == 1)
        def _():
            fwd_left(s // 2, ref).wait_recv()

        core(24 + s, ref).start()

    def far_step(t, carry):
        when_four(t - d, far_upper)
        when_four(t - 4 + d, far_lower)
        return carry

    lax.fori_loop(0, 8, far_step, 0)

    any_w = w_slot(me)

    def wait_core(n, carry):
        core(n, any_w).wait_recv()
        return carry

    lax.fori_loop(0, 32, wait_core, 0)

    def heads(n):
        return pl.ds(n * 2, 2)

    def x_step(n, o):
        return remote(
            q_send.at[heads(n), (0, 1, 3, 2)[o]], qx.at[heads(n), x], qx_s.at[n, o],
            qx_r.at[n, o], x_dev[o],
        )

    def z_step(n, src, to):
        o = (to - zl + 4) % 4
        return remote(
            src, q_out.at[heads(n), zl], qz_s.at[n, o], qz_r.at[n, o], (me, to)
        )

    def z_move(n, src, frm):
        @pl.when(frm != zl)
        def _():
            z_step(n, src, frm).start()

        @pl.when(frm == zl)
        def _():
            pltpu.make_async_copy(
                src, q_out.at[heads(n), zl], loc.at[3 + n]
            ).start()

    def project(n, carry):
        columns = pl.ds(pl.multiple_of(n * 256, 256), 256)
        both = jnp.dot(tok_all[...], wq_all[:, columns], preferred_element_type=F32)
        for h in range(2):
            head = turn(both[:, h * 128 : h * 128 + 128], q_gain, pl.ds(0, 4 * quarter))
            q_send[n * 2 + h] = head.reshape(4, quarter, 128)
        for o in (1, 3, 2):
            x_step(n, o).start()
        z_move(n, q_send.at[heads(n), 0], x)
        return carry

    own_keys = pl.ds(pl.multiple_of(mine * 16, 16), 16)

    def plane(m, n):
        return remote(
            picked.at[m, n], kv_all.at[m, :, own_keys], p2_s.at[m, n], p2_r.at[m, mine],
            half_plane(n),
        )

    def pick(m, n):
        block = block_of[half_plane(n)[0]]
        for i in range(7):
            slot = slot_of[jnp.maximum(block - 6 + i, 0)]
            picked[m, n, i] = (got_k, got_v)[m][slot]

    def send_plane(m):
        for dx, dy, dk in PLACES:
            n = ((x + dx) % 4) * 8 + ((y + dy) % 4) * 2 + (k + dk) % 2
            pick(m, n)
            plane(m, n).start()
        pick(m, mine)
        pltpu.make_async_copy(picked.at[m, mine], kv_all.at[m, :, own_keys], loc.at[m]).start()

    def pass_on(n, carry):
        for o in (1, 3, 2):
            frm = (x - o + 4) % 4
            remote(
                q_send.at[heads(n), 0], qx.at[heads(n), frm], qx_s.at[n, o], qx_r.at[n, o],
                (ctx_of(frm, y, zh, k), zl),
            ).wait_recv()
            z_move(n, qx.at[heads(n), frm], frm)
        return carry

    lax.fori_loop(0, 4, project, 0)
    lax.fori_loop(0, 2, pass_on, 0)
    wait_pieces(0)
    wait_pieces(1)
    send_plane(0)
    lax.fori_loop(2, 4, pass_on, 0)
    wait_pieces(2)
    send_plane(1)


    def q_here(n, carry):
        pltpu.make_async_copy(
            q_send.at[heads(n), 0], q_out.at[heads(n), zl], loc.at[3 + n]
        ).wait()
        for o in (1, 2, 3):
            frm = (zl - o + 4) % 4
            remote(
                q_send.at[heads(n), 0], q_out.at[heads(n), frm], qz_s.at[n, o], qz_r.at[n, o],
                (me, frm),
            ).wait_recv()
        return carry

    lax.fori_loop(0, 4, q_here, 0)
    for m in range(2):
        pltpu.make_async_copy(picked.at[m, mine], kv_all.at[m, :, own_keys], loc.at[m]).wait()

    def plane_here(o, carry):
        n = (mine + o) % 32
        theirs = pl.ds(pl.multiple_of(n * 16, 16), 16)
        for m in range(2):
            remote(
                picked.at[m, n], kv_all.at[m, :, theirs], p2_s.at[m, n], p2_r.at[m, n],
                half_plane(n),
            ).wait_recv()
        return carry

    lax.fori_loop(1, 32, plane_here, 0)
    attend(q_out, kv_all, k_mask, q_mask, o_ref)

    def drain_q(n, carry):
        for o in (1, 2, 3):
            x_step(n, o).wait_send()
            z_step(n, q_send.at[heads(n), 0], (zl + o) % 4).wait_send()
        return carry

    lax.fori_loop(0, 4, drain_q, 0)

    def drain_piece(r, carry):
        @pl.when((x != zl) | (r != rest))
        def _():
            for m in range(3):
                remote(*piece(m, r, rest, to_piece(r)), (zl * 16 + r, x)).wait_send()

        return carry

    lax.fori_loop(0, 16, drain_piece, 0)

    def drain_plane(o, carry):
        for m in range(2):
            plane(m, (mine + o) % 32).wait_send()
        return carry

    lax.fori_loop(1, 32, drain_plane, 0)

    def drain_core(n, carry):
        core(n, any_w).wait_send()
        return carry

    lax.fori_loop(0, 32, drain_core, 0)

    def drain_y(s, carry):
        right, left = y_own(s, any_w)
        right.wait_send()
        left.wait_send()
        return carry

    lax.fori_loop(0, 8, drain_y, 0)

    def drain_four(i, carry):
        zp(i).wait_send()
        fwd_right(i, any_w).wait_send()
        fwd_left(i, any_w).wait_send()

        @pl.when((d == 0) | (d >= 2))
        def _():
            zm(i, zh_u).wait_send()
            km(i).wait_send()

        @pl.when(d <= 2)
        def _():
            kp(i).wait_send()

        @pl.when(d != 0)
        def _():
            kv_core(i, key_part(i)).wait_send()
            kv_core(4 + i, value_part(i)).wait_send()

        return carry

    lax.fori_loop(0, 4, drain_four, 0)
    for copy in sends:
        copy.wait_send()
    fwd_a.wait_send()
    fwd_b.wait_send()

    @pl.when(d != 0)
    def _():
        w1.wait_send()


def front(block_of, slot_of, segs, freqs, tokens, norm_gain, w_query, w_key, w_value, q_gain, k_gain):
    vmem = pl.BlockSpec(memory_space=pltpu.VMEM)
    dma = pltpu.SemaphoreType.DMA
    pair = lambda *n: [dma(n), dma(n)]
    rows, width = tokens.shape
    columns = w_query.shape[1]
    flops = 2 * 4 * rows * width * (columns + 256)
    return pl.pallas_call(
        front_kernel,
        out_shape=jax.ShapeDtypeStruct((4 * rows, columns), BF16),
        in_specs=[pl.BlockSpec(memory_space=pltpu.SMEM)] * 2 + [vmem] * 5
        + [pl.BlockSpec(memory_space=pl.ANY)] * 2 + [vmem] * 2,
        out_specs=vmem,
        scratch_shapes=[
            pltpu.VMEM((4 * rows, width), BF16),
            pltpu.VMEM((width, columns), BF16),
            pltpu.VMEM((width, 256), BF16),
            pltpu.VMEM((8, 4, rows, 128), BF16),
            pltpu.VMEM((8, 4, rows, 128), BF16),
            pltpu.VMEM((2, 8, 4, 16, 128), BF16),
            pltpu.VMEM((64, 16, 128), BF16),
            pltpu.VMEM((64, 16, 128), BF16),
            pltpu.VMEM((2, 32, 7, 16, 128), BF16),
            pltpu.VMEM((8, 4, rows, 128), BF16),
            pltpu.VMEM((2, 7, 4 * rows, 128), BF16),
            pltpu.VMEM((4 * rows, 128), F32),
            pltpu.VMEM((4 * rows, 128), F32),
            pltpu.VMEM((7, 4 * rows, 128), BF16),
            pltpu.VMEM((4 * rows, 128), BF16),
            dma((7,)),
        ] + pair(6) + [dma((1,)), dma((4,))] + pair(4) + pair(4) + pair(8) + pair(8)
        + pair(4) + pair(4) + pair(32) + pair(4) + pair(4) + pair(8)
        + pair(4, 4) + pair(4, 4) + pair(3, 16) + pair(2, 32) + [dma((3,))],
        cost_estimate=pl.CostEstimate(flops=flops, bytes_accessed=10 << 20, transcendentals=0),
        compiler_params=pltpu.CompilerParams(
            collective_id=0, has_side_effects=True, vmem_limit_bytes=56 << 20
        ),
    )(block_of, slot_of, segs, freqs, tokens, norm_gain, w_query, w_key, w_value, q_gain, k_gain)


def shards(tokens, norm_gain, w_query, w_key, w_value, query_gain, key_gain, segments, block_of):
    blocks = jnp.arange(64, dtype=jnp.int32)
    ahead = (blocks // 16 - lax.axis_index("tensor") + 4) % 4
    slot = (blocks % 16) * 4 + ahead + ahead // 2 - ahead // 3 * 2
    slot_of = jnp.sum(jnp.where(block_of[None, :] == blocks[:, None], slot[None, :], 0), 1)
    freqs = jnp.asarray(yarn_frequencies(128) * 2, F32)
    return front(
        block_of, slot_of, segments.reshape(-1, 1, 128), freqs[None, :], tokens,
        norm_gain[None, :], w_query, w_key, w_value, query_gain[None, :], key_gain[None, :],
    )


def solution(mesh):
    return jax.shard_map(
        shards,
        mesh=mesh,
        in_specs=(
            P(("context", "tensor"), None),
            P(),
            P("context", "tensor"),
            P(None, "tensor"),
            P(None, "tensor"),
            P(),
            P(),
            P(),
            P(),
        ),
        out_specs=P("context", "tensor"),
        check_vma=False,
    )
```

```python
import math

import jax
import jax.numpy as jnp
from jax import lax
from jax.experimental import pallas as pl
from jax.experimental.pallas import tpu as pltpu
from jax.sharding import PartitionSpec as P

MESH = pl.DeviceIdType.MESH
BF16 = jnp.bfloat16
F32 = jnp.float32
ROPE_SCALE = 0.1 * math.log(4.0) + 1.0
STEPS = (
    (1, 0), (0, 1), (3, 0), (0, 3), (1, 1), (3, 3), (1, 3), (3, 1),
    (2, 0), (0, 2), (2, 1), (1, 2), (2, 3), (3, 2), (2, 2),
)
PLACES = ((0, 0, 1),) + tuple((dx, dy, dk) for dk in (0, 1) for dx, dy in STEPS)


def yarn_frequencies(dim):
    theta = 1000000.0
    factor = 4.0
    initial = 32768.0
    lowest = math.floor(dim * math.log(initial / (32.0 * 2 * math.pi)) / (2 * math.log(theta)))
    highest = math.ceil(dim * math.log(initial / (1.0 * 2 * math.pi)) / (2 * math.log(theta)))
    lowest = max(lowest, 0)
    highest = min(highest, dim - 1)
    spread = max(highest - lowest, 0.001)
    result = []
    for index in range(dim // 2):
        base_freq = theta ** (-2.0 * index / dim)
        ramp = min(max((index - lowest) / spread, 0.0), 1.0)
        result.append(base_freq / factor * ramp + base_freq * (1.0 - ramp))
    return result


def ctx_of(x, y, zh, k):
    return x * 16 + y * 4 + zh * 2 + k


def place():
    c = lax.axis_index("context")
    return c // 16, (c // 4) % 4, (c // 2) % 2, c % 2, lax.axis_index("tensor")


def attend(q_ref, kv_ref, k_mask, q_mask, o_ref):
    heads = q_ref.shape[0]
    length = q_mask.shape[0]
    span = 6 * length
    step = 256
    scale = 128 ** (-0.5) * math.log2(math.e)
    ones = jnp.ones((step, 128), BF16)

    def score(h, r):
        quarters = step // 128
        q = q_ref[h, pl.ds(r * quarters, quarters)].reshape(step, 128)
        q = jnp.concatenate([q, q_mask[pl.ds(r * step, step), :]], -1)
        tiles = []
        top = None
        for at in range(r * step, span + r * step + step, step):
            rows = (at // length, pl.ds(at % length, step))
            keys = jnp.concatenate([kv_ref[(0,) + rows], k_mask[rows]], -1)
            s = lax.dot_general(q, keys, (((1,), (1,)), ((), ())), preferred_element_type=F32)
            if at == span + r * step:
                here = lax.broadcasted_iota(jnp.int32, s.shape, 0)
                s = jnp.where(lax.broadcasted_iota(jnp.int32, s.shape, 1) <= here, s, -1e30)
            tiles.append((rows, s))
            for c in range(0, step, 128):
                best = s[:, c : c + 128]
                top = best if top is None else jnp.maximum(top, best)
        return tiles, jnp.max(top, -1, keepdims=True)

    def finish(h, r, tiles, top):
        summed = None
        for rows, s in tiles:
            e = jnp.exp2((s - top) * scale).astype(BF16)
            values = jnp.concatenate([kv_ref[(1,) + rows], ones], -1)
            part = jnp.dot(e, values, preferred_element_type=F32)
            summed = part if summed is None else summed + part
        out = summed[:, :128] / summed[:, 128:]
        columns = pl.ds(pl.multiple_of(h * 128, 128), 128)
        o_ref[pl.ds(r * step, step), columns] = out.astype(BF16)

    def some(g, carry):
        ahead = None
        for n in range(4):
            for r in range(length // step):
                h = g * 4 + n
                now = (h, r) + score(h, r)
                if ahead is not None:
                    finish(*ahead)
                ahead = now
        finish(*ahead)
        return carry

    lax.fori_loop(0, heads // 4, some, 0)


def front_kernel(
    block_of, slot_of, segs, freqs, tok, norm_gain, wq, wk, wv, q_gain, k_gain,
    o_ref,
    tok_all, wq_all, wkv_all, q_send, qx, kv_send, got_k, got_v, picked,
    q_out, kv_all, cosine, sine, k_mask, q_mask,
    loc, tok_s, tok_r, w1_s, w1_r, zp_s, zp_r, zm_s, zm_r,
    yr_s, yr_r, yl_s, yl_r, fr_s, fr_r, fl_s, fl_r, co_s, co_r,
    kp_s, kp_r, km_s, km_r, kc_s, kc_r,
    qx_s, qx_r, qz_s, qz_r, p1_s, p1_r, p2_s, p2_r, own_s,
):
    x, y, zh, k, zl = place()
    me = ctx_of(x, y, zh, k)
    z = zh * 4 + zl
    d = (zl - x + 4) % 4
    zh_u = ((z - d + 8) % 8) // 4
    zh_d = 1 - zh_u

    def at_z(pos):
        pos = pos % 8
        return (ctx_of(x, y, pos // 4, k), pos % 4)

    up, down = at_z(z + 1), at_z(z + 7)
    x_dev = [(ctx_of((x + o) % 4, y, zh, k), zl) for o in range(4)]
    y_right, y_left = (ctx_of(x, (y + 1) % 4, zh, k), zl), (ctx_of(x, (y + 3) % 4, zh, k), zl)
    other = (ctx_of(x, y, zh, 1 - k), zl)

    rest = y * 4 + zh * 2 + k
    mine = x * 8 + y * 2 + k

    def half_plane(n):
        return (ctx_of(n // 8, (n // 2) % 4, zh, n % 2), zl)

    barrier = pltpu.get_barrier_semaphore()

    def greet(dev):
        pl.semaphore_signal(barrier, inc=1, device_id=dev, device_id_type=MESH)

    for dev in (x_dev[1], x_dev[2], x_dev[3], up, down, y_right, y_left, other):
        greet(dev)
    for o in range(1, 4):
        greet((me, (zl + o) % 4))

    def greet_piece(r, carry):
        @pl.when((x != zl) | (r != rest))
        def _():
            greet((zl * 16 + r, x))

        return carry

    lax.fori_loop(0, 16, greet_piece, 0)

    def greet_plane(o, carry):
        greet(half_plane((mine + o) % 32))
        return carry

    lax.fori_loop(1, 32, greet_plane, 0)

    quarter = tok.shape[0]
    width = tok.shape[1]

    def norm_rows(n, carry):
        rows = pl.ds(pl.multiple_of(n * 16, 16), 16)
        wide = tok[rows, :].astype(F32)
        mean = jnp.mean(wide * wide, -1, keepdims=True)
        wide = wide * lax.rsqrt(mean + 1e-06) * norm_gain[...]
        tok_all[rows, :] = wide.astype(BF16)
        return carry

    pl.semaphore_wait(barrier, 8 + 3 + 15 + 31 + ((x - zl + 4) % 4 + 3) // 4)

    def remote(src, dst, ss, rs, dev):
        return pltpu.make_async_remote_copy(
            src_ref=src, dst_ref=dst, send_sem=ss, recv_sem=rs, device_id=dev, device_id_type=MESH
        )

    half = quarter // 2

    def tok_copy(n, src, dst, part, dev):
        ref = lambda slot: tok_all.at[pl.ds(slot * quarter + part * half, half)]
        return remote(ref(src), ref(dst), tok_s.at[n], tok_r.at[n], dev)

    def w_slot(c):
        return wq_all.at[pl.ds(pl.multiple_of(c * w_rows, 16), w_rows)]

    w_rows = wq.shape[0]
    sends = [
        tok_copy(0, 0, 2, 0, x_dev[1]),
        tok_copy(3, 0, 1, 1, x_dev[3]),
        tok_copy(1, 0, 2, 1, x_dev[1]),
        tok_copy(2, 0, 1, 0, x_dev[3]),
    ]
    w1_index = (x - zl + 4) % 4
    w1 = remote(wq, w_slot(me), w1_s.at[0], w1_r.at[w1_index], (ctx_of(zl, y, zh, k), zl))
    own_w = pltpu.make_async_copy(wq, w_slot(me), loc.at[2])

    @pl.when(d != 0)
    def _():
        w1.start()

    @pl.when(d == 0)
    def _():
        own_w.start()

    own_k = pltpu.make_async_copy(wk, wkv_all.at[:, pl.ds(0, 128)], loc.at[0])
    own_v = pltpu.make_async_copy(wv, wkv_all.at[:, pl.ds(128, 128)], loc.at[1])

    @pl.when(d == 0)
    def _():
        own_k.start()
        own_v.start()

    def slot(i, zhalf, yy):
        return w_slot(ctx_of((x + i) % 4, yy, zhalf, k))

    def zp(i):
        ref = slot(i, zh_u, y)
        return remote(ref, ref, zp_s.at[i], zp_r.at[i], up)

    def zm(i, zhalf):
        ref = slot(i, zhalf, y)
        return remote(ref, ref, zm_s.at[i], zm_r.at[i], down)

    def core(n, ref):
        return remote(ref, ref, co_s.at[n], co_r.at[n], other)

    def y_own(s, ref):
        return (
            remote(ref, ref, yr_s.at[s], yr_r.at[s], y_right),
            remote(ref, ref, yl_s.at[s], yl_r.at[s], y_left),
        )

    def fwd_right(i2, ref):
        return remote(ref, ref, fr_s.at[i2], fr_r.at[i2], y_right)

    def fwd_left(i2, ref):
        return remote(ref, ref, fl_s.at[i2], fl_r.at[i2], y_left)

    def spread(s, ref):
        right, left = y_own(s, ref)
        right.start()
        left.start()
        core(s, ref).start()

    def when_four(i, act):
        @pl.when((i >= 0) & (i < 4))
        def _():
            act(i)

    def z_upper(i):
        ref = slot(i, zh_u, y)

        @pl.when(d == 0)
        def _():
            @pl.when(i == 0)
            def _():
                own_w.wait()

            @pl.when(i != 0)
            def _():
                remote(ref, ref, w1_s.at[0], w1_r.at[i], other).wait_recv()

            zm(i, zh_u).start()

        @pl.when(d != 0)
        def _():
            zp(i).wait_recv()

        zp(i).start()
        spread(i, ref)

    def z_lower(i):
        ref = slot(i, zh_d, y)

        @pl.when(d == 0)
        def _():
            remote(ref, ref, zp_s.at[i], zp_r.at[i], up).wait_recv()

        @pl.when(d != 0)
        def _():
            zm(i, zh_d).wait_recv()

        @pl.when(d >= 2)
        def _():
            zm(i, zh_d).start()

        spread(4 + i, ref)

    rows = wk.shape[0] // 8

    def part(i):
        return pl.ds(pl.multiple_of((k * 4 + i) * rows, 16), rows)

    def key_part(i):
        return wkv_all.at[part(i), pl.ds(0, 128)]

    def value_part(i):
        return wkv_all.at[part(i), pl.ds(128, 128)]

    def kv_core(n, ref):
        return remote(ref, ref, kc_s.at[n], kc_r.at[n], other)

    def kp(i):
        return remote(key_part(i), key_part(i), kp_s.at[i], kp_r.at[i], up)

    def km(i):
        return remote(value_part(i), value_part(i), km_s.at[i], km_r.at[i], down)

    y_l, y_r, y_far = (y + 3) % 4, (y + 1) % 4, (y + 2) % 4

    def ring(i, s, zhalf):
        ref = slot(i, zhalf, y_l)
        y_own(s, ref)[0].wait_recv()

        @pl.when(i % 2 == 0)
        def _():
            fwd_right(s // 2, ref).start()

        core(8 + s, ref).start()
        ref2 = slot(i, zhalf, y_r)
        y_own(s, ref2)[1].wait_recv()

        @pl.when(i % 2 == 1)
        def _():
            fwd_left(s // 2, ref2).start()

        core(16 + s, ref2).start()

    def kv_upper(i):
        @pl.when(d != 0)
        def _():
            kp(i).wait_recv()
            kv_core(i, key_part(i)).start()

            @pl.when(d != 3)
            def _():
                kp(i).start()

    def kv_lower(i):
        @pl.when(d != 0)
        def _():
            km(i).wait_recv()
            kv_core(4 + i, value_part(i)).start()

            @pl.when(d != 1)
            def _():
                km(i).start()

    def ring_upper(i):
        ring(i, i, zh_u)

    def ring_lower(i):
        ring(i, 4 + i, zh_d)

    lane = lax.broadcasted_iota(jnp.int32, (128, 128), 1)

    def doc_row(at, absent):
        return jnp.where(at >= 0, segs[jnp.maximum(at, 0)], absent).astype(F32)

    def down_rows(row):
        return jnp.broadcast_to(row, (128, 128)).T

    def rope_table(n):
        row = block_of[((x + n + n // 2 - n // 3 * 2) % 4) * 16 + rest] * 4 + zl
        docs = down_rows(segs[row].astype(F32))

        def count(j, total):
            return total + jnp.where(doc_row(row - 24 + j, -1) < docs, 1.0, 0.0)

        before = lax.fori_loop(0, 25, count, jnp.zeros((128, 128), F32))
        here = lax.broadcasted_iota(jnp.int32, (128, 1), 0).astype(F32)
        offset = 3072.0 + here - jnp.sum(before, -1, keepdims=True)
        angle = offset * freqs[...]
        rows = pl.ds(pl.multiple_of(n * 128, 128), 128)
        cosine[rows, :] = jnp.cos(angle) * ROPE_SCALE
        turned = jnp.sin(angle) * ROPE_SCALE
        sine[rows, :] = jnp.where(lane < 64, -turned, turned)

    def mask_rows(n):
        for j in range(4):
            docs = down_rows(doc_row(block_of[me] * 4 - 24 + n * 4 + j, 63))
            same = docs == lane.astype(F32)
            k_mask[n, pl.ds(j * 128, 128), :] = jnp.where(same, 1.0, 0.0).astype(BF16)

            @pl.when(n == 6)
            def _():
                q_mask[pl.ds(j * 128, 128), :] = jnp.where(same, 0.0, -1e30).astype(BF16)

    def step(t, carry):
        when_four(t - d, z_upper)
        when_four(t - 4 + d, z_lower)

        @pl.when((d == 0) & (t == 3))
        def _():
            own_k.wait()
            own_v.wait()
            for i in range(4):
                kp(i).start()
                km(i).start()

        when_four(t - 4 - d, kv_upper)
        when_four(t - 8 + d, kv_lower)
        when_four(t - 4 - d, ring_upper)
        when_four(t - 8 + d, ring_lower)
        when_four(t - 1, rope_table)

        @pl.when((t >= 4) & (t < 11))
        def _():
            mask_rows(t - 4)

        return carry

    lax.fori_loop(0, 1, step, 0)
    lax.fori_loop(0, quarter // 16, norm_rows, 0)
    for copy in sends:
        copy.start()
    lax.fori_loop(1, 7, step, 0)

    tok_copy(0, 0, 2, 0, x_dev[1]).wait_recv()
    fwd_a = tok_copy(4, 2, 3, 0, x_dev[1])
    fwd_a.start()
    tok_copy(3, 0, 1, 1, x_dev[3]).wait_recv()
    fwd_b = tok_copy(5, 1, 3, 1, x_dev[3])
    fwd_b.start()

    lax.fori_loop(7, 12, step, 0)

    tok_copy(1, 0, 2, 1, x_dev[1]).wait_recv()
    tok_copy(2, 0, 1, 0, x_dev[3]).wait_recv()

    @pl.when(d != 0)
    def _():
        def core_part(i, carry):
            kv_core(i, key_part(i)).wait_recv()
            kv_core(4 + i, value_part(i)).wait_recv()
            return carry

        lax.fori_loop(0, 4, core_part, 0)

    def turn(t, gain, rows):
        t = t * lax.rsqrt(jnp.mean(t * t, -1, keepdims=True) + 1e-06) * gain[...]
        return (t * cosine[rows, :] + pltpu.roll(t, 64, 1) * sine[rows, :]).astype(BF16)

    def keys_values(first, count):
        rows = pl.ds(first * quarter, count * quarter)
        both = jnp.dot(tok_all[rows, :], wkv_all[...], preferred_element_type=F32)
        key = turn(both[:, :128], k_gain, rows)
        value = both[:, 128:].astype(BF16)
        for p in range(8):
            for n in range(count):
                at = n * quarter + p * 16
                kv_send[0, p, first + n] = key[at : at + 16]
                kv_send[1, p, first + n] = value[at : at + 16]

    early = pl.ds(0, 3)

    def piece(m, r, src_rest, dst_p):
        if m == 0:
            src, dst = kv_send.at[0, dst_p, early], got_k.at[pl.ds(src_rest * 4, 3)]
        elif m == 1:
            src, dst = kv_send.at[0, dst_p, 3], got_k.at[src_rest * 4 + 3]
        else:
            src, dst = kv_send.at[1, dst_p], got_v.at[pl.ds(src_rest * 4, 4)]
        return src, dst, p1_s.at[m, r], p1_r.at[m, src_rest]

    def to_piece(r):
        return (r // 4) * 2 + r % 2

    def send_pieces(m):
        def send_piece(o, carry):
            r = (rest + o) % 16

            @pl.when((x != zl) | (r != rest))
            def _():
                remote(*piece(m, r, rest, to_piece(r)), (zl * 16 + r, x)).start()

            return carry

        lax.fori_loop(0, 16, send_piece, 0)

        @pl.when(x == zl)
        def _():
            src, dst, _, _ = piece(m, rest, rest, to_piece(rest))
            pltpu.make_async_copy(src, dst, own_s.at[m]).start()

    def wait_pieces(m):
        def wait_piece(r, carry):
            @pl.when((x != zl) | (r != rest))
            def _():
                remote(*piece(m, r, r, 0), (zl * 16 + r, x)).wait_recv()

            return carry

        lax.fori_loop(0, 16, wait_piece, 0)

        @pl.when(x == zl)
        def _():
            src, dst, _, _ = piece(m, rest, rest, to_piece(rest))
            pltpu.make_async_copy(src, dst, own_s.at[m]).wait()

    keys_values(0, 3)
    send_pieces(0)
    tok_copy(4, 2, 3, 0, x_dev[1]).wait_recv()
    tok_copy(5, 1, 3, 1, x_dev[3]).wait_recv()
    keys_values(3, 1)
    send_pieces(1)
    send_pieces(2)

    def far_upper(i):
        finish(i, i, zh_u)

    def far_lower(i):
        finish(i, 4 + i, zh_d)

    def finish(i, s, zhalf):
        ref = slot(i, zhalf, y_far)

        @pl.when(i % 2 == 0)
        def _():
            fwd_right(s // 2, ref).wait_recv()

        @pl.when(i % 2 == 1)
        def _():
            fwd_left(s // 2, ref).wait_recv()

        core(24 + s, ref).start()

    def far_step(t, carry):
        when_four(t - d, far_upper)
        when_four(t - 4 + d, far_lower)
        return carry

    lax.fori_loop(0, 8, far_step, 0)

    any_w = w_slot(me)

    def wait_core(n, carry):
        core(n, any_w).wait_recv()
        return carry

    lax.fori_loop(0, 32, wait_core, 0)

    def heads(n):
        return pl.ds(n * 2, 2)

    def x_step(n, o):
        return remote(
            q_send.at[heads(n), (0, 1, 3, 2)[o]], qx.at[heads(n), x], qx_s.at[n, o],
            qx_r.at[n, o], x_dev[o],
        )

    def z_step(n, src, to):
        o = (to - zl + 4) % 4
        return remote(
            src, q_out.at[heads(n), zl], qz_s.at[n, o], qz_r.at[n, o], (me, to)
        )

    def z_move(n, src, frm):
        @pl.when(frm != zl)
        def _():
            z_step(n, src, frm).start()

        @pl.when(frm == zl)
        def _():
            pltpu.make_async_copy(
                src, q_out.at[heads(n), zl], loc.at[3 + n]
            ).start()

    def project(n, carry):
        columns = pl.ds(pl.multiple_of(n * 256, 256), 256)
        both = jnp.dot(tok_all[...], wq_all[:, columns], preferred_element_type=F32)
        for h in range(2):
            head = turn(both[:, h * 128 : h * 128 + 128], q_gain, pl.ds(0, 4 * quarter))
            q_send[n * 2 + h] = head.reshape(4, quarter, 128)
        for o in (1, 3, 2):
            x_step(n, o).start()
        z_move(n, q_send.at[heads(n), 0], x)
        return carry

    own_keys = pl.ds(pl.multiple_of(mine * 16, 16), 16)

    def plane(m, n):
        return remote(
            picked.at[m, n], kv_all.at[m, :, own_keys], p2_s.at[m, n], p2_r.at[m, mine],
            half_plane(n),
        )

    def pick(m, n):
        block = block_of[half_plane(n)[0]]
        for i in range(7):
            slot = slot_of[jnp.maximum(block - 6 + i, 0)]
            picked[m, n, i] = (got_k, got_v)[m][slot]

    def send_plane(m):
        for dx, dy, dk in PLACES:
            n = ((x + dx) % 4) * 8 + ((y + dy) % 4) * 2 + (k + dk) % 2
            pick(m, n)
            plane(m, n).start()
        pick(m, mine)
        pltpu.make_async_copy(picked.at[m, mine], kv_all.at[m, :, own_keys], loc.at[m]).start()

    def pass_on(n, carry):
        for o in (1, 3, 2):
            frm = (x - o + 4) % 4
            remote(
                q_send.at[heads(n), 0], qx.at[heads(n), frm], qx_s.at[n, o], qx_r.at[n, o],
                (ctx_of(frm, y, zh, k), zl),
            ).wait_recv()
            z_move(n, qx.at[heads(n), frm], frm)
        return carry

    lax.fori_loop(0, 4, project, 0)
    lax.fori_loop(0, 4, pass_on, 0)
    wait_pieces(0)
    wait_pieces(1)
    send_plane(0)
    wait_pieces(2)
    send_plane(1)


    def q_here(n, carry):
        pltpu.make_async_copy(
            q_send.at[heads(n), 0], q_out.at[heads(n), zl], loc.at[3 + n]
        ).wait()
        for o in (1, 2, 3):
            frm = (zl - o + 4) % 4
            remote(
                q_send.at[heads(n), 0], q_out.at[heads(n), frm], qz_s.at[n, o], qz_r.at[n, o],
                (me, frm),
            ).wait_recv()
        return carry

    lax.fori_loop(0, 4, q_here, 0)
    for m in range(2):
        pltpu.make_async_copy(picked.at[m, mine], kv_all.at[m, :, own_keys], loc.at[m]).wait()

    def plane_here(o, carry):
        n = (mine + o) % 32
        theirs = pl.ds(pl.multiple_of(n * 16, 16), 16)
        for m in range(2):
            remote(
                picked.at[m, n], kv_all.at[m, :, theirs], p2_s.at[m, n], p2_r.at[m, n],
                half_plane(n),
            ).wait_recv()
        return carry

    lax.fori_loop(1, 32, plane_here, 0)
    attend(q_out, kv_all, k_mask, q_mask, o_ref)

    def drain_q(n, carry):
        for o in (1, 2, 3):
            x_step(n, o).wait_send()
            z_step(n, q_send.at[heads(n), 0], (zl + o) % 4).wait_send()
        return carry

    lax.fori_loop(0, 4, drain_q, 0)

    def drain_piece(r, carry):
        @pl.when((x != zl) | (r != rest))
        def _():
            for m in range(3):
                remote(*piece(m, r, rest, to_piece(r)), (zl * 16 + r, x)).wait_send()

        return carry

    lax.fori_loop(0, 16, drain_piece, 0)

    def drain_plane(o, carry):
        for m in range(2):
            plane(m, (mine + o) % 32).wait_send()
        return carry

    lax.fori_loop(1, 32, drain_plane, 0)

    def drain_core(n, carry):
        core(n, any_w).wait_send()
        return carry

    lax.fori_loop(0, 32, drain_core, 0)

    def drain_y(s, carry):
        right, left = y_own(s, any_w)
        right.wait_send()
        left.wait_send()
        return carry

    lax.fori_loop(0, 8, drain_y, 0)

    def drain_four(i, carry):
        zp(i).wait_send()
        fwd_right(i, any_w).wait_send()
        fwd_left(i, any_w).wait_send()

        @pl.when((d == 0) | (d >= 2))
        def _():
            zm(i, zh_u).wait_send()
            km(i).wait_send()

        @pl.when(d <= 2)
        def _():
            kp(i).wait_send()

        @pl.when(d != 0)
        def _():
            kv_core(i, key_part(i)).wait_send()
            kv_core(4 + i, value_part(i)).wait_send()

        return carry

    lax.fori_loop(0, 4, drain_four, 0)
    for copy in sends:
        copy.wait_send()
    fwd_a.wait_send()
    fwd_b.wait_send()

    @pl.when(d != 0)
    def _():
        w1.wait_send()


def front(block_of, slot_of, segs, freqs, tokens, norm_gain, w_query, w_key, w_value, q_gain, k_gain):
    vmem = pl.BlockSpec(memory_space=pltpu.VMEM)
    dma = pltpu.SemaphoreType.DMA
    pair = lambda *n: [dma(n), dma(n)]
    rows, width = tokens.shape
    columns = w_query.shape[1]
    flops = 2 * 4 * rows * width * (columns + 256)
    return pl.pallas_call(
        front_kernel,
        out_shape=jax.ShapeDtypeStruct((4 * rows, columns), BF16),
        in_specs=[pl.BlockSpec(memory_space=pltpu.SMEM)] * 2 + [vmem] * 5
        + [pl.BlockSpec(memory_space=pl.ANY)] * 2 + [vmem] * 2,
        out_specs=vmem,
        scratch_shapes=[
            pltpu.VMEM((4 * rows, width), BF16),
            pltpu.VMEM((width, columns), BF16),
            pltpu.VMEM((width, 256), BF16),
            pltpu.VMEM((8, 4, rows, 128), BF16),
            pltpu.VMEM((8, 4, rows, 128), BF16),
            pltpu.VMEM((2, 8, 4, 16, 128), BF16),
            pltpu.VMEM((64, 16, 128), BF16),
            pltpu.VMEM((64, 16, 128), BF16),
            pltpu.VMEM((2, 32, 7, 16, 128), BF16),
            pltpu.VMEM((8, 4, rows, 128), BF16),
            pltpu.VMEM((2, 7, 4 * rows, 128), BF16),
            pltpu.VMEM((4 * rows, 128), F32),
            pltpu.VMEM((4 * rows, 128), F32),
            pltpu.VMEM((7, 4 * rows, 128), BF16),
            pltpu.VMEM((4 * rows, 128), BF16),
            dma((7,)),
        ] + pair(6) + [dma((1,)), dma((4,))] + pair(4) + pair(4) + pair(8) + pair(8)
        + pair(4) + pair(4) + pair(32) + pair(4) + pair(4) + pair(8)
        + pair(4, 4) + pair(4, 4) + pair(3, 16) + pair(2, 32) + [dma((3,))],
        cost_estimate=pl.CostEstimate(flops=flops, bytes_accessed=10 << 20, transcendentals=0),
        compiler_params=pltpu.CompilerParams(
            collective_id=0, has_side_effects=True, vmem_limit_bytes=56 << 20
        ),
    )(block_of, slot_of, segs, freqs, tokens, norm_gain, w_query, w_key, w_value, q_gain, k_gain)


def shards(tokens, norm_gain, w_query, w_key, w_value, query_gain, key_gain, segments, block_of):
    blocks = jnp.arange(64, dtype=jnp.int32)
    ahead = (blocks // 16 - lax.axis_index("tensor") + 4) % 4
    slot = (blocks % 16) * 4 + ahead + ahead // 2 - ahead // 3 * 2
    slot_of = jnp.sum(jnp.where(block_of[None, :] == blocks[:, None], slot[None, :], 0), 1)
    freqs = jnp.asarray(yarn_frequencies(128) * 2, F32)
    return front(
        block_of, slot_of, segments.reshape(-1, 1, 128), freqs[None, :], tokens,
        norm_gain[None, :], w_query, w_key, w_value, query_gain[None, :], key_gain[None, :],
    )


def solution(mesh):
    return jax.shard_map(
        shards,
        mesh=mesh,
        in_specs=(
            P(("context", "tensor"), None),
            P(),
            P("context", "tensor"),
            P(None, "tensor"),
            P(None, "tensor"),
            P(),
            P(),
            P(),
            P(),
        ),
        out_specs=P("context", "tensor"),
        check_vma=False,
    )
```
